256 devices in a mesh: dp: 32 (over z_hi, y, core), shard: 8 (over z_lo, x).
Axes of the slice: x: 4, y: 4, z: 8 (z_hi: 4, z_lo: 2; z = z_hi * 2 + z_lo), core: 2. Of those that a mesh axis runs over, the one named last changes fastest.
Arguments:
- inputs: bfloat16 [16384, 8192], P('dp', 'shard'), may hold values from -6 to 6
- key_grads: bfloat16 [16384, 1024], P('dp'), may hold values from -6 to 6
- error: bfloat16 [32, 8192, 1024], P('dp', 'shard'), may hold values from -6 to 6
- momentum: bfloat16 [8192, 1024], P('shard'), may hold values from -0.59765625 to 0.59765625
- q_start: float32 [1024, 64], replicated, may hold values from -6 to 6
Outputs:
- new_error: bfloat16 [32, 8192, 1024], P('dp', 'shard')
- new_momentum: bfloat16 [8192, 1024], P('shard')
- q_factor: float32 [1024, 64], replicated
The draws below stay inside these ranges and needn't reach their ends.
All inputs are finite; a program needn't handle non-finite values.
Results may differ from the reference program's by a relative error of at most 0.001.
Values sent between devices are 32-bit elements; how exact they have to be, the bound alone decides.
No kernel may reach another device: no remote copies, remote signals or barrier semaphores. Data moves between devices by JAX's collectives and lax.ppermute only.
A program may use at most 64 MiB of HBM per device.

```python
import math
import jax
import jax.numpy as jnp
from jax import lax

D = 8192
KVW = 1024
RANK = 64
ITERS = 3
TOK = 512
TOKENS = 16384
N_DP = 32


def shard_levels(own_key, shape, split, least, high):
    def one(dim, shards_of):
        heights = jax.random.uniform(jax.random.fold_in(jax.random.fold_in(own_key, 6), dim), (shards_of,), jnp.float32, least / len(split), high / len(split))
        return jnp.repeat(jnp.exp(heights), shape[dim] // shards_of).reshape((-1,) + (1,) * (len(shape) - dim - 1))

    gain = one(*split[0])
    for cut in split[1:]:
        gain = gain * one(*cut)
    return gain


def bell_draw(rng, shape, deviation, most, cuts=(), held_as=jnp.bfloat16):
    level = shard_levels(rng, shape, cuts, -0.22, 0.18) if cuts else 1.0
    result = jax.random.normal(rng, shape, jnp.float32) * deviation * level
    return jnp.minimum(jnp.maximum(result, -most), most).astype(held_as)


def setup_inputs(seed: int = 0) -> dict:
    key_of = jax.random.split(jax.random.key(seed), 6)
    inputs = bell_draw(key_of[0], (TOKENS, D), 1.0, 6.0, ((0, 32), (1, 8)))
    key_grads = bell_draw(key_of[1], (TOKENS, KVW), 1.0, 6.0, ((0, 32),))
    error = bell_draw(key_of[2], (N_DP, D, KVW), 1.0, 6.0, ((0, 32), (1, 8)))
    momentum = bell_draw(key_of[3], (D, KVW), 0.1, 0.59765625, ((0, 8),))
    q_start = bell_draw(key_of[4], (KVW, RANK), 1.0, 6.0, (), jnp.float32)
    return dict(inputs=inputs, key_grads=key_grads, error=error, momentum=momentum, q_start=q_start)


HIGH = lax.Precision.HIGHEST

def reference(inputs, key_grads, error, momentum, q_start):
    acts = inputs.reshape(N_DP, TOK, D)
    grads = key_grads.reshape(N_DP, TOK, KVW)
    factor = 1.0 / math.sqrt(TOK)

    def merge_one(items):
        act_rows, grad_rows, err_rows = items
        product = lax.dot_general(act_rows.astype(jnp.float32), grad_rows.astype(jnp.float32), (((0,), (0,)), ((), ())), preferred_element_type=jnp.float32)
        return product * factor + err_rows.astype(jnp.float32)
    merged = lax.map(merge_one, (acts, grads, error))
    q_now = q_start
    p_hat = None
    for turn in range(ITERS):
        p_left = jnp.einsum('rdk,kc->dc', merged, q_now, precision=HIGH)
        gram = jnp.dot(p_left.T, p_left, precision=HIGH)
        lower = jnp.linalg.cholesky(gram)
        p_hat = lax.linalg.triangular_solve(lower, p_left, left_side=False, lower=True, transpose_a=True)
        q_now = jnp.einsum('rdk,dc->kc', merged, p_hat, precision=HIGH) / N_DP
    approx = jnp.dot(p_hat, q_now.T, precision=HIGH)
    new_error = (merged - approx[None]).astype(jnp.bfloat16)
    new_momentum = (0.9 * momentum.astype(jnp.float32) + approx).astype(jnp.bfloat16)
    return (new_error, new_momentum, q_now)
```

```python
import math

import jax
import jax.numpy as jnp
from jax import lax
from jax.experimental import pallas as pl
from jax.experimental.pallas import tpu as pltpu
from jax.sharding import PartitionSpec as P

ITERS = 3
HIGH = lax.Precision.HIGHEST
ROWS = (((0,), (0,)), ((), ()))
LANES = (((1,), (1,)), ((), ()))
F32 = jnp.float32
BF16 = jnp.bfloat16
VMEM = pl.BlockSpec(memory_space=pltpu.VMEM)
SMEM = pl.BlockSpec(memory_space=pltpu.SMEM)

Y_GROUPS = [[z * 8 + y * 2 + c for y in range(4)] for z in range(4) for c in range(2)]
Z_GROUPS = [[z * 8 + y * 2 + c for z in range(4)] for y in range(4) for c in range(2)]
ZY_GROUPS = [[z * 8 + y * 2 + c for z in range(4) for y in range(4)] for c in range(2)]


def dp_shift(x, dy, dc):
    pairs = []
    for i in range(32):
        z, y, c = i // 8, (i // 2) % 4, i % 2
        pairs.append((i, z * 8 + (y + dy) % 4 * 2 + (c + dc) % 2))
    return lax.ppermute(x, "dp", pairs)


def exchange(x, groups, axis="dp"):
    return lax.all_to_all(x, axis, 0, 0, axis_index_groups=groups)


def gather(x, n, groups, axis="dp"):
    return exchange(jnp.broadcast_to(x[None], (n,) + x.shape), groups, axis)


def params(mib, **more):
    return pltpu.CompilerParams(vmem_limit_bytes=mib << 20, **more)


def cost(flops, read):
    return pl.CostEstimate(flops=flops, bytes_accessed=read, transcendentals=0)


def split2(x):
    hi = x.astype(BF16)
    return hi, (x - hi.astype(F32)).astype(BF16)


def split3(x):
    hi = x.astype(BF16)
    rest = x - hi.astype(F32)
    mid = rest.astype(BF16)
    return hi, mid, (rest - mid.astype(F32)).astype(BF16)


def merge_kernel(half_ref, acts_ref, grads_ref, err_ref, out_ref):
    factor = 1.0 / math.sqrt(acts_ref.shape[0])
    product = lax.dot_general(acts_ref[...], grads_ref[...], ROWS, preferred_element_type=F32)
    out_ref[0] = product * factor + err_ref[0].astype(F32)


def merge(half, inputs, key_grads, error):
    tok, d = inputs.shape
    k = key_grads.shape[1]
    return pl.pallas_call(
        merge_kernel,
        out_shape=jax.ShapeDtypeStruct((4, d // 2, k // 4), F32),
        grid_spec=pltpu.PrefetchScalarGridSpec(
            num_scalar_prefetch=1,
            grid=(4,),
            in_specs=[
                pl.BlockSpec((tok, d // 2), lambda i, half: (0, half[0])),
                pl.BlockSpec((tok, k // 4), lambda i, half: (0, i)),
                pl.BlockSpec((1, d // 2, k // 4), lambda i, half: (0, half[0], i)),
            ],
            out_specs=pl.BlockSpec((1, d // 2, k // 4), lambda i, half: (i, 0, 0)),
        ),
        compiler_params=params(56),
        cost_estimate=cost(tok * d * k, 5 << 20),
        name="merge",
    )(half.reshape(1), inputs, key_grads, error)


def sum_turn_kernel(x_ref, out_ref):
    out_ref[...] = (x_ref[0] + x_ref[1] + x_ref[2] + x_ref[3]).T


def sum_turn(x):
    _, d, k = x.shape
    return pl.pallas_call(
        sum_turn_kernel,
        out_shape=jax.ShapeDtypeStruct((k, d), F32),
        grid=(d // 128,),
        in_specs=[pl.BlockSpec((4, 128, k), lambda i: (0, i, 0))],
        out_specs=pl.BlockSpec((k, 128), lambda i: (0, i)),
        compiler_params=params(24),
        cost_estimate=cost(4 * d * k, 20 * d * k),
        name="sum_turn",
    )(x)


def block_kernel(pos_ref, u0, u1, u2, of_y, sent_ref, mine_ref):
    core = pos_ref[0]
    rows = jnp.concatenate([u0[...], u1[...], u2[...]], axis=0)
    block = lax.dot_general(rows, of_y[...], LANES, precision=HIGH, preferred_element_type=F32)

    def put(ref, part):
        for e in range(3):
            for s in range(8):
                ref[s, e] = part[64 * e + 8 * s:64 * e + 8 * s + 8]

    @pl.when(core == 0)
    def _():
        put(mine_ref, block[:, :128])
        put(sent_ref, block[:, 128:])

    @pl.when(core == 1)
    def _():
        put(mine_ref, block[:, 128:])
        put(sent_ref, block[:, :128])


def g_block(pos, units, of_y):
    k, d = of_y.shape
    return pl.pallas_call(
        block_kernel,
        out_shape=(jax.ShapeDtypeStruct((8, 3, 8, 128), F32),) * 2,
        in_specs=[SMEM] + [VMEM] * 4,
        out_specs=(VMEM, VMEM),
        compiler_params=params(24),
        cost_estimate=cost(2 * 6 * 192 * k * d, 2 << 20),
        name="g_block",
    )(pos, *units, of_y)


def inverse_factor(gram):
    n = gram.shape[0]
    tiles = n // 8
    gram = 0.5 * (gram + gram.T)
    row = lax.broadcasted_iota(jnp.int32, (n, n), 0)
    col = lax.broadcasted_iota(jnp.int32, (n, n), 1)
    both = jnp.concatenate([gram, jnp.where(row == col, 1.0, 0.0)], axis=1)
    b = [both[8 * r:8 * r + 8] for r in range(tiles)]
    sub = lax.broadcasted_iota(jnp.int32, (8, 2 * n), 0)
    out = []
    for t in range(tiles):
        c = {
            (r, k): jnp.broadcast_to(b[r][:, 8 * t + k:8 * t + k + 1], (8, 2 * n))
            for r in range(t, tiles)
            for k in range(8)
        }
        pivots = jnp.ones((8, 2 * n), F32)
        for k in range(8):
            pivot = jnp.broadcast_to(c[t, k][k:k + 1], (8, 2 * n))
            pivots = jnp.where(sub == k, pivot, pivots)
            turn = 1.0 / pivot
            lead = jnp.broadcast_to(b[t][k:k + 1], (8, 2 * n))
            heads = {l: jnp.broadcast_to(c[t, l][k:k + 1], (8, 2 * n)) for l in range(k + 1, 8)}
            for r in range(t, tiles):
                m = c[r, k] * turn
                if r == t:
                    m = jnp.where(sub > k, m, 0.0)
                b[r] = b[r] - m * lead
                for l in range(k + 1, 8):
                    c[r, l] = c[r, l] - m * heads[l]
        out.append(b[t] / jnp.sqrt(pivots))
    return jnp.concatenate(out, axis=0)[:, n:]


def iterate_kernel(pos_ref, own_ref, away_ref, q_ref, q_out, w_out, hi_ref, mid_ref, low_ref):
    s = pl.program_id(0)
    parts = (hi_ref, mid_ref, low_ref)
    for ref, core in ((own_ref, pos_ref[0]), (away_ref, 1 - pos_ref[0])):
        for z in range(4):
            for y in range(4):
                to = pl.ds(pl.multiple_of(y * 256 + core * 128, 128), 128)
                for e in range(3):
                    start = (y - e) % 4 * 256 + z * 64 + s * 16
                    at = pl.ds(pl.multiple_of(start, 16), 16)
                    both = jnp.concatenate([ref[0, z * 4 + y, e], ref[1, z * 4 + y, e]], axis=0)
                    for part, value in zip(parts, split3(both)):
                        part[at, to] = value

    @pl.when(s == pl.num_programs(0) - 1)
    def _():
        for y in range(4):
            here, after = pl.ds(y * 256, 256), pl.ds((y + 1) % 4 * 256, 256)
            for part in parts:
                part[after, here] = part[here, after].T
        q = q_ref[...]
        n = q.shape[0]
        for turn in range(ITERS):
            hi, mid, low = split3(q)
            by_hi = jnp.dot(jnp.concatenate([hi, mid, low], axis=0), hi_ref[...], preferred_element_type=F32)
            by_mid = jnp.dot(jnp.concatenate([hi, mid], axis=0), mid_ref[...], preferred_element_type=F32)
            by_low = jnp.dot(hi, low_ref[...], preferred_element_type=F32)
            small = by_hi[2 * n:] + by_mid[n:] + by_low
            u = by_hi[:n] + (by_hi[n:2 * n] + by_mid[:n] + small)
            gram = lax.dot_general(q, u, LANES, precision=HIGH, preferred_element_type=F32)
            inv = inverse_factor(gram)
            if turn == ITERS - 1:
                w_out[...] = jnp.dot(inv, q, precision=HIGH, preferred_element_type=F32)
            q = jnp.dot(inv, u, precision=HIGH, preferred_element_type=F32) * (1.0 / 32)
        q_out[...] = q


def iterate(pos, own, away, q):
    n, k = q.shape
    part = pl.BlockSpec((2,) + own.shape[1:], lambda s: (s, 0, 0, 0, 0))
    whole = pl.BlockSpec((n, k), lambda s: (0, 0))
    return pl.pallas_call(
        iterate_kernel,
        out_shape=(jax.ShapeDtypeStruct(q.shape, F32),) * 2,
        grid=(own.shape[0] // 2,),
        in_specs=[SMEM, part, part, whole],
        out_specs=(whole, whole),
        scratch_shapes=[pltpu.VMEM((k, k), BF16)] * 3,
        compiler_params=params(40),
        cost_estimate=cost(36 * n * k * k, 4 * k * k),
        name="iterations",
    )(pos, own, away, q)


def left_kernel(pos_ref, w_ref, m0, m1, m2, m3, out_ref):
    total = None
    n = w_ref.shape[0]
    for turn, ref in enumerate((m0, m1, m2, m3)):
        at = pl.multiple_of(((pos_ref[1] + 4 - turn) % 4) * 256, 256)
        whi, wlow = split2(w_ref[:, pl.ds(at, 256)])
        mhi, mlow = split2(ref[...])
        both = jnp.dot(jnp.concatenate([whi, wlow], axis=0), mhi, preferred_element_type=F32)
        part = both[:n] + (both[n:] + jnp.dot(whi, mlow, preferred_element_type=F32))
        total = part if total is None else total + part
    out_ref[...] = total


def left(pos, w, blocks):
    n, d = w.shape[0], blocks[0].shape[1]
    return pl.pallas_call(
        left_kernel,
        out_shape=jax.ShapeDtypeStruct((n, d), F32),
        in_specs=[SMEM] + [VMEM] * 5,
        out_specs=VMEM,
        compiler_params=params(24),
        cost_estimate=cost(6 * n * d * 1024, 2 << 20),
        name="left",
    )(pos, w, *blocks)


def finish_kernel(pos_ref, mine, other, mom, own, away, q, err_out, mom_out, q_parts):
    i = pl.program_id(0)

    @pl.when(i == 0)
    def _():
        hi, low = split2(q[...])
        q_parts[...] = jnp.concatenate([hi, hi, low, low], axis=0)

    def step(merged, p_t):
        hi, low = split2(p_t[...])
        p_parts = jnp.concatenate([hi, low, hi, low], axis=0)
        for n in range(4):
            cols = pl.ds(256 * n, 256)
            approx = lax.dot_general(p_parts, q_parts[:, cols], ROWS, preferred_element_type=F32)
            err_out[0, :, cols] = (merged[n] - approx).astype(BF16)
            mom_out[:, cols] = (0.9 * mom[:, cols].astype(F32) + approx).astype(BF16)

    first = i < pl.num_programs(0) // 2

    @pl.when(first)
    def _():
        step(mine, own)

    @pl.when(jnp.logical_not(first))
    def _():
        step(other, away)


def finish(pos, mine, other, error, momentum, own, away, q):
    n, k = q.shape
    d = momentum.shape[0]
    rows = 256
    half = d // rows // 2

    def row(i, pos):
        return jnp.where(i < half, pos[0], 1 - pos[0]) * half + i % half

    def early(i):
        return jnp.minimum(i, half - 1)

    def late(i):
        return jnp.maximum(i - half, 0)

    return pl.pallas_call(
        finish_kernel,
        out_shape=(jax.ShapeDtypeStruct(error.shape, BF16), jax.ShapeDtypeStruct(momentum.shape, BF16)),
        grid_spec=pltpu.PrefetchScalarGridSpec(
            num_scalar_prefetch=1,
            grid=(d // rows,),
            in_specs=[
                pl.BlockSpec((4, rows, k // 4), lambda i, pos: (0, early(i), 0)),
                pl.BlockSpec((4, rows, k // 4), lambda i, pos: (0, late(i), 0)),
                pl.BlockSpec((rows, k), lambda i, pos: (row(i, pos), 0)),
                pl.BlockSpec((n, rows), lambda i, pos: (0, early(i))),
                pl.BlockSpec((n, rows), lambda i, pos: (0, late(i))),
                pl.BlockSpec((n, k), lambda i, pos: (0, 0)),
            ],
            out_specs=(
                pl.BlockSpec((1, rows, k), lambda i, pos: (0, row(i, pos), 0)),
                pl.BlockSpec((rows, k), lambda i, pos: (row(i, pos), 0)),
            ),
            scratch_shapes=[pltpu.VMEM((4 * n, k), BF16)],
        ),
        compiler_params=params(24),
        cost_estimate=cost(8 * n * d * k, 10 << 20),
        name="finish",
    )(pos, mine, other, momentum, own, away, q)


def shards(inputs, key_grads, error, momentum, q_start):
    i = lax.axis_index("dp")
    y, c = (i // 2) % 4, i % 2
    pos = jnp.stack([c, y])

    other = merge(1 - c, inputs, key_grads, error)
    sent = dp_shift(other, 0, 1)
    mine = merge(c, inputs, key_grads, error)
    pieces = exchange(mine + sent, Y_GROUPS)
    unit = exchange(sum_turn(pieces).reshape(4, 64, 512), Z_GROUPS).sum(axis=0)
    units = [unit] + [dp_shift(unit, dy, 0) for dy in (1, 2)]
    of_y = gather(unit, 4, Z_GROUPS).reshape(256, 512)

    to_core, part = g_block(pos, units, of_y)
    part = part + dp_shift(to_core, 0, 1)
    part = exchange(part, None, "shard").sum(axis=0)
    part = gather(part, 16, ZY_GROUPS)
    part, of_y = lax.optimization_barrier((part, of_y))
    blocks = [of_y] + [dp_shift(of_y, dy, 0) for dy in (1, 2, 3)]
    part = gather(part, 8, None, "shard")
    part, blocks = lax.optimization_barrier((part, blocks))
    q_t, w = iterate(pos, part, dp_shift(part, 0, 1), q_start.T)

    own = left(pos, w, blocks)
    away = dp_shift(own, 0, 1)
    new_error, new_momentum = finish(pos, mine, other, error, momentum, own, away, q_t)
    return (new_error, new_momentum, q_t.T)


def solution(mesh):
    return jax.shard_map(
        shards,
        mesh=mesh,
        in_specs=(P("dp", "shard"), P("dp", None), P("dp", "shard", None), P("shard", None), P()),
        out_specs=(P("dp", "shard", None), P("shard", None), P()),
        check_vma=False,
    )
```

```python
import functools
import math

import jax
import jax.numpy as jnp
from jax import lax
from jax.experimental import pallas as pl
from jax.experimental.pallas import tpu as pltpu
from jax.sharding import PartitionSpec as P

ITERS = 3
HIGH = lax.Precision.HIGHEST
ROWS = (((0,), (0,)), ((), ()))
LANES = (((1,), (1,)), ((), ()))
F32 = jnp.float32
BF16 = jnp.bfloat16
VMEM = pl.BlockSpec(memory_space=pltpu.VMEM)
SMEM = pl.BlockSpec(memory_space=pltpu.SMEM)

Z_GROUPS = [[z * 8 + y * 2 + c for z in range(4)] for y in range(4) for c in range(2)]
ZY_GROUPS = [[z * 8 + y * 2 + c for z in range(4) for y in range(4)] for c in range(2)]


def dp_shift(x, dz=0, dy=0, dc=0):
    pairs = []
    for i in range(32):
        z, y, c = i // 8, (i // 2) % 4, i % 2
        pairs.append((i, (z + dz) % 4 * 8 + (y + dy) % 4 * 2 + (c + dc) % 2))
    return lax.ppermute(x, "dp", pairs)


def ring_sum(opposite, following, before, step):
    relay_on, relay_back = step(opposite[0], 1), step(opposite[1], -1)
    second, first = step(following[1], 1), step(before[0], -1)
    relay_on, relay_back, second, first = lax.optimization_barrier((relay_on, relay_back, second, first))
    on, back = step(following[0] + relay_on, 1), step(before[1] + relay_back, -1)
    return on, second, first, back


def exchange(x, groups, axis="dp"):
    return lax.all_to_all(x, axis, 0, 0, axis_index_groups=groups)


def gather(x, n, groups, axis="dp"):
    return exchange(jnp.broadcast_to(x[None], (n,) + x.shape), groups, axis)


def params(mib, **more):
    return pltpu.CompilerParams(vmem_limit_bytes=mib << 20, **more)


def cost(flops, read):
    return pl.CostEstimate(flops=flops, bytes_accessed=read, transcendentals=0)


def split2(x):
    hi = x.astype(BF16)
    return hi, (x - hi.astype(F32)).astype(BF16)


def split3(x):
    hi = x.astype(BF16)
    rest = x - hi.astype(F32)
    mid = rest.astype(BF16)
    return hi, mid, (rest - mid.astype(F32)).astype(BF16)


def merge_kernel(turns, added, pos_ref, acts, grads, err, *refs):
    sent, refs = (refs[0], refs[1:]) if added else (None, refs)
    out_ref, refs = refs[0], refs[1:]
    sums, refs = (refs[:2 * len(turns)], refs[2 * len(turns):]) if added else ((), refs)
    x_buf, k_buf, e_buf, sems = refs
    half, y = pos_ref[0], pos_ref[1]
    tok, d = x_buf.shape
    at_d = pl.ds(pl.multiple_of(half * d, 128), d)
    copies = [pltpu.make_async_copy(acts.at[:, at_d], x_buf, sems.at[0])]
    for n, turn in enumerate(turns):
        cols = pl.ds(pl.multiple_of((y + turn) % 4 * 256, 128), 256)
        copies.append(pltpu.make_async_copy(grads.at[:, cols], k_buf.at[n], sems.at[1 + 2 * n]))
        copies.append(pltpu.make_async_copy(err.at[0, at_d, cols], e_buf.at[n], sems.at[2 + 2 * n]))
    for copy in copies:
        copy.start()
    copies[0].wait()
    factor = 1.0 / math.sqrt(tok)
    for n in range(len(turns)):
        copies[1 + 2 * n].wait()
        product = lax.dot_general(x_buf[...], k_buf[n], ROWS, preferred_element_type=F32)
        copies[2 + 2 * n].wait()
        merged = product * factor + e_buf[n].astype(F32)
        out_ref[n] = merged
        if added:
            total = merged + sent[n]
            sums[2 * n][...] = total[:d // 2]
            sums[2 * n + 1][...] = total[d // 2:]


def merge(half, y, turns, inputs, key_grads, error, sent=None):
    tok, d = inputs.shape
    d = d // 2
    n = len(turns)
    added = sent is not None
    in_hbm = pl.BlockSpec(memory_space=pltpu.HBM)
    outs = [jax.ShapeDtypeStruct((n, d, 256), F32)]
    if added:
        outs += [jax.ShapeDtypeStruct((d // 2, 256), F32)] * (2 * n)
    result = pl.pallas_call(
        functools.partial(merge_kernel, turns, added),
        out_shape=tuple(outs),
        in_specs=[SMEM] + [in_hbm] * 3 + [VMEM] * added,
        out_specs=(VMEM,) * len(outs),
        scratch_shapes=[
            pltpu.VMEM((tok, d), BF16),
            pltpu.VMEM((n, tok, 256), BF16),
            pltpu.VMEM((n, d, 256), BF16),
            pltpu.SemaphoreType.DMA((1 + 2 * n,)),
        ],
        compiler_params=params(58),
        cost_estimate=cost(2 * tok * d * 256 * n, (1 + 2 * n) << 19),
        name="merge",
    )(jnp.stack([half, y]), inputs, key_grads, error, *([sent] if added else []))
    return result[0], list(result[1:])


def sum_turn_kernel(pos_ref, top, end, on, second, first, back, *refs):
    outs, own_ref, turned = refs[:6], refs[6], refs[7]
    turned[:, :256] = (top[...] + (on[...] + first[...])).T
    turned[:, 256:] = (end[...] + (second[...] + back[...])).T
    z = pos_ref[2]
    for n, turn in enumerate((2, 1, 3)):
        at = (z + turn) % 4 * 64
        for h in range(2):
            outs[2 * n + h][...] = turned[pl.ds(pl.multiple_of(at + 32 * h, 32), 32), :]
    own_ref[...] = turned[pl.ds(pl.multiple_of(z * 64, 64), 64), :]


def sum_turn(pos, top, end, came):
    half = jax.ShapeDtypeStruct((32, 512), F32)
    return pl.pallas_call(
        sum_turn_kernel,
        out_shape=(half,) * 6 + (jax.ShapeDtypeStruct((64, 512), F32),),
        in_specs=[SMEM] + [VMEM] * 6,
        out_specs=(VMEM,) * 7,
        scratch_shapes=[pltpu.VMEM((256, 512), F32)],
        compiler_params=params(24),
        cost_estimate=cost(4 << 17, 3 << 20),
        name="sum_turn",
    )(pos, top, end, *came)


def unit_kernel(own, on, second, first, back, unit_ref, copies_ref):
    for h, (a, b) in enumerate(((on, first), (second, back))):
        rows = pl.ds(32 * h, 32)
        total = own[rows, :] + (a[...] + b[...])
        unit_ref[rows, :] = total
        for z in range(4):
            copies_ref[z, rows, :] = total


def make_unit(own, came):
    return pl.pallas_call(
        unit_kernel,
        out_shape=(jax.ShapeDtypeStruct((64, 512), F32), jax.ShapeDtypeStruct((4, 64, 512), F32)),
        in_specs=[VMEM] * 5,
        out_specs=(VMEM, VMEM),
        compiler_params=params(24),
        cost_estimate=cost(1 << 17, 1 << 20),
        name="make_unit",
    )(own, *came)


def block_kernel(pos_ref, u0, u1, u2, of_y, sent_ref, mine_ref):
    core = pos_ref[0]
    rows = jnp.concatenate([u0[...], u1[...], u2[...]], axis=0)
    block = lax.dot_general(rows, of_y[...], LANES, precision=HIGH, preferred_element_type=F32)

    def put(ref, part):
        for e in range(3):
            for s in range(8):
                ref[s, e] = part[64 * e + 8 * s:64 * e + 8 * s + 8]

    @pl.when(core == 0)
    def _():
        put(mine_ref, block[:, :128])
        put(sent_ref, block[:, 128:])

    @pl.when(core == 1)
    def _():
        put(mine_ref, block[:, 128:])
        put(sent_ref, block[:, :128])


def g_block(pos, units, of_y):
    k, d = of_y.shape
    return pl.pallas_call(
        block_kernel,
        out_shape=(jax.ShapeDtypeStruct((8, 3, 8, 128), F32),) * 2,
        in_specs=[SMEM] + [VMEM] * 4,
        out_specs=(VMEM, VMEM),
        compiler_params=params(24),
        cost_estimate=cost(2 * 6 * 192 * k * d, 2 << 20),
        name="g_block",
    )(pos, *units, of_y)


def inverse_factor(gram):
    n = gram.shape[0]
    tiles = n // 8
    gram = 0.5 * (gram + gram.T)
    row = lax.broadcasted_iota(jnp.int32, (n, n), 0)
    col = lax.broadcasted_iota(jnp.int32, (n, n), 1)
    both = jnp.concatenate([gram, jnp.where(row == col, 1.0, 0.0)], axis=1)
    b = [both[8 * r:8 * r + 8] for r in range(tiles)]
    sub = lax.broadcasted_iota(jnp.int32, (8, 2 * n), 0)
    out = []
    for t in range(tiles):
        c = {
            (r, k): jnp.broadcast_to(b[r][:, 8 * t + k:8 * t + k + 1], (8, 2 * n))
            for r in range(t, tiles)
            for k in range(8)
        }
        pivots = jnp.ones((8, 2 * n), F32)
        for k in range(8):
            pivot = jnp.broadcast_to(c[t, k][k:k + 1], (8, 2 * n))
            pivots = jnp.where(sub == k, pivot, pivots)
            turn = 1.0 / pivot
            lead = jnp.broadcast_to(b[t][k:k + 1], (8, 2 * n))
            heads = {l: jnp.broadcast_to(c[t, l][k:k + 1], (8, 2 * n)) for l in range(k + 1, 8)}
            for r in range(t, tiles):
                m = c[r, k] * turn
                if r == t:
                    m = jnp.where(sub > k, m, 0.0)
                b[r] = b[r] - m * lead
                for l in range(k + 1, 8):
                    c[r, l] = c[r, l] - m * heads[l]
        out.append(b[t] / jnp.sqrt(pivots))
    return jnp.concatenate(out, axis=0)[:, n:]


def iterate_kernel(pos_ref, own_ref, away_ref, q_ref, q_out, w_out, hi_ref, mid_ref, low_ref):
    s = pl.program_id(0)
    parts = (hi_ref, mid_ref, low_ref)
    for ref, core in ((own_ref, pos_ref[0]), (away_ref, 1 - pos_ref[0])):
        for z in range(4):
            for y in range(4):
                to = pl.ds(pl.multiple_of(y * 256 + core * 128, 128), 128)
                for e in range(3):
                    start = (y - e) % 4 * 256 + z * 64 + s * 16
                    at = pl.ds(pl.multiple_of(start, 16), 16)
                    both = jnp.concatenate([ref[0, z * 4 + y, e], ref[1, z * 4 + y, e]], axis=0)
                    for part, value in zip(parts, split3(both)):
                        part[at, to] = value

    @pl.when(s == pl.num_programs(0) - 1)
    def _():
        for y in range(4):
            here, after = pl.ds(y * 256, 256), pl.ds((y + 1) % 4 * 256, 256)
            for part in parts:
                part[after, here] = part[here, after].T
        q = q_ref[...]
        n = q.shape[0]
        def product(x, y_hi, y_mid, y_low, dims):
            hi, mid, low = x
            by_hi = lax.dot_general(jnp.concatenate([hi, mid, low], axis=0), y_hi, dims, preferred_element_type=F32)
            by_mid = lax.dot_general(jnp.concatenate([hi, mid], axis=0), y_mid, dims, preferred_element_type=F32)
            by_low = lax.dot_general(hi, y_low, dims, preferred_element_type=F32)
            small = by_hi[2 * n:] + by_mid[n:] + by_low
            return by_hi[:n] + (by_hi[n:2 * n] + by_mid[:n] + small)

        def solve(inv, x):
            hi, mid, low = split3(inv)
            left_parts = jnp.concatenate([hi, hi, mid, mid, hi, low], axis=1)
            right_parts = jnp.concatenate([x[0], x[1], x[0], x[1], x[2], x[0]], axis=0)
            return jnp.dot(left_parts, right_parts, preferred_element_type=F32)

        for turn in range(ITERS):
            q_parts = split3(q)
            u = product(q_parts, hi_ref[...], mid_ref[...], low_ref[...], (((1,), (0,)), ((), ())))
            u_parts = split3(u)
            inv = inverse_factor(product(u_parts, *q_parts, LANES))
            if turn == ITERS - 1:
                w_out[...] = solve(inv, q_parts)
            q = solve(inv, u_parts) * (1.0 / 32)
        q_out[...] = q


def iterate(pos, own, away, q):
    n, k = q.shape
    part = pl.BlockSpec((2,) + own.shape[1:], lambda s: (s, 0, 0, 0, 0))
    whole = pl.BlockSpec((n, k), lambda s: (0, 0))
    return pl.pallas_call(
        iterate_kernel,
        out_shape=(jax.ShapeDtypeStruct(q.shape, F32),) * 2,
        grid=(own.shape[0] // 2,),
        in_specs=[SMEM, part, part, whole],
        out_specs=(whole, whole),
        scratch_shapes=[pltpu.VMEM((k, k), BF16)] * 3,
        compiler_params=params(40),
        cost_estimate=cost(36 * n * k * k, 4 * k * k),
        name="iterations",
    )(pos, own, away, q)


def left_kernel(pos_ref, w_ref, m0, m1, m3, m2_top, m2_end, out_ref):
    total = None
    n = w_ref.shape[0]
    for turn, start, ref in ((0, 0, m0), (3, 0, m1), (1, 0, m3), (2, 0, m2_top), (2, 128, m2_end)):
        at = pl.multiple_of((pos_ref[1] + turn) % 4 * 256 + start, 128)
        whi, wlow = split2(w_ref[:, pl.ds(at, ref.shape[0])])
        mhi, mlow = split2(ref[...])
        both = jnp.dot(jnp.concatenate([whi, wlow], axis=0), mhi, preferred_element_type=F32)
        part = both[:n] + (both[n:] + jnp.dot(whi, mlow, preferred_element_type=F32))
        total = part if total is None else total + part
    out_ref[...] = total


def left(pos, w, blocks):
    n, d = w.shape[0], blocks[0].shape[1]
    return pl.pallas_call(
        left_kernel,
        out_shape=jax.ShapeDtypeStruct((n, d), F32),
        in_specs=[SMEM] + [VMEM] * 6,
        out_specs=VMEM,
        compiler_params=params(24),
        cost_estimate=cost(6 * n * d * 1024, 2 << 20),
        name="left",
    )(pos, w, *blocks)


TURNS = (2, 1, 3, 0)


def finish_kernel(pos_ref, mine_opp, mine, other_opp, other, mom, own, away, q, err_out, mom_out, q_parts):
    i = pl.program_id(0)

    @pl.when(i == 0)
    def _():
        hi, low = split2(q[...])
        q_parts[...] = jnp.concatenate([hi, hi, low, low], axis=0)

    def step(opp, rest, p_t):
        hi, low = split2(p_t[...])
        p_parts = jnp.concatenate([hi, low, hi, low], axis=0)
        for n, turn in enumerate(TURNS):
            cols = pl.ds(pl.multiple_of((pos_ref[1] + turn) % 4 * 256, 256), 256)
            merged = opp[0] if n == 0 else rest[n - 1]
            approx = lax.dot_general(p_parts, q_parts[:, cols], ROWS, preferred_element_type=F32)
            err_out[0, :, cols] = (merged - approx).astype(BF16)
            mom_out[:, cols] = (0.9 * mom[:, cols].astype(F32) + approx).astype(BF16)

    first = i < pl.num_programs(0) // 2

    @pl.when(first)
    def _():
        step(mine_opp, mine, own)

    @pl.when(jnp.logical_not(first))
    def _():
        step(other_opp, other, away)


def finish(pos, pieces, error, momentum, own, away, q):
    n, k = q.shape
    d = momentum.shape[0]
    rows = 256
    half = d // rows // 2

    def row(i, pos):
        return jnp.where(i < half, pos[0], 1 - pos[0]) * half + i % half

    def early(i):
        return jnp.minimum(i, half - 1)

    def late(i):
        return jnp.maximum(i - half, 0)

    def pieces_at(count, when):
        return pl.BlockSpec((count, rows, 256), lambda i, pos: (0, when(i), 0))

    return pl.pallas_call(
        finish_kernel,
        out_shape=(jax.ShapeDtypeStruct(error.shape, BF16), jax.ShapeDtypeStruct(momentum.shape, BF16)),
        grid_spec=pltpu.PrefetchScalarGridSpec(
            num_scalar_prefetch=1,
            grid=(d // rows,),
            in_specs=[
                pieces_at(1, early),
                pieces_at(3, early),
                pieces_at(1, late),
                pieces_at(3, late),
                pl.BlockSpec((rows, k), lambda i, pos: (row(i, pos), 0)),
                pl.BlockSpec((n, rows), lambda i, pos: (0, early(i))),
                pl.BlockSpec((n, rows), lambda i, pos: (0, late(i))),
                pl.BlockSpec((n, k), lambda i, pos: (0, 0)),
            ],
            out_specs=(
                pl.BlockSpec((1, rows, k), lambda i, pos: (0, row(i, pos), 0)),
                pl.BlockSpec((rows, k), lambda i, pos: (row(i, pos), 0)),
            ),
            scratch_shapes=[pltpu.VMEM((4 * n, k), BF16)],
        ),
        compiler_params=params(24),
        cost_estimate=cost(8 * n * d * k, 10 << 20),
        name="finish",
    )(pos, *pieces, momentum, own, away, q)


def shards(inputs, key_grads, error, momentum, q_start):
    i = lax.axis_index("dp")
    z, y, c = i // 8, (i // 2) % 4, i % 2
    pos = jnp.stack([c, y, z])

    args = (inputs, key_grads, error)
    other_opp, _ = merge(1 - c, y, TURNS[:1], *args)
    other_opp, away_core = lax.optimization_barrier((other_opp, 1 - c))
    sent_opp = dp_shift(other_opp, dc=1)
    other, _ = merge(away_core, y, TURNS[1:], *args)
    sent = dp_shift(other, dc=1)
    mine_opp, opposite = merge(c, y, TURNS[:1], *args, sent_opp)
    mine, sums = merge(c, y, TURNS[1:], *args, sent)
    came = ring_sum(opposite, sums[0:2], sums[2:4], lambda x, d: dp_shift(x, dy=d))
    *cut, own = sum_turn(pos, *sums[4:6], came)
    came = ring_sum(cut[0:2], cut[2:4], cut[4:6], lambda x, d: dp_shift(x, dz=d))
    unit, copies = make_unit(own, came)
    units = [unit] + [dp_shift(unit, dy=dy) for dy in (1, 2)]
    of_y = exchange(copies, Z_GROUPS).reshape(256, 512)
    of_y, *units = lax.optimization_barrier((of_y, *units))

    to_core, part = g_block(pos, units, of_y)
    part = part + dp_shift(to_core, dc=1)
    m1, m3 = dp_shift(of_y, dy=1), dp_shift(of_y, dy=-1)
    part = exchange(part, None, "shard").sum(axis=0)
    part, m1, m3 = lax.optimization_barrier((part, m1, m3))
    part = gather(part, 16, ZY_GROUPS)
    part, m1, m3 = lax.optimization_barrier((part, m1, m3))
    m2_top, m2_end = dp_shift(m1[:128], dy=1), dp_shift(m3[128:], dy=-1)
    part = gather(part, 8, None, "shard")
    part, m2_top, m2_end = lax.optimization_barrier((part, m2_top, m2_end))
    q_t, w = iterate(pos, part, dp_shift(part, dc=1), q_start.T)

    blocks = [of_y, m1, m3, m2_top, m2_end]
    own = left(pos, w, blocks)
    away = dp_shift(own, dc=1)
    new_error, new_momentum = finish(
        pos, (mine_opp, mine, other_opp, other), error, momentum, own, away, q_t
    )
    return (new_error, new_momentum, q_t.T)


def solution(mesh):
    return jax.shard_map(
        shards,
        mesh=mesh,
        in_specs=(P("dp", "shard"), P("dp", None), P("dp", "shard", None), P("shard", None), P()),
        out_specs=(P("dp", "shard", None), P("shard", None), P()),
        check_vma=False,
    )
```

```python
import functools
import math

import jax
import jax.numpy as jnp
from jax import lax
from jax.experimental import pallas as pl
from jax.experimental.pallas import tpu as pltpu
from jax.sharding import PartitionSpec as P

ITERS = 3
HIGH = lax.Precision.HIGHEST
ROWS = (((0,), (0,)), ((), ()))
LANES = (((1,), (1,)), ((), ()))
F32 = jnp.float32
BF16 = jnp.bfloat16
VMEM = pl.BlockSpec(memory_space=pltpu.VMEM)
SMEM = pl.BlockSpec(memory_space=pltpu.SMEM)

Z_GROUPS = [[z * 8 + y * 2 + c for z in range(4)] for y in range(4) for c in range(2)]
ZY_GROUPS = [[z * 8 + y * 2 + c for z in range(4) for y in range(4)] for c in range(2)]


def dp_shift(x, dz=0, dy=0, dc=0):
    pairs = []
    for i in range(32):
        z, y, c = i // 8, (i // 2) % 4, i % 2
        pairs.append((i, (z + dz) % 4 * 8 + (y + dy) % 4 * 2 + (c + dc) % 2))
    return lax.ppermute(x, "dp", pairs)


def ring_sum(opposite, following, before, step):
    relay_on, relay_back = step(opposite[0], 1), step(opposite[1], -1)
    second, first = step(following[1], 1), step(before[0], -1)
    relay_on, relay_back, second, first = lax.optimization_barrier((relay_on, relay_back, second, first))
    on, back = step(following[0] + relay_on, 1), step(before[1] + relay_back, -1)
    return on, second, first, back


def small_ring_sum(opposite, following, before, step):
    n = opposite[0].shape[0]
    relay_on, relay_back = step(opposite[0], 1), step(opposite[1], -1)
    on = step(following + jnp.pad(relay_on, ((0, n), (0, 0))), 1)
    back = step(before + jnp.pad(relay_back, ((n, 0), (0, 0))), -1)
    return on, back


def exchange(x, groups, axis="dp"):
    return lax.all_to_all(x, axis, 0, 0, axis_index_groups=groups)


def params(mib, **more):
    return pltpu.CompilerParams(vmem_limit_bytes=mib << 20, **more)


def cost(flops, read):
    return pl.CostEstimate(flops=flops, bytes_accessed=read, transcendentals=0)


def split2(x):
    hi = x.astype(BF16)
    return hi, (x - hi.astype(F32)).astype(BF16)


def split3(x):
    hi = x.astype(BF16)
    rest = x - hi.astype(F32)
    mid = rest.astype(BF16)
    return hi, mid, (rest - mid.astype(F32)).astype(BF16)


def merge_kernel(turns, own, added, pos_ref, acts, grads, err, *refs):
    sent, refs = (refs[0], refs[1:]) if added else (None, refs)
    out_ref, sums = refs[0], refs[1:]
    half = pos_ref[0] if own else 1 - pos_ref[0]
    d = acts.shape[1] // 2
    at_d = pl.ds(pl.multiple_of(half * d, 512), d)
    factor = 1.0 / math.sqrt(acts.shape[0])
    x = acts[:, at_d]
    for n, turn in enumerate(turns):
        cols = pl.ds(pl.multiple_of((pos_ref[1] + turn) % 4 * 256, 256), 256)
        product = lax.dot_general(x, grads[:, cols], ROWS, preferred_element_type=F32)
        merged = product * factor + err[0, at_d, cols].astype(F32)
        out_ref[n] = merged
        if added:
            total = merged + sent[n]
            sums[2 * n][...] = total[:d // 2]
            sums[2 * n + 1][...] = total[d // 2:]


def merge(pos, own, turns, inputs, key_grads, error, sent=None):
    tok, d = inputs.shape
    d = d // 2
    n = len(turns)
    added = sent is not None
    outs = [jax.ShapeDtypeStruct((n, d, 256), F32)]
    if added:
        outs += [jax.ShapeDtypeStruct((d // 2, 256), F32)] * (2 * n)
    result = pl.pallas_call(
        functools.partial(merge_kernel, turns, own, added),
        out_shape=tuple(outs),
        in_specs=[SMEM] + [VMEM] * (3 + added),
        out_specs=(VMEM,) * len(outs),
        compiler_params=params(24),
        cost_estimate=cost(2 * tok * d * 256 * n, (1 + 2 * n) << 19),
        name="merge",
    )(pos, inputs, key_grads, error, *([sent] if added else []))
    return result[0], list(result[1:])


def sum_turn_kernel(pos_ref, top, end, on, second, first, back, opp_top, opp_end, after, before, own, turned):
    turned[:, :256] = (top[...] + (on[...] + first[...])).T
    turned[:, 256:] = (end[...] + (second[...] + back[...])).T
    z = pos_ref[2]

    def rows(turn, start, size):
        return turned[pl.ds(pl.multiple_of((z + turn) % 4 * 64 + start, 32), size), :]

    opp_top[...] = rows(2, 0, 32)
    opp_end[...] = rows(2, 32, 32)
    after[...] = rows(1, 0, 64)
    before[...] = rows(3, 0, 64)
    own[...] = rows(0, 0, 64)


def sum_turn(pos, top, end, came):
    outs = tuple(jax.ShapeDtypeStruct((n, 512), F32) for n in (32, 32, 64, 64, 64))
    return pl.pallas_call(
        sum_turn_kernel,
        out_shape=outs,
        in_specs=[SMEM] + [VMEM] * 6,
        out_specs=(VMEM,) * 5,
        scratch_shapes=[pltpu.VMEM((256, 512), F32)],
        compiler_params=params(24),
        cost_estimate=cost(4 << 17, 3 << 20),
        name="sum_turn",
    )(pos, top, end, *came)


def spread_kernel(leading, keep, *refs):
    refs, outs = refs[:-1 - keep], refs[-1 - keep:]
    terms = [refs[0][i] for i in range(refs[0].shape[0])] if leading else [ref[...] for ref in refs]
    total = terms[0]
    for term in terms[1:]:
        total = total + term
    copies_ref = outs[0]
    for i in range(copies_ref.shape[0]):
        copies_ref[i] = total
    if keep:
        outs[1][...] = total


def spread(parts, copies, leading=False, keep=False):
    shape = parts[0].shape[1:] if leading else parts[0].shape
    outs = (jax.ShapeDtypeStruct((copies,) + shape, F32), jax.ShapeDtypeStruct(shape, F32))[:1 + keep]
    return pl.pallas_call(
        functools.partial(spread_kernel, leading, keep),
        out_shape=outs,
        in_specs=[VMEM] * len(parts),
        out_specs=(VMEM,) * len(outs),
        compiler_params=params(24),
        cost_estimate=cost(1 << 17, 1 << 20),
        name="spread",
    )(*parts)


def block_kernel(pos_ref, u0, u1, u2, of_y, sent_ref, mine_ref):
    core = pos_ref[0]
    rows = jnp.concatenate([u0[...], u1[...], u2[...]], axis=0)
    block = lax.dot_general(rows, of_y[...], LANES, precision=HIGH, preferred_element_type=F32)

    def put(ref, part):
        for e in range(3):
            for s in range(8):
                ref[s, e] = part[64 * e + 8 * s:64 * e + 8 * s + 8]

    @pl.when(core == 0)
    def _():
        put(mine_ref, block[:, :128])
        put(sent_ref, block[:, 128:])

    @pl.when(core == 1)
    def _():
        put(mine_ref, block[:, 128:])
        put(sent_ref, block[:, :128])


def g_block(pos, units, of_y):
    k, d = of_y.shape
    return pl.pallas_call(
        block_kernel,
        out_shape=(jax.ShapeDtypeStruct((8, 3, 8, 128), F32),) * 2,
        in_specs=[SMEM] + [VMEM] * 4,
        out_specs=(VMEM, VMEM),
        compiler_params=params(24),
        cost_estimate=cost(2 * 6 * 192 * k * d, 2 << 20),
        name="g_block",
    )(pos, *units, of_y)


def inverse_factor(gram):
    n = gram.shape[0]
    tiles = n // 8
    gram = 0.5 * (gram + gram.T)
    row = lax.broadcasted_iota(jnp.int32, (n, n), 0)
    col = lax.broadcasted_iota(jnp.int32, (n, n), 1)
    both = jnp.concatenate([gram, jnp.where(row == col, 1.0, 0.0)], axis=1)
    b = [both[8 * r:8 * r + 8] for r in range(tiles)]
    sub = lax.broadcasted_iota(jnp.int32, (8, 2 * n), 0)
    out = []
    for t in range(tiles):
        c = {
            (r, k): jnp.broadcast_to(b[r][:, 8 * t + k:8 * t + k + 1], (8, 2 * n))
            for r in range(t, tiles)
            for k in range(8)
        }
        pivots = jnp.ones((8, 2 * n), F32)
        for k in range(8):
            pivot = jnp.broadcast_to(c[t, k][k:k + 1], (8, 2 * n))
            pivots = jnp.where(sub == k, pivot, pivots)
            turn = pl.reciprocal(pivot, approx=True)
            turn = turn + turn * (1.0 - pivot * turn)
            turn = turn + turn * (1.0 - pivot * turn)
            lead = jnp.broadcast_to(b[t][k:k + 1], (8, 2 * n))
            heads = {l: jnp.broadcast_to(c[t, l][k:k + 1], (8, 2 * n)) for l in range(k + 1, 8)}
            for r in range(t, tiles):
                m = c[r, k] * turn
                for l in range(k + 1, 8):
                    c[r, l] = c[r, l] - m * heads[l]
                if r == t:
                    m = jnp.where(sub > k, m, 0.0)
                b[r] = b[r] - m * lead
        out.append(b[t] / jnp.sqrt(pivots))
    return jnp.concatenate(out, axis=0)[:, n:]


def iterate_kernel(pos_ref, own_ref, away_ref, q_ref, q_out, w_out, hi_ref, mid_ref, low_ref):
    s = pl.program_id(0)
    parts = (hi_ref, mid_ref, low_ref)
    for ref, core in ((own_ref, pos_ref[0]), (away_ref, 1 - pos_ref[0])):
        for z in range(4):
            for y in range(4):
                to = pl.ds(pl.multiple_of(y * 256 + core * 128, 128), 128)
                for e in range(3):
                    start = (y - e) % 4 * 256 + z * 64 + s * 16
                    at = pl.ds(pl.multiple_of(start, 16), 16)
                    both = jnp.concatenate([ref[0, z * 4 + y, e], ref[1, z * 4 + y, e]], axis=0)
                    for part, value in zip(parts, split3(both)):
                        part[at, to] = value

    @pl.when(s == pl.num_programs(0) - 1)
    def _():
        for y in range(4):
            here, after = pl.ds(y * 256, 256), pl.ds((y + 1) % 4 * 256, 256)
            for part in parts:
                part[after, here] = part[here, after].T
        q = q_ref[...]
        n = q.shape[0]
        def product(x, y_hi, y_mid, y_low, dims):
            hi, mid, low = x
            by_hi = lax.dot_general(jnp.concatenate([hi, mid, low], axis=0), y_hi, dims, preferred_element_type=F32)
            by_mid = lax.dot_general(jnp.concatenate([hi, mid], axis=0), y_mid, dims, preferred_element_type=F32)
            by_low = lax.dot_general(hi, y_low, dims, preferred_element_type=F32)
            small = by_hi[2 * n:] + by_mid[n:] + by_low
            return by_hi[:n] + (by_hi[n:2 * n] + by_mid[:n] + small)

        def solve(inv, x):
            hi, mid, low = split3(inv)
            left_parts = jnp.concatenate([hi, hi, mid, mid, hi, low], axis=1)
            right_parts = jnp.concatenate([x[0], x[1], x[0], x[1], x[2], x[0]], axis=0)
            return jnp.dot(left_parts, right_parts, preferred_element_type=F32)

        for turn in range(ITERS):
            q_parts = split3(q)
            u = product(q_parts, hi_ref[...], mid_ref[...], low_ref[...], (((1,), (0,)), ((), ())))
            u_parts = split3(u)
            inv = inverse_factor(product(u_parts, *q_parts, LANES))
            if turn == ITERS - 1:
                w_out[...] = solve(inv, q_parts)
            q = solve(inv, u_parts) * (1.0 / 32)
        q_out[...] = q


def iterate(pos, own, away, q):
    n, k = q.shape
    part = pl.BlockSpec((2,) + own.shape[1:], lambda s: (s, 0, 0, 0, 0))
    whole = pl.BlockSpec((n, k), lambda s: (0, 0))
    return pl.pallas_call(
        iterate_kernel,
        out_shape=(jax.ShapeDtypeStruct(q.shape, F32),) * 2,
        grid=(own.shape[0] // 2,),
        in_specs=[SMEM, part, part, whole],
        out_specs=(whole, whole),
        scratch_shapes=[pltpu.VMEM((k, k), BF16)] * 3,
        compiler_params=params(40),
        cost_estimate=cost(36 * n * k * k, 4 * k * k),
        name="iterations",
    )(pos, own, away, q)


def left_kernel(pos_ref, w_ref, m0, m1, m3, m2_top, m2_end, out_ref):
    total = None
    n = w_ref.shape[0]
    for turn, start, ref in ((0, 0, m0), (3, 0, m1), (1, 0, m3), (2, 0, m2_top), (2, 128, m2_end)):
        at = pl.multiple_of((pos_ref[1] + turn) % 4 * 256 + start, 128)
        whi, wlow = split2(w_ref[:, pl.ds(at, ref.shape[0])])
        mhi, mlow = split2(ref[...])
        both = jnp.dot(jnp.concatenate([whi, wlow], axis=0), mhi, preferred_element_type=F32)
        part = both[:n] + (both[n:] + jnp.dot(whi, mlow, preferred_element_type=F32))
        total = part if total is None else total + part
    out_ref[...] = total


def left(pos, w, blocks):
    n, d = w.shape[0], blocks[0].shape[1]
    return pl.pallas_call(
        left_kernel,
        out_shape=jax.ShapeDtypeStruct((n, d), F32),
        in_specs=[SMEM] + [VMEM] * 6,
        out_specs=VMEM,
        compiler_params=params(24),
        cost_estimate=cost(6 * n * d * 1024, 2 << 20),
        name="left",
    )(pos, w, *blocks)


TURNS = (2, 1, 3, 0)


def finish_kernel(pos_ref, mine_opp, mine, other_opp, other, mom, own, away, q, err_out, mom_out, q_parts):
    i = pl.program_id(0)

    @pl.when(i == 0)
    def _():
        hi, low = split2(q[...])
        q_parts[...] = jnp.concatenate([hi, hi, low, low], axis=0)

    def step(opp, rest, p_t):
        hi, low = split2(p_t[...])
        p_parts = jnp.concatenate([hi, low, hi, low], axis=0)
        for n, turn in enumerate(TURNS):
            cols = pl.ds(pl.multiple_of((pos_ref[1] + turn) % 4 * 256, 256), 256)
            merged = opp[0] if n == 0 else rest[n - 1]
            approx = lax.dot_general(p_parts, q_parts[:, cols], ROWS, preferred_element_type=F32)
            err_out[0, :, cols] = (merged - approx).astype(BF16)
            mom_out[:, cols] = (0.9 * mom[:, cols].astype(F32) + approx).astype(BF16)

    first = i < pl.num_programs(0) // 2

    @pl.when(first)
    def _():
        step(mine_opp, mine, own)

    @pl.when(jnp.logical_not(first))
    def _():
        step(other_opp, other, away)


def finish(pos, pieces, error, momentum, own, away, q):
    n, k = q.shape
    d = momentum.shape[0]
    rows = 256
    half = d // rows // 2

    def row(i, pos):
        return jnp.where(i < half, pos[0], 1 - pos[0]) * half + i % half

    def early(i):
        return jnp.minimum(i, half - 1)

    def late(i):
        return jnp.maximum(i - half, 0)

    def pieces_at(count, when):
        return pl.BlockSpec((count, rows, 256), lambda i, pos: (0, when(i), 0))

    return pl.pallas_call(
        finish_kernel,
        out_shape=(jax.ShapeDtypeStruct(error.shape, BF16), jax.ShapeDtypeStruct(momentum.shape, BF16)),
        grid_spec=pltpu.PrefetchScalarGridSpec(
            num_scalar_prefetch=1,
            grid=(d // rows,),
            in_specs=[
                pieces_at(1, early),
                pieces_at(3, early),
                pieces_at(1, late),
                pieces_at(3, late),
                pl.BlockSpec((rows, k), lambda i, pos: (row(i, pos), 0)),
                pl.BlockSpec((n, rows), lambda i, pos: (0, early(i))),
                pl.BlockSpec((n, rows), lambda i, pos: (0, late(i))),
                pl.BlockSpec((n, k), lambda i, pos: (0, 0)),
            ],
            out_specs=(
                pl.BlockSpec((1, rows, k), lambda i, pos: (0, row(i, pos), 0)),
                pl.BlockSpec((rows, k), lambda i, pos: (row(i, pos), 0)),
            ),
            scratch_shapes=[pltpu.VMEM((4 * n, k), BF16)],
        ),
        compiler_params=params(24),
        cost_estimate=cost(8 * n * d * k, 10 << 20),
        name="finish",
    )(pos, *pieces, momentum, own, away, q)


def shards(inputs, key_grads, error, momentum, q_start):
    i = lax.axis_index("dp")
    z, y, c = i // 8, (i // 2) % 4, i % 2
    pos = jnp.stack([c, y, z])

    args = (inputs, key_grads, error)
    other_opp, _ = merge(pos, False, TURNS[:1], *args)
    other_opp, pos = lax.optimization_barrier((other_opp, pos))
    sent_opp = dp_shift(other_opp, dc=1)
    other, _ = merge(pos, False, TURNS[1:], *args)
    sent = dp_shift(other, dc=1)
    mine_opp, opposite = merge(pos, True, TURNS[:1], *args, sent_opp)
    mine, sums = merge(pos, True, TURNS[1:], *args, sent)
    came = ring_sum(opposite, sums[0:2], sums[2:4], lambda x, d: dp_shift(x, dy=d))
    *opposite, after, before, own = sum_turn(pos, *sums[4:6], came)
    came = small_ring_sum(opposite, after, before, lambda x, d: dp_shift(x, dz=d))
    copies, unit = spread([own, *came], 4, keep=True)
    units = [unit] + [dp_shift(unit, dy=dy) for dy in (1, 2)]
    of_y = exchange(copies, Z_GROUPS).reshape(256, 512)
    of_y, *units = lax.optimization_barrier((of_y, *units))

    to_core, part = g_block(pos, units, of_y)
    part = part + dp_shift(to_core, dc=1)
    m1, m3 = dp_shift(of_y, dy=1), dp_shift(of_y, dy=-1)
    (copies,) = spread([exchange(part, None, "shard")], 16, leading=True)
    copies, m1, m3 = lax.optimization_barrier((copies, m1, m3))
    part = exchange(copies, ZY_GROUPS)
    part, m1, m3 = lax.optimization_barrier((part, m1, m3))
    m2_top, m2_end = dp_shift(m1[:128], dy=1), dp_shift(m3[128:], dy=-1)
    part = exchange(spread([part], 8)[0], None, "shard")
    part, m2_top, m2_end = lax.optimization_barrier((part, m2_top, m2_end))
    q_t, w = iterate(pos, part, dp_shift(part, dc=1), q_start.T)

    blocks = [of_y, m1, m3, m2_top, m2_end]
    own = left(pos, w, blocks)
    away = dp_shift(own, dc=1)
    new_error, new_momentum = finish(
        pos, (mine_opp, mine, other_opp, other), error, momentum, own, away, q_t
    )
    return (new_error, new_momentum, q_t.T)


def solution(mesh):
    return jax.shard_map(
        shards,
        mesh=mesh,
        in_specs=(P("dp", "shard"), P("dp", None), P("dp", "shard", None), P("shard", None), P()),
        out_specs=(P("dp", "shard", None), P("shard", None), P()),
        check_vma=False,
    )
```

```python
import functools
import math

import jax
import jax.numpy as jnp
from jax import lax
from jax.experimental import pallas as pl
from jax.experimental.pallas import tpu as pltpu
from jax.sharding import PartitionSpec as P

ITERS = 3
HIGH = lax.Precision.HIGHEST
ROWS = (((0,), (0,)), ((), ()))
LANES = (((1,), (1,)), ((), ()))
F32 = jnp.float32
BF16 = jnp.bfloat16
VMEM = pl.BlockSpec(memory_space=pltpu.VMEM)
SMEM = pl.BlockSpec(memory_space=pltpu.SMEM)

Z_GROUPS = [[z * 8 + y * 2 + c for z in range(4)] for y in range(4) for c in range(2)]
ZY_GROUPS = [[z * 8 + y * 2 + c for z in range(4) for y in range(4)] for c in range(2)]


def dp_shift(x, dz=0, dy=0, dc=0):
    pairs = []
    for i in range(32):
        z, y, c = i // 8, (i // 2) % 4, i % 2
        pairs.append((i, (z + dz) % 4 * 8 + (y + dy) % 4 * 2 + (c + dc) % 2))
    return lax.ppermute(x, "dp", pairs)


def ring_sum(opposite, following, before, step):
    relay_on, relay_back = step(opposite[0], 1), step(opposite[1], -1)
    second, first = step(following[1], 1), step(before[0], -1)
    relay_on, relay_back, second, first = lax.optimization_barrier((relay_on, relay_back, second, first))
    on, back = step(following[0] + relay_on, 1), step(before[1] + relay_back, -1)
    return on, second, first, back


def small_ring_sum(opposite, following, before, step):
    n = opposite[0].shape[0]
    relay_on, relay_back = step(opposite[0], 1), step(opposite[1], -1)
    on = step(following + jnp.pad(relay_on, ((0, n), (0, 0))), 1)
    back = step(before + jnp.pad(relay_back, ((n, 0), (0, 0))), -1)
    return on, back


def exchange(x, groups, axis="dp"):
    return lax.all_to_all(x, axis, 0, 0, axis_index_groups=groups)


def params(mib, **more):
    return pltpu.CompilerParams(vmem_limit_bytes=mib << 20, **more)


def cost(flops, read):
    return pl.CostEstimate(flops=flops, bytes_accessed=read, transcendentals=0)


def split2(x):
    hi = x.astype(BF16)
    return hi, (x - hi.astype(F32)).astype(BF16)


def split3(x):
    hi = x.astype(BF16)
    rest = x - hi.astype(F32)
    mid = rest.astype(BF16)
    return hi, mid, (rest - mid.astype(F32)).astype(BF16)


def merge_kernel(turns, own, added, pos_ref, acts, grads, err, *refs):
    sent, refs = (refs[0], refs[1:]) if added else (None, refs)
    out_ref, sums = refs[0], refs[1:]
    half = pos_ref[0] if own else 1 - pos_ref[0]
    d = acts.shape[1] // 2
    at_d = pl.ds(pl.multiple_of(half * d, 512), d)
    factor = 1.0 / math.sqrt(acts.shape[0])
    x = acts[:, at_d]
    for n, turn in enumerate(turns):
        cols = pl.ds(pl.multiple_of((pos_ref[1] + turn) % 4 * 256, 256), 256)
        product = lax.dot_general(x, grads[:, cols], ROWS, preferred_element_type=F32)
        merged = product * factor + err[0, at_d, cols].astype(F32)
        out_ref[n] = merged
        if added:
            total = merged + sent[n]
            sums[2 * n][...] = total[:d // 2]
            sums[2 * n + 1][...] = total[d // 2:]


def merge(pos, own, turns, inputs, key_grads, error, sent=None):
    tok, d = inputs.shape
    d = d // 2
    n = len(turns)
    added = sent is not None
    outs = [jax.ShapeDtypeStruct((n, d, 256), F32)]
    if added:
        outs += [jax.ShapeDtypeStruct((d // 2, 256), F32)] * (2 * n)
    result = pl.pallas_call(
        functools.partial(merge_kernel, turns, own, added),
        out_shape=tuple(outs),
        in_specs=[SMEM] + [VMEM] * (3 + added),
        out_specs=(VMEM,) * len(outs),
        compiler_params=params(16),
        cost_estimate=cost(2 * tok * d * 256 * n, (1 + 2 * n) << 19),
        name="merge",
    )(pos, inputs, key_grads, error, *([sent] if added else []))
    return result[0], list(result[1:])


def sum_turn_kernel(pos_ref, top, end, on, second, first, back, opp_top, opp_end, after, before, own, turned):
    turned[:, :256] = (top[...] + (on[...] + first[...])).T
    turned[:, 256:] = (end[...] + (second[...] + back[...])).T
    z = pos_ref[2]

    def rows(turn, start, size):
        return turned[pl.ds(pl.multiple_of((z + turn) % 4 * 64 + start, 32), size), :]

    opp_top[...] = rows(2, 0, 32)
    opp_end[...] = rows(2, 32, 32)
    after[...] = rows(1, 0, 64)
    before[...] = rows(3, 0, 64)
    own[...] = rows(0, 0, 64)


def sum_turn(pos, top, end, came):
    outs = tuple(jax.ShapeDtypeStruct((n, 512), F32) for n in (32, 32, 64, 64, 64))
    return pl.pallas_call(
        sum_turn_kernel,
        out_shape=outs,
        in_specs=[SMEM] + [VMEM] * 6,
        out_specs=(VMEM,) * 5,
        scratch_shapes=[pltpu.VMEM((256, 512), F32)],
        compiler_params=params(16),
        cost_estimate=cost(4 << 17, 3 << 20),
        name="sum_turn",
    )(pos, top, end, *came)


def spread_kernel(leading, keep, *refs):
    refs, outs = refs[:-1 - keep], refs[-1 - keep:]
    terms = [refs[0][i] for i in range(refs[0].shape[0])] if leading else [ref[...] for ref in refs]
    total = terms[0]
    for term in terms[1:]:
        total = total + term
    copies_ref = outs[0]
    for i in range(copies_ref.shape[0]):
        copies_ref[i] = total
    if keep:
        outs[1][...] = total


def spread(parts, copies, leading=False, keep=False):
    shape = parts[0].shape[1:] if leading else parts[0].shape
    outs = (jax.ShapeDtypeStruct((copies,) + shape, F32), jax.ShapeDtypeStruct(shape, F32))[:1 + keep]
    return pl.pallas_call(
        functools.partial(spread_kernel, leading, keep),
        out_shape=outs,
        in_specs=[VMEM] * len(parts),
        out_specs=(VMEM,) * len(outs),
        compiler_params=params(16),
        cost_estimate=cost(1 << 17, 1 << 20),
        name="spread",
    )(*parts)


def block_kernel(pos_ref, u0, u1, u2, of_y, sent_ref, mine_ref):
    core = pos_ref[0]
    rows = jnp.concatenate([u0[...], u1[...], u2[...]], axis=0)
    block = lax.dot_general(rows, of_y[...], LANES, precision=HIGH, preferred_element_type=F32)

    def put(ref, part):
        for e in range(3):
            for s in range(8):
                ref[s, e] = part[64 * e + 8 * s:64 * e + 8 * s + 8]

    @pl.when(core == 0)
    def _():
        put(mine_ref, block[:, :128])
        put(sent_ref, block[:, 128:])

    @pl.when(core == 1)
    def _():
        put(mine_ref, block[:, 128:])
        put(sent_ref, block[:, :128])


def g_block(pos, units, of_y):
    k, d = of_y.shape
    return pl.pallas_call(
        block_kernel,
        out_shape=(jax.ShapeDtypeStruct((8, 3, 8, 128), F32),) * 2,
        in_specs=[SMEM] + [VMEM] * 4,
        out_specs=(VMEM, VMEM),
        compiler_params=params(16),
        cost_estimate=cost(2 * 6 * 192 * k * d, 2 << 20),
        name="g_block",
    )(pos, *units, of_y)


def inverse_factor(gram):
    n = gram.shape[0]
    tiles = n // 8
    gram = 0.5 * (gram + gram.T)
    row = lax.broadcasted_iota(jnp.int32, (n, n), 0)
    col = lax.broadcasted_iota(jnp.int32, (n, n), 1)
    both = jnp.concatenate([gram, jnp.where(row == col, 1.0, 0.0)], axis=1)
    b = [both[8 * r:8 * r + 8] for r in range(tiles)]
    sub = lax.broadcasted_iota(jnp.int32, (8, 2 * n), 0)
    out = []
    for t in range(tiles):
        c = {
            (r, k): jnp.broadcast_to(b[r][:, 8 * t + k:8 * t + k + 1], (8, 2 * n))
            for r in range(t, tiles)
            for k in range(8)
        }
        pivots = jnp.ones((8, 2 * n), F32)
        for k in range(8):
            pivot = jnp.broadcast_to(c[t, k][k:k + 1], (8, 2 * n))
            pivots = jnp.where(sub == k, pivot, pivots)
            turn = 1.0 / pivot
            lead = jnp.broadcast_to(b[t][k:k + 1], (8, 2 * n))
            heads = {l: jnp.broadcast_to(c[t, l][k:k + 1], (8, 2 * n)) for l in range(k + 1, 8)}
            for r in range(t, tiles):
                m = c[r, k] * turn
                for l in range(k + 1, 8):
                    c[r, l] = c[r, l] - m * heads[l]
                if r == t:
                    m = jnp.where(sub > k, m, 0.0)
                b[r] = b[r] - m * lead
        out.append(b[t] / jnp.sqrt(pivots))
    return jnp.concatenate(out, axis=0)[:, n:]


def iterate_kernel(pos_ref, own_ref, away_ref, q_ref, q_out, w_out, hi_ref, mid_ref, low_ref):
    s = pl.program_id(0)
    parts = (hi_ref, mid_ref, low_ref)
    for ref, core in ((own_ref, pos_ref[0]), (away_ref, 1 - pos_ref[0])):
        for z in range(4):
            for y in range(4):
                to = pl.ds(pl.multiple_of(y * 256 + core * 128, 128), 128)
                for e in range(3):
                    start = (y - e) % 4 * 256 + z * 64 + s * 16
                    at = pl.ds(pl.multiple_of(start, 16), 16)
                    both = jnp.concatenate([ref[0, z * 4 + y, e], ref[1, z * 4 + y, e]], axis=0)
                    for part, value in zip(parts, split3(both)):
                        part[at, to] = value

    @pl.when(s == pl.num_programs(0) - 1)
    def _():
        for y in range(4):
            here, after = pl.ds(y * 256, 256), pl.ds((y + 1) % 4 * 256, 256)
            for part in parts:
                part[after, here] = part[here, after].T
        q = q_ref[...]
        n = q.shape[0]
        def product(x, y_hi, y_mid, y_low, dims):
            hi, mid, low = x
            by_hi = lax.dot_general(jnp.concatenate([hi, mid, low], axis=0), y_hi, dims, preferred_element_type=F32)
            by_mid = lax.dot_general(jnp.concatenate([hi, mid], axis=0), y_mid, dims, preferred_element_type=F32)
            by_low = lax.dot_general(hi, y_low, dims, preferred_element_type=F32)
            small = by_hi[2 * n:] + by_mid[n:] + by_low
            return by_hi[:n] + (by_hi[n:2 * n] + by_mid[:n] + small)

        def solve(inv, x):
            hi, mid, low = split3(inv)
            left_parts = jnp.concatenate([hi, hi, mid, mid, hi, low], axis=1)
            right_parts = jnp.concatenate([x[0], x[1], x[0], x[1], x[2], x[0]], axis=0)
            return jnp.dot(left_parts, right_parts, preferred_element_type=F32)

        def times_g(x):
            return product(x, hi_ref[...], mid_ref[...], low_ref[...], (((1,), (0,)), ((), ())))

        q_parts = split3(q)
        u = times_g(q_parts)
        for turn in range(ITERS):
            u_parts = split3(u)
            gram = product(u_parts, *q_parts, LANES)
            last = turn == ITERS - 1
            v_parts = None if last else split3(times_g(u_parts))
            inv = inverse_factor(gram)
            if last:
                w_out[...] = solve(inv, q_parts)
            q = solve(inv, u_parts) * (1.0 / 32)
            if not last:
                q_parts = split3(q)
                u = solve(inv, v_parts) * (1.0 / 32)
        q_out[...] = q


def iterate(pos, own, away, q):
    n, k = q.shape
    part = pl.BlockSpec((2,) + own.shape[1:], lambda s: (s, 0, 0, 0, 0))
    whole = pl.BlockSpec((n, k), lambda s: (0, 0))
    return pl.pallas_call(
        iterate_kernel,
        out_shape=(jax.ShapeDtypeStruct(q.shape, F32),) * 2,
        grid=(own.shape[0] // 2,),
        in_specs=[SMEM, part, part, whole],
        out_specs=(whole, whole),
        scratch_shapes=[pltpu.VMEM((k, k), BF16)] * 3,
        compiler_params=params(20),
        cost_estimate=cost(36 * n * k * k, 4 * k * k),
        name="iterations",
    )(pos, own, away, q)


def left_kernel(pos_ref, w_ref, m0, m1, m3, m2_top, m2_end, out_ref):
    total = None
    n = w_ref.shape[0]
    for turn, start, ref in ((0, 0, m0), (3, 0, m1), (1, 0, m3), (2, 0, m2_top), (2, 128, m2_end)):
        at = pl.multiple_of((pos_ref[1] + turn) % 4 * 256 + start, 128)
        whi, wlow = split2(w_ref[:, pl.ds(at, ref.shape[0])])
        mhi, mlow = split2(ref[...])
        both = jnp.dot(jnp.concatenate([whi, wlow], axis=0), mhi, preferred_element_type=F32)
        part = both[:n] + (both[n:] + jnp.dot(whi, mlow, preferred_element_type=F32))
        total = part if total is None else total + part
    out_ref[...] = total


def left(pos, w, blocks):
    n, d = w.shape[0], blocks[0].shape[1]
    return pl.pallas_call(
        left_kernel,
        out_shape=jax.ShapeDtypeStruct((n, d), F32),
        in_specs=[SMEM] + [VMEM] * 6,
        out_specs=VMEM,
        compiler_params=params(16),
        cost_estimate=cost(6 * n * d * 1024, 2 << 20),
        name="left",
    )(pos, w, *blocks)


TURNS = (2, 1, 3, 0)


def finish_kernel(pos_ref, mine_opp, mine, other_opp, other, mom, own, away, q, err_out, mom_out, q_parts):
    i = pl.program_id(0)

    @pl.when(i == 0)
    def _():
        hi, low = split2(q[...])
        q_parts[...] = jnp.concatenate([hi, hi, low, low], axis=0)

    def step(opp, rest, p_t):
        hi, low = split2(p_t[...])
        p_parts = jnp.concatenate([hi, low, hi, low], axis=0)
        for n, turn in enumerate(TURNS):
            cols = pl.ds(pl.multiple_of((pos_ref[1] + turn) % 4 * 256, 256), 256)
            merged = opp[0] if n == 0 else rest[n - 1]
            approx = lax.dot_general(p_parts, q_parts[:, cols], ROWS, preferred_element_type=F32)
            err_out[0, :, cols] = (merged - approx).astype(BF16)
            mom_out[:, cols] = (0.9 * mom[:, cols].astype(F32) + approx).astype(BF16)

    first = i < pl.num_programs(0) // 2

    @pl.when(first)
    def _():
        step(mine_opp, mine, own)

    @pl.when(jnp.logical_not(first))
    def _():
        step(other_opp, other, away)


def finish(pos, pieces, error, momentum, own, away, q):
    n, k = q.shape
    d = momentum.shape[0]
    rows = 256
    half = d // rows // 2

    def row(i, pos):
        return jnp.where(i < half, pos[0], 1 - pos[0]) * half + i % half

    def early(i):
        return jnp.minimum(i, half - 1)

    def late(i):
        return jnp.maximum(i - half, 0)

    def pieces_at(count, when):
        return pl.BlockSpec((count, rows, 256), lambda i, pos: (0, when(i), 0))

    return pl.pallas_call(
        finish_kernel,
        out_shape=(jax.ShapeDtypeStruct(error.shape, BF16), jax.ShapeDtypeStruct(momentum.shape, BF16)),
        grid_spec=pltpu.PrefetchScalarGridSpec(
            num_scalar_prefetch=1,
            grid=(d // rows,),
            in_specs=[
                pieces_at(1, early),
                pieces_at(3, early),
                pieces_at(1, late),
                pieces_at(3, late),
                pl.BlockSpec((rows, k), lambda i, pos: (row(i, pos), 0)),
                pl.BlockSpec((n, rows), lambda i, pos: (0, early(i))),
                pl.BlockSpec((n, rows), lambda i, pos: (0, late(i))),
                pl.BlockSpec((n, k), lambda i, pos: (0, 0)),
            ],
            out_specs=(
                pl.BlockSpec((1, rows, k), lambda i, pos: (0, row(i, pos), 0)),
                pl.BlockSpec((rows, k), lambda i, pos: (row(i, pos), 0)),
            ),
            scratch_shapes=[pltpu.VMEM((4 * n, k), BF16)],
        ),
        compiler_params=params(16),
        cost_estimate=cost(8 * n * d * k, 10 << 20),
        name="finish",
    )(pos, *pieces, momentum, own, away, q)


def shards(inputs, key_grads, error, momentum, q_start):
    i = lax.axis_index("dp")
    z, y, c = i // 8, (i // 2) % 4, i % 2
    pos = jnp.stack([c, y, z])

    args = (inputs, key_grads, error)
    other_opp, _ = merge(pos, False, TURNS[:1], *args)
    other_opp, pos = lax.optimization_barrier((other_opp, pos))
    sent_opp = dp_shift(other_opp, dc=1)
    other, _ = merge(pos, False, TURNS[1:], *args)
    other, sent_opp = lax.optimization_barrier((other, sent_opp))
    sent = dp_shift(other, dc=1)
    mine_opp, opposite = merge(pos, True, TURNS[:1], *args, sent_opp)
    mine, sums = merge(pos, True, TURNS[1:], *args, sent)
    came = ring_sum(opposite, sums[0:2], sums[2:4], lambda x, d: dp_shift(x, dy=d))
    *opposite, after, before, own = sum_turn(pos, *sums[4:6], came)
    came = small_ring_sum(opposite, after, before, lambda x, d: dp_shift(x, dz=d))
    copies, unit = spread([own, *came], 4, keep=True)
    units = [unit] + [dp_shift(unit, dy=dy) for dy in (1, 2)]
    of_y = exchange(copies, Z_GROUPS).reshape(256, 512)
    of_y, *units = lax.optimization_barrier((of_y, *units))

    to_core, part = g_block(pos, units, of_y)
    part = part + dp_shift(to_core, dc=1)
    m1, m3 = dp_shift(of_y, dy=1), dp_shift(of_y, dy=-1)
    (copies,) = spread([exchange(part, None, "shard")], 16, leading=True)
    copies, m1, m3 = lax.optimization_barrier((copies, m1, m3))
    part = exchange(copies, ZY_GROUPS)
    part, m1, m3 = lax.optimization_barrier((part, m1, m3))
    m2_top, m2_end = dp_shift(m1[:128], dy=1), dp_shift(m3[128:], dy=-1)
    part = exchange(spread([part], 8)[0], None, "shard")
    part, m2_top, m2_end = lax.optimization_barrier((part, m2_top, m2_end))
    q_t, w = iterate(pos, part, dp_shift(part, dc=1), q_start.T)

    blocks = [of_y, m1, m3, m2_top, m2_end]
    own = left(pos, w, blocks)
    away = dp_shift(own, dc=1)
    new_error, new_momentum = finish(
        pos, (mine_opp, mine, other_opp, other), error, momentum, own, away, q_t
    )
    return (new_error, new_momentum, q_t.T)


def solution(mesh):
    return jax.shard_map(
        shards,
        mesh=mesh,
        in_specs=(P("dp", "shard"), P("dp", None), P("dp", "shard", None), P("shard", None), P()),
        out_specs=(P("dp", "shard", None), P("shard", None), P()),
        check_vma=False,
    )
```

```python
import functools
import math

import jax
import jax.numpy as jnp
from jax import lax
from jax.experimental import pallas as pl
from jax.experimental.pallas import tpu as pltpu
from jax.sharding import PartitionSpec as P

ITERS = 3
HIGH = lax.Precision.HIGHEST
ROWS = (((0,), (0,)), ((), ()))
LANES = (((1,), (1,)), ((), ()))
F32 = jnp.float32
BF16 = jnp.bfloat16
VMEM = pl.BlockSpec(memory_space=pltpu.VMEM)
SMEM = pl.BlockSpec(memory_space=pltpu.SMEM)

Z_GROUPS = [[z * 8 + y * 2 + c for z in range(4)] for y in range(4) for c in range(2)]
ZY_GROUPS = [[z * 8 + y * 2 + c for z in range(4) for y in range(4)] for c in range(2)]


def dp_shift(x, dz=0, dy=0, dc=0):
    pairs = []
    for i in range(32):
        z, y, c = i // 8, (i // 2) % 4, i % 2
        pairs.append((i, (z + dz) % 4 * 8 + (y + dy) % 4 * 2 + (c + dc) % 2))
    return lax.ppermute(x, "dp", pairs)


def ring_sum(opposite, following, before, step):
    relay_on, relay_back = step(opposite[0], 1), step(opposite[1], -1)
    second, first = step(following[1], 1), step(before[0], -1)
    relay_on, relay_back, second, first = lax.optimization_barrier((relay_on, relay_back, second, first))
    on, back = step(following[0] + relay_on, 1), step(before[1] + relay_back, -1)
    return on, second, first, back


def small_ring_sum(opposite, following, before, step):
    n = opposite[0].shape[0]
    relay_on, relay_back = step(opposite[0], 1), step(opposite[1], -1)
    on = step(following + jnp.pad(relay_on, ((0, n), (0, 0))), 1)
    back = step(before + jnp.pad(relay_back, ((n, 0), (0, 0))), -1)
    return on, back


def exchange(x, groups, axis="dp"):
    return lax.all_to_all(x, axis, 0, 0, axis_index_groups=groups)


def params(mib, **more):
    return pltpu.CompilerParams(vmem_limit_bytes=mib << 20, **more)


def cost(flops, read):
    return pl.CostEstimate(flops=flops, bytes_accessed=read, transcendentals=0)


def split2(x):
    hi = x.astype(BF16)
    return hi, (x - hi.astype(F32)).astype(BF16)


def split3(x):
    hi = x.astype(BF16)
    rest = x - hi.astype(F32)
    mid = rest.astype(BF16)
    return hi, mid, (rest - mid.astype(F32)).astype(BF16)


def merge_kernel(turns, own, pos_ref, acts, grads, err, *refs):
    half = pos_ref[0] if own else 1 - pos_ref[0]
    d = acts.shape[1] // 2
    at_d = pl.ds(pl.multiple_of(half * d, 512), d)
    factor = 1.0 / math.sqrt(acts.shape[0])
    x = acts[:, at_d]
    for n, turn in enumerate(turns):
        cols = pl.ds(pl.multiple_of((pos_ref[1] + turn) % 4 * 256, 256), 256)
        product = lax.dot_general(x, grads[:, cols], ROWS, preferred_element_type=F32)
        merged = product * factor + err[0, at_d, cols].astype(F32)
        if own:
            total = merged + refs[0][n]
            refs[1 + 2 * n][...] = total[:d // 2]
            refs[2 + 2 * n][...] = total[d // 2:]
        else:
            refs[0][n] = merged


def merge(pos, turns, inputs, key_grads, error, sent=None):
    tok, d = inputs.shape
    d = d // 2
    n = len(turns)
    own = sent is not None
    outs = (jax.ShapeDtypeStruct((d // 2, 256), F32),) * (2 * n) if own else jax.ShapeDtypeStruct((n, d, 256), F32)
    return pl.pallas_call(
        functools.partial(merge_kernel, turns, own),
        out_shape=outs,
        in_specs=[SMEM] + [VMEM] * (3 + own),
        out_specs=(VMEM,) * (2 * n) if own else VMEM,
        compiler_params=params(16),
        cost_estimate=cost(2 * tok * d * 256 * n, (1 + 2 * n) << 19),
        name="merge",
    )(pos, inputs, key_grads, error, *([sent] if own else []))


def merge_all_kernel(acts, grads, err, q, out_ref, q_parts):
    factor = 1.0 / math.sqrt(acts.shape[0])
    product = lax.dot_general(acts[...], grads[...], ROWS, preferred_element_type=F32)
    out_ref[...] = product * factor + err[0].astype(F32)

    @pl.when(pl.program_id(0) == 0)
    def _():
        for n, part in enumerate(split3(q[...])):
            q_parts[n] = part


def merge_all(inputs, key_grads, error, q):
    tok, d = inputs.shape
    k = key_grads.shape[1]
    rows = 256
    return pl.pallas_call(
        merge_all_kernel,
        out_shape=(jax.ShapeDtypeStruct((d, k), F32), jax.ShapeDtypeStruct((3,) + q.shape, BF16)),
        grid=(d // rows,),
        in_specs=[
            pl.BlockSpec((tok, rows), lambda i: (0, i)),
            pl.BlockSpec((tok, k), lambda i: (0, 0)),
            pl.BlockSpec((1, rows, k), lambda i: (0, i, 0)),
            pl.BlockSpec(q.shape, lambda i: (0, 0)),
        ],
        out_specs=(
            pl.BlockSpec((rows, k), lambda i: (i, 0)),
            pl.BlockSpec((3,) + q.shape, lambda i: (0, 0, 0)),
        ),
        compiler_params=params(16),
        cost_estimate=cost(2 * tok * d * k, 8 << 20),
        name="merge_all",
    )(inputs, key_grads, error, q)


def sum_turn_kernel(pos_ref, top, end, on, second, first, back, opp_top, opp_end, after, before, own, turned):
    turned[:, :256] = (top[...] + (on[...] + first[...])).T
    turned[:, 256:] = (end[...] + (second[...] + back[...])).T
    z = pos_ref[2]

    def rows(turn, start, size):
        return turned[pl.ds(pl.multiple_of((z + turn) % 4 * 64 + start, 32), size), :]

    opp_top[...] = rows(2, 0, 32)
    opp_end[...] = rows(2, 32, 32)
    after[...] = rows(1, 0, 64)
    before[...] = rows(3, 0, 64)
    own[...] = rows(0, 0, 64)


def sum_turn(pos, top, end, came):
    outs = tuple(jax.ShapeDtypeStruct((n, 512), F32) for n in (32, 32, 64, 64, 64))
    return pl.pallas_call(
        sum_turn_kernel,
        out_shape=outs,
        in_specs=[SMEM] + [VMEM] * 6,
        out_specs=(VMEM,) * 5,
        scratch_shapes=[pltpu.VMEM((256, 512), F32)],
        compiler_params=params(16),
        cost_estimate=cost(4 << 17, 3 << 20),
        name="sum_turn",
    )(pos, top, end, *came)


def spread_kernel(leading, keep, *refs):
    refs, outs = refs[:-1 - keep], refs[-1 - keep:]
    terms = [refs[0][i] for i in range(refs[0].shape[0])] if leading else [ref[...] for ref in refs]
    total = terms[0]
    for term in terms[1:]:
        total = total + term
    copies_ref = outs[0]
    for i in range(copies_ref.shape[0]):
        copies_ref[i] = total
    if keep:
        outs[1][...] = total


def spread(parts, copies, leading=False, keep=False):
    shape = parts[0].shape[1:] if leading else parts[0].shape
    outs = (jax.ShapeDtypeStruct((copies,) + shape, F32), jax.ShapeDtypeStruct(shape, F32))[:1 + keep]
    return pl.pallas_call(
        functools.partial(spread_kernel, leading, keep),
        out_shape=outs,
        in_specs=[VMEM] * len(parts),
        out_specs=(VMEM,) * len(outs),
        compiler_params=params(16),
        cost_estimate=cost(1 << 17, 1 << 20),
        name="spread",
    )(*parts)


def block_kernel(pos_ref, u0, u1, u2, of_y, sent_ref, mine_ref):
    core = pos_ref[0]
    rows = jnp.concatenate([u0[...], u1[...], u2[...]], axis=0)
    block = lax.dot_general(rows, of_y[...], LANES, precision=HIGH, preferred_element_type=F32)

    def put(ref, part):
        for e in range(3):
            for s in range(8):
                ref[s, e] = part[64 * e + 8 * s:64 * e + 8 * s + 8]

    @pl.when(core == 0)
    def _():
        put(mine_ref, block[:, :128])
        put(sent_ref, block[:, 128:])

    @pl.when(core == 1)
    def _():
        put(mine_ref, block[:, 128:])
        put(sent_ref, block[:, :128])


def g_block(pos, units, of_y):
    k, d = of_y.shape
    return pl.pallas_call(
        block_kernel,
        out_shape=(jax.ShapeDtypeStruct((8, 3, 8, 128), F32),) * 2,
        in_specs=[SMEM] + [VMEM] * 4,
        out_specs=(VMEM, VMEM),
        compiler_params=params(16),
        cost_estimate=cost(2 * 6 * 192 * k * d, 2 << 20),
        name="g_block",
    )(pos, *units, of_y)


def inverse_factor(gram):
    n = gram.shape[0]
    tiles = n // 8
    row = lax.broadcasted_iota(jnp.int32, (n, n), 0)
    col = lax.broadcasted_iota(jnp.int32, (n, n), 1)
    diagonal = jnp.where(row == col, gram, 0.0)
    scale = lax.rsqrt(jnp.sum(diagonal, axis=0, keepdims=True))
    gram = gram * lax.rsqrt(jnp.sum(diagonal, axis=1, keepdims=True)) * scale
    both = jnp.concatenate([gram, jnp.where(row == col, 1.0, 0.0)], axis=1)
    b = [both[8 * r:8 * r + 8] for r in range(tiles)]
    sub = lax.broadcasted_iota(jnp.int32, (8, 2 * n), 0)

    def spread_row(x, k):
        return jnp.broadcast_to(x[k:k + 1], (8, 2 * n))

    out = []
    for t in range(tiles):
        c = {
            (r, k): jnp.broadcast_to(b[r][:, 8 * t + k:8 * t + k + 1], (8, 2 * n))
            for r in range(t, tiles)
            for k in range(8)
        }
        pivots = jnp.ones((8, 2 * n), F32)
        for k in range(0, 8, 2):
            here, after = c[t, k], c[t, k + 1]
            p11, p12 = spread_row(here, k), spread_row(after, k)
            p21, p22 = spread_row(here, k + 1), spread_row(after, k + 1)
            det = p11 * p22 - p12 * p21
            turn, turn_one = 1.0 / det, 1.0 / p11
            pivots = jnp.where(sub == k, p11, jnp.where(sub == k + 1, det * turn_one, pivots))
            lead, lead_after = spread_row(b[t], k), spread_row(b[t], k + 1)
            heads = {l: (spread_row(c[t, l], k), spread_row(c[t, l], k + 1)) for l in range(k + 2, 8)}
            for r in range(t, tiles):
                m = (c[r, k] * p22 - c[r, k + 1] * p21) * turn
                m_after = (c[r, k + 1] * p11 - c[r, k] * p12) * turn
                for l in range(k + 2, 8):
                    c[r, l] = c[r, l] - (m * heads[l][0] + m_after * heads[l][1])
                if r == t:
                    m = jnp.where(sub > k + 1, m, jnp.where(sub == k + 1, p21 * turn_one, 0.0))
                    m_after = jnp.where(sub > k + 1, m_after, 0.0)
                b[r] = b[r] - (m * lead + m_after * lead_after)
        out.append(b[t] / jnp.sqrt(pivots))
    return jnp.concatenate(out, axis=0)[:, n:] * scale


def iterate_kernel(pos_ref, own_ref, away_ref, q_ref, q_out, w_out, hi_ref, mid_ref, low_ref):
    s = pl.program_id(0)
    parts = (hi_ref, mid_ref, low_ref)
    for ref, core in ((own_ref, pos_ref[0]), (away_ref, 1 - pos_ref[0])):
        for z in range(4):
            for y in range(4):
                to = pl.ds(pl.multiple_of(y * 256 + core * 128, 128), 128)
                for e in range(3):
                    start = (y - e) % 4 * 256 + z * 64 + s * 16
                    at = pl.ds(pl.multiple_of(start, 16), 16)
                    both = jnp.concatenate([ref[0, z * 4 + y, e], ref[1, z * 4 + y, e]], axis=0)
                    for part, value in zip(parts, split3(both)):
                        part[at, to] = value

    @pl.when(s == pl.num_programs(0) - 1)
    def _():
        for y in range(4):
            here, after = pl.ds(y * 256, 256), pl.ds((y + 1) % 4 * 256, 256)
            for part in parts:
                part[after, here] = part[here, after].T
        n = q_out.shape[0]
        def product(x, y_hi, y_mid, y_low, dims):
            hi, mid, low = x
            by_hi = lax.dot_general(jnp.concatenate([hi, mid, low], axis=0), y_hi, dims, preferred_element_type=F32)
            by_mid = lax.dot_general(jnp.concatenate([hi, mid], axis=0), y_mid, dims, preferred_element_type=F32)
            by_low = lax.dot_general(hi, y_low, dims, preferred_element_type=F32)
            small = by_hi[2 * n:] + by_mid[n:] + by_low
            return by_hi[:n] + (by_hi[n:2 * n] + by_mid[:n] + small)

        def solve(inv, x):
            hi, mid, low = split3(inv)
            left_parts = jnp.concatenate([hi, hi, mid, mid, hi, low], axis=1)
            right_parts = jnp.concatenate([x[0], x[1], x[0], x[1], x[2], x[0]], axis=0)
            return jnp.dot(left_parts, right_parts, preferred_element_type=F32)

        def times_g(x):
            return product(x, hi_ref[...], mid_ref[...], low_ref[...], (((1,), (0,)), ((), ())))

        q_parts = [q_ref[i] for i in range(3)]
        u = times_g(q_parts)
        for turn in range(ITERS):
            u_parts = split3(u)
            gram = product(u_parts, *q_parts, LANES)
            last = turn == ITERS - 1
            v_parts = None if last else split3(times_g(u_parts))
            inv = inverse_factor(gram)
            if last:
                w_out[...] = solve(inv, q_parts)
            q = solve(inv, u_parts) * (1.0 / 32)
            if not last:
                q_parts = split3(q)
                u = solve(inv, v_parts) * (1.0 / 32)
        q_out[...] = q


def iterate(pos, own, away, q_parts):
    _, n, k = q_parts.shape
    part = pl.BlockSpec((2,) + own.shape[1:], lambda s: (s, 0, 0, 0, 0))
    whole = pl.BlockSpec((n, k), lambda s: (0, 0))
    return pl.pallas_call(
        iterate_kernel,
        out_shape=(jax.ShapeDtypeStruct((n, k), F32),) * 2,
        grid=(own.shape[0] // 2,),
        in_specs=[SMEM, part, part, pl.BlockSpec((3, n, k), lambda s: (0, 0, 0))],
        out_specs=(whole, whole),
        scratch_shapes=[pltpu.VMEM((k, k), BF16)] * 3,
        compiler_params=params(20),
        cost_estimate=cost(36 * n * k * k, 4 * k * k),
        name="iterations",
    )(pos, own, away, q_parts)


def left_kernel(pos_ref, w_ref, m0, m1, m3, m2_top, m2_end, out_ref):
    total = None
    n = w_ref.shape[0]
    for turn, start, ref in ((0, 0, m0), (3, 0, m1), (1, 0, m3), (2, 0, m2_top), (2, 128, m2_end)):
        at = pl.multiple_of((pos_ref[1] + turn) % 4 * 256 + start, 128)
        whi, wlow = split2(w_ref[:, pl.ds(at, ref.shape[0])])
        mhi, mlow = split2(ref[...])
        both = jnp.dot(jnp.concatenate([whi, wlow], axis=0), mhi, preferred_element_type=F32)
        part = both[:n] + (both[n:] + jnp.dot(whi, mlow, preferred_element_type=F32))
        total = part if total is None else total + part
    out_ref[...] = total


def left(pos, w, blocks):
    n, d = w.shape[0], blocks[0].shape[1]
    return pl.pallas_call(
        left_kernel,
        out_shape=jax.ShapeDtypeStruct((n, d), F32),
        in_specs=[SMEM] + [VMEM] * 6,
        out_specs=VMEM,
        compiler_params=params(16),
        cost_estimate=cost(6 * n * d * 1024, 2 << 20),
        name="left",
    )(pos, w, *blocks)


def finish_kernel(pos_ref, merged, mom, own, away, q, err_out, mom_out, q_parts):
    i = pl.program_id(0)

    @pl.when(i == 0)
    def _():
        hi, low = split2(q[...])
        q_parts[...] = jnp.concatenate([hi, hi, low, low], axis=0)

    first = i < pl.num_programs(0) // 2
    hi, low = split2(jnp.where(first, own[...], away[...]))
    p_parts = jnp.concatenate([hi, low, hi, low], axis=0)
    for n in range(4):
        cols = pl.ds(256 * n, 256)
        approx = lax.dot_general(p_parts, q_parts[:, cols], ROWS, preferred_element_type=F32)
        err_out[0, :, cols] = (merged[:, cols] - approx).astype(BF16)
        mom_out[:, cols] = (0.9 * mom[:, cols].astype(F32) + approx).astype(BF16)


def finish(pos, merged, momentum, own, away, q):
    n, k = q.shape
    d = momentum.shape[0]
    rows = 256
    half = d // rows // 2

    def row(i, pos):
        return jnp.where(i < half, pos[0], 1 - pos[0]) * half + i % half

    block = pl.BlockSpec((rows, k), lambda i, pos: (row(i, pos), 0))
    return pl.pallas_call(
        finish_kernel,
        out_shape=(jax.ShapeDtypeStruct((1, d, k), BF16), jax.ShapeDtypeStruct(momentum.shape, BF16)),
        grid_spec=pltpu.PrefetchScalarGridSpec(
            num_scalar_prefetch=1,
            grid=(d // rows,),
            in_specs=[
                block,
                block,
                pl.BlockSpec((n, rows), lambda i, pos: (0, jnp.minimum(i, half - 1))),
                pl.BlockSpec((n, rows), lambda i, pos: (0, jnp.maximum(i - half, 0))),
                pl.BlockSpec((n, k), lambda i, pos: (0, 0)),
            ],
            out_specs=(pl.BlockSpec((1, rows, k), lambda i, pos: (0, row(i, pos), 0)), block),
            scratch_shapes=[pltpu.VMEM((4 * n, k), BF16)],
        ),
        compiler_params=params(16),
        cost_estimate=cost(8 * n * d * k, 12 << 20),
        name="finish",
    )(pos, merged, momentum, own, away, q)


TURNS = (2, 1, 3, 0)


def shards(inputs, key_grads, error, momentum, q_start):
    i = lax.axis_index("dp")
    z, y, c = i // 8, (i // 2) % 4, i % 2
    pos = jnp.stack([c, y, z])

    args = (inputs, key_grads, error)
    other, pos = lax.optimization_barrier((merge(pos, TURNS[:1], *args), pos))
    sent_opp = dp_shift(other, dc=1)
    other, sent_opp = lax.optimization_barrier((merge(pos, TURNS[1:], *args), sent_opp))
    sent = dp_shift(other, dc=1)
    opposite = merge(pos, TURNS[:1], *args, sent_opp)
    sums = merge(pos, TURNS[1:], *args, sent)
    came = ring_sum(opposite, sums[0:2], sums[2:4], lambda x, d: dp_shift(x, dy=d))
    *opposite, after, before, own = sum_turn(pos, *sums[4:6], came)
    came = small_ring_sum(opposite, after, before, lambda x, d: dp_shift(x, dz=d))
    copies, unit = spread([own, *came], 4, keep=True)
    units = [unit] + [dp_shift(unit, dy=dy) for dy in (1, 2)]
    of_y = exchange(copies, Z_GROUPS).reshape(256, 512)
    of_y, *units = lax.optimization_barrier((of_y, *units))

    to_core, part = g_block(pos, units, of_y)
    to_core, of_y = lax.optimization_barrier((to_core, of_y))
    part = part + dp_shift(to_core, dc=1)
    m1, m3 = dp_shift(of_y, dy=1), dp_shift(of_y, dy=-1)
    (copies,) = spread([exchange(part, None, "shard")], 16, leading=True)
    copies, m1, m3 = lax.optimization_barrier((copies, m1, m3))
    part = exchange(copies, ZY_GROUPS)
    part, m1, m3, args, q_t = lax.optimization_barrier((part, m1, m3, args, q_start.T))
    m2_top, m2_end = dp_shift(m1[:128], dy=1), dp_shift(m3[128:], dy=-1)
    part = exchange(spread([part], 8)[0], None, "shard")
    part, m2_top, m2_end, merged, q_parts = lax.optimization_barrier(
        (part, m2_top, m2_end, *merge_all(*args, q_t))
    )
    q_t, w = iterate(pos, part, dp_shift(part, dc=1), q_parts)

    blocks = [of_y, m1, m3, m2_top, m2_end]
    own = left(pos, w, blocks)
    away = dp_shift(own, dc=1)
    new_error, new_momentum = finish(pos, merged, momentum, own, away, q_t)
    return (new_error, new_momentum, q_t.T)


def solution(mesh):
    return jax.shard_map(
        shards,
        mesh=mesh,
        in_specs=(P("dp", "shard"), P("dp", None), P("dp", "shard", None), P("shard", None), P()),
        out_specs=(P("dp", "shard", None), P("shard", None), P()),
        check_vma=False,
    )
```

```python
import functools
import math

import jax
import jax.numpy as jnp
from jax import lax
from jax.experimental import pallas as pl
from jax.experimental.pallas import tpu as pltpu
from jax.sharding import PartitionSpec as P

ITERS = 3
HIGH = lax.Precision.HIGHEST
ROWS = (((0,), (0,)), ((), ()))
LANES = (((1,), (1,)), ((), ()))
F32 = jnp.float32
BF16 = jnp.bfloat16
VMEM = pl.BlockSpec(memory_space=pltpu.VMEM)
SMEM = pl.BlockSpec(memory_space=pltpu.SMEM)

Z_GROUPS = [[z * 8 + y * 2 + c for z in range(4)] for y in range(4) for c in range(2)]
ZY_GROUPS = [[z * 8 + y * 2 + c for z in range(4) for y in range(4)] for c in range(2)]


def dp_shift(x, dz=0, dy=0, dc=0):
    pairs = []
    for i in range(32):
        z, y, c = i // 8, (i // 2) % 4, i % 2
        pairs.append((i, (z + dz) % 4 * 8 + (y + dy) % 4 * 2 + (c + dc) % 2))
    return lax.ppermute(x, "dp", pairs)


def ring_sum(opposite, following, before, own, step):
    relay_on, relay_back = step(opposite[0], 1), step(opposite[1], -1)
    second, first = step(following[1], 1), step(before[0], -1)
    on, back = step(following[0] + relay_on, 1), step(before[1] + relay_back, -1)
    return own[0] + first, own[1] + second, on, back


def small_ring_sum(opposite, following, before, step):
    n = opposite[0].shape[0]
    relay_on, relay_back = step(opposite[0], 1), step(opposite[1], -1)
    on = step(following + jnp.pad(relay_on, ((0, n), (0, 0))), 1)
    back = step(before + jnp.pad(relay_back, ((n, 0), (0, 0))), -1)
    return on, back


def exchange(x, groups, axis="dp"):
    return lax.all_to_all(x, axis, 0, 0, axis_index_groups=groups)


def params(mib, **more):
    return pltpu.CompilerParams(vmem_limit_bytes=mib << 20, **more)


def cost(flops, read):
    return pl.CostEstimate(flops=flops, bytes_accessed=read, transcendentals=0)


def split2(x):
    hi = x.astype(BF16)
    return hi, (x - hi.astype(F32)).astype(BF16)


def split3(x):
    hi = x.astype(BF16)
    rest = x - hi.astype(F32)
    mid = rest.astype(BF16)
    return hi, mid, (rest - mid.astype(F32)).astype(BF16)


def merge_kernel(turns, own, pos_ref, acts, grads, err, *refs):
    half = pos_ref[0] if own else 1 - pos_ref[0]
    d = acts.shape[1] // 2
    at_d = pl.ds(pl.multiple_of(half * d, 512), d)
    factor = 1.0 / math.sqrt(acts.shape[0])
    x = acts[:, at_d]
    for n, turn in enumerate(turns):
        cols = pl.ds(pl.multiple_of((pos_ref[1] + turn) % 4 * 256, 256), 256)
        product = lax.dot_general(x, grads[:, cols], ROWS, preferred_element_type=F32)
        merged = product * factor + err[0, at_d, cols].astype(F32)
        if own:
            total = merged + refs[0][n]
            refs[1 + 2 * n][...] = total[:d // 2]
            refs[2 + 2 * n][...] = total[d // 2:]
        else:
            refs[0][n] = merged


def merge(pos, turns, inputs, key_grads, error, sent=None):
    tok, d = inputs.shape
    d = d // 2
    n = len(turns)
    own = sent is not None
    outs = (jax.ShapeDtypeStruct((d // 2, 256), F32),) * (2 * n) if own else jax.ShapeDtypeStruct((n, d, 256), F32)
    return pl.pallas_call(
        functools.partial(merge_kernel, turns, own),
        out_shape=outs,
        in_specs=[SMEM] + [VMEM] * (3 + own),
        out_specs=(VMEM,) * (2 * n) if own else VMEM,
        compiler_params=params(16),
        cost_estimate=cost(2 * tok * d * 256 * n, (1 + 2 * n) << 19),
        name="merge",
    )(pos, inputs, key_grads, error, *([sent] if own else []))


def merge_all_kernel(acts, grads, err, q, out_ref, q_parts):
    factor = 1.0 / math.sqrt(acts.shape[0])
    product = lax.dot_general(acts[...], grads[...], ROWS, preferred_element_type=F32)
    out_ref[...] = product * factor + err[0].astype(F32)

    @pl.when(pl.program_id(0) == 0)
    def _():
        for n, part in enumerate(split3(q[...])):
            q_parts[n] = part


def merge_all(inputs, key_grads, error, q):
    tok, d = inputs.shape
    k = key_grads.shape[1]
    rows = 256
    return pl.pallas_call(
        merge_all_kernel,
        out_shape=(jax.ShapeDtypeStruct((d, k), F32), jax.ShapeDtypeStruct((3,) + q.shape, BF16)),
        grid=(d // rows,),
        in_specs=[
            pl.BlockSpec((tok, rows), lambda i: (0, i)),
            pl.BlockSpec((tok, k), lambda i: (0, 0)),
            pl.BlockSpec((1, rows, k), lambda i: (0, i, 0)),
            pl.BlockSpec(q.shape, lambda i: (0, 0)),
        ],
        out_specs=(
            pl.BlockSpec((rows, k), lambda i: (i, 0)),
            pl.BlockSpec((3,) + q.shape, lambda i: (0, 0, 0)),
        ),
        compiler_params=params(16),
        cost_estimate=cost(2 * tok * d * k, 8 << 20),
        name="merge_all",
    )(inputs, key_grads, error, q)


def sum_turn_kernel(pos_ref, top, end, on, back, opp_top, opp_end, after, before, own, turned):
    turned[:, :256] = (top[...] + on[...]).T
    turned[:, 256:] = (end[...] + back[...]).T
    z = pos_ref[2]

    def rows(turn, start, size):
        return turned[pl.ds(pl.multiple_of((z + turn) % 4 * 64 + start, 32), size), :]

    opp_top[...] = rows(2, 0, 32)
    opp_end[...] = rows(2, 32, 32)
    after[...] = rows(1, 0, 64)
    before[...] = rows(3, 0, 64)
    own[...] = rows(0, 0, 64)


def sum_turn(pos, parts):
    outs = tuple(jax.ShapeDtypeStruct((n, 512), F32) for n in (32, 32, 64, 64, 64))
    return pl.pallas_call(
        sum_turn_kernel,
        out_shape=outs,
        in_specs=[SMEM] + [VMEM] * 4,
        out_specs=(VMEM,) * 5,
        scratch_shapes=[pltpu.VMEM((256, 512), F32)],
        compiler_params=params(12),
        cost_estimate=cost(4 << 17, 3 << 20),
        name="sum_turn",
    )(pos, *parts)


def spread_kernel(leading, keep, *refs):
    refs, outs = refs[:-1 - keep], refs[-1 - keep:]
    terms = [refs[0][i] for i in range(refs[0].shape[0])] if leading else [ref[...] for ref in refs]
    total = terms[0]
    for term in terms[1:]:
        total = total + term
    copies_ref = outs[0]
    for i in range(copies_ref.shape[0]):
        copies_ref[i] = total
    if keep:
        outs[1][...] = total


def spread(parts, copies, leading=False, keep=False):
    shape = parts[0].shape[1:] if leading else parts[0].shape
    outs = (jax.ShapeDtypeStruct((copies,) + shape, F32), jax.ShapeDtypeStruct(shape, F32))[:1 + keep]
    return pl.pallas_call(
        functools.partial(spread_kernel, leading, keep),
        out_shape=outs,
        in_specs=[VMEM] * len(parts),
        out_specs=(VMEM,) * len(outs),
        compiler_params=params(10),
        cost_estimate=cost(1 << 17, 1 << 20),
        name="spread",
    )(*parts)


def block_kernel(pos_ref, u0, u1, u2, of_y, sent_ref, mine_ref):
    core = pos_ref[0]
    rows = jnp.concatenate([u0[...], u1[...], u2[...]], axis=0)
    block = lax.dot_general(rows, of_y[...], LANES, precision=HIGH, preferred_element_type=F32)

    def put(ref, part):
        for e in range(3):
            for s in range(8):
                ref[s, e] = part[64 * e + 8 * s:64 * e + 8 * s + 8]

    @pl.when(core == 0)
    def _():
        put(mine_ref, block[:, :128])
        put(sent_ref, block[:, 128:])

    @pl.when(core == 1)
    def _():
        put(mine_ref, block[:, 128:])
        put(sent_ref, block[:, :128])


def g_block(pos, units, of_y):
    k, d = of_y.shape
    return pl.pallas_call(
        block_kernel,
        out_shape=(jax.ShapeDtypeStruct((8, 3, 8, 128), F32),) * 2,
        in_specs=[SMEM] + [VMEM] * 4,
        out_specs=(VMEM, VMEM),
        compiler_params=params(12),
        cost_estimate=cost(2 * 6 * 192 * k * d, 2 << 20),
        name="g_block",
    )(pos, *units, of_y)


def inverse_factor(gram):
    n = gram.shape[0]
    tiles = n // 8
    row = lax.broadcasted_iota(jnp.int32, (n, n), 0)
    col = lax.broadcasted_iota(jnp.int32, (n, n), 1)
    diagonal = jnp.where(row == col, gram, 0.0)
    scale = lax.rsqrt(jnp.sum(diagonal, axis=0, keepdims=True))
    gram = gram * lax.rsqrt(jnp.sum(diagonal, axis=1, keepdims=True)) * scale
    both = jnp.concatenate([gram, jnp.where(row == col, 1.0, 0.0)], axis=1)
    b = [both[8 * r:8 * r + 8] for r in range(tiles)]
    sub = lax.broadcasted_iota(jnp.int32, (8, 2 * n), 0)

    def spread_row(x, k):
        return jnp.broadcast_to(x[k:k + 1], (8, 2 * n))

    out = []
    for t in range(tiles):
        c = {
            (r, k): jnp.broadcast_to(b[r][:, 8 * t + k:8 * t + k + 1], (8, 2 * n))
            for r in range(t, tiles)
            for k in range(8)
        }
        pivots = jnp.ones((8, 2 * n), F32)
        for k in range(0, 8, 2):
            here, after = c[t, k], c[t, k + 1]
            p11, p12 = spread_row(here, k), spread_row(after, k)
            p21, p22 = spread_row(here, k + 1), spread_row(after, k + 1)
            det = p11 * p22 - p12 * p21
            turn, turn_one = 1.0 / det, 1.0 / p11
            pivots = jnp.where(sub == k, p11, jnp.where(sub == k + 1, det * turn_one, pivots))
            lead, lead_after = spread_row(b[t], k), spread_row(b[t], k + 1)
            heads = {l: (spread_row(c[t, l], k), spread_row(c[t, l], k + 1)) for l in range(k + 2, 8)}
            for r in range(t, tiles):
                m = (c[r, k] * p22 - c[r, k + 1] * p21) * turn
                m_after = (c[r, k + 1] * p11 - c[r, k] * p12) * turn
                for l in range(k + 2, 8):
                    c[r, l] = c[r, l] - (m * heads[l][0] + m_after * heads[l][1])
                if r == t:
                    m = jnp.where(sub > k + 1, m, jnp.where(sub == k + 1, p21 * turn_one, 0.0))
                    m_after = jnp.where(sub > k + 1, m_after, 0.0)
                b[r] = b[r] - (m * lead + m_after * lead_after)
        out.append(b[t] / jnp.sqrt(pivots))
    return jnp.concatenate(out, axis=0)[:, n:] * scale


def iterate_kernel(pos_ref, own_ref, away_ref, q_ref, q_out, w_out, hi_ref, mid_ref, low_ref):
    s = pl.program_id(0)
    parts = (hi_ref, mid_ref, low_ref)
    for ref, core in ((own_ref, pos_ref[0]), (away_ref, 1 - pos_ref[0])):
        for z in range(4):
            ready = []
            for y in range(4):
                for e in range(3):
                    both = jnp.concatenate([ref[0, z * 4 + y, e], ref[1, z * 4 + y, e]], axis=0)
                    ready.append((y, e, split3(both)))
            for y, e, values in ready:
                to = pl.ds(pl.multiple_of(y * 256 + core * 128, 128), 128)
                at = pl.ds(pl.multiple_of((y - e) % 4 * 256 + z * 64 + s * 16, 16), 16)
                for part, value in zip(parts, values):
                    part[at, to] = value

    @pl.when(s == pl.num_programs(0) - 1)
    def _():
        for y in range(4):
            here, after = pl.ds(y * 256, 256), pl.ds((y + 1) % 4 * 256, 256)
            for part in parts:
                part[after, here] = part[here, after].T
        n = q_out.shape[0]
        def product(x, y_hi, y_mid, y_low, dims):
            hi, mid, low = x
            by_hi = lax.dot_general(jnp.concatenate([hi, mid, low], axis=0), y_hi, dims, preferred_element_type=F32)
            by_mid = lax.dot_general(jnp.concatenate([hi, mid], axis=0), y_mid, dims, preferred_element_type=F32)
            by_low = lax.dot_general(hi, y_low, dims, preferred_element_type=F32)
            small = by_hi[2 * n:] + by_mid[n:] + by_low
            return by_hi[:n] + (by_hi[n:2 * n] + by_mid[:n] + small)

        def solve(inv, x):
            hi, mid, low = split3(inv)
            left_parts = jnp.concatenate([hi, hi, mid, mid, hi, low], axis=1)
            right_parts = jnp.concatenate([x[0], x[1], x[0], x[1], x[2], x[0]], axis=0)
            return jnp.dot(left_parts, right_parts, preferred_element_type=F32)

        def times_g(x):
            return product(x, hi_ref[...], mid_ref[...], low_ref[...], (((1,), (0,)), ((), ())))

        q_parts = [q_ref[i] for i in range(3)]
        u = times_g(q_parts)
        for turn in range(ITERS):
            u_parts = split3(u)
            gram = product(u_parts, *q_parts, LANES)
            last = turn == ITERS - 1
            v_parts = None if last else split3(times_g(u_parts))
            inv = inverse_factor(gram)
            if last:
                w_out[...] = solve(inv, q_parts)
            q = solve(inv, u_parts) * (1.0 / 32)
            if not last:
                q_parts = split3(q)
                u = solve(inv, v_parts) * (1.0 / 32)
        q_out[...] = q


def iterate(pos, own, away, q_parts):
    _, n, k = q_parts.shape
    part = pl.BlockSpec((2,) + own.shape[1:], lambda s: (s, 0, 0, 0, 0))
    whole = pl.BlockSpec((n, k), lambda s: (0, 0))
    return pl.pallas_call(
        iterate_kernel,
        out_shape=(jax.ShapeDtypeStruct((n, k), F32),) * 2,
        grid=(own.shape[0] // 2,),
        in_specs=[SMEM, part, part, pl.BlockSpec((3, n, k), lambda s: (0, 0, 0))],
        out_specs=(whole, whole),
        scratch_shapes=[pltpu.VMEM((k, k), BF16)] * 3,
        compiler_params=params(20),
        cost_estimate=cost(36 * n * k * k, 4 * k * k),
        name="iterations",
    )(pos, own, away, q_parts)


def left_kernel(pos_ref, w_ref, m0, m1, m3, m2_top, m2_end, out_ref):
    total = None
    n = w_ref.shape[0]
    for turn, start, ref in ((0, 0, m0), (3, 0, m1), (1, 0, m3), (2, 0, m2_top), (2, 128, m2_end)):
        at = pl.multiple_of((pos_ref[1] + turn) % 4 * 256 + start, 128)
        whi, wlow = split2(w_ref[:, pl.ds(at, ref.shape[0])])
        mhi, mlow = split2(ref[...])
        both = jnp.dot(jnp.concatenate([whi, wlow], axis=0), mhi, preferred_element_type=F32)
        part = both[:n] + (both[n:] + jnp.dot(whi, mlow, preferred_element_type=F32))
        total = part if total is None else total + part
    out_ref[...] = total


def left(pos, w, blocks):
    n, d = w.shape[0], blocks[0].shape[1]
    return pl.pallas_call(
        left_kernel,
        out_shape=jax.ShapeDtypeStruct((n, d), F32),
        in_specs=[SMEM] + [VMEM] * 6,
        out_specs=VMEM,
        compiler_params=params(12),
        cost_estimate=cost(6 * n * d * 1024, 2 << 20),
        name="left",
    )(pos, w, *blocks)


def finish_kernel(pos_ref, merged, mom, own, away, q, err_out, mom_out, q_parts):
    i = pl.program_id(0)

    @pl.when(i == 0)
    def _():
        hi, low = split2(q[...])
        q_parts[...] = jnp.concatenate([hi, hi, low, low], axis=0)

    first = i < pl.num_programs(0) // 2
    hi, low = split2(jnp.where(first, own[...], away[...]))
    p_parts = jnp.concatenate([hi, low, hi, low], axis=0)
    for n in range(4):
        cols = pl.ds(256 * n, 256)
        approx = lax.dot_general(p_parts, q_parts[:, cols], ROWS, preferred_element_type=F32)
        err_out[0, :, cols] = (merged[:, cols] - approx).astype(BF16)
        mom_out[:, cols] = (0.9 * mom[:, cols].astype(F32) + approx).astype(BF16)


def finish(pos, merged, momentum, own, away, q):
    n, k = q.shape
    d = momentum.shape[0]
    rows = 256
    half = d // rows // 2

    def row(i, pos):
        return jnp.where(i < half, pos[0], 1 - pos[0]) * half + i % half

    block = pl.BlockSpec((rows, k), lambda i, pos: (row(i, pos), 0))
    return pl.pallas_call(
        finish_kernel,
        out_shape=(jax.ShapeDtypeStruct((1, d, k), BF16), jax.ShapeDtypeStruct(momentum.shape, BF16)),
        grid_spec=pltpu.PrefetchScalarGridSpec(
            num_scalar_prefetch=1,
            grid=(d // rows,),
            in_specs=[
                block,
                block,
                pl.BlockSpec((n, rows), lambda i, pos: (0, jnp.minimum(i, half - 1))),
                pl.BlockSpec((n, rows), lambda i, pos: (0, jnp.maximum(i - half, 0))),
                pl.BlockSpec((n, k), lambda i, pos: (0, 0)),
            ],
            out_specs=(pl.BlockSpec((1, rows, k), lambda i, pos: (0, row(i, pos), 0)), block),
            scratch_shapes=[pltpu.VMEM((4 * n, k), BF16)],
        ),
        compiler_params=params(16),
        cost_estimate=cost(8 * n * d * k, 12 << 20),
        name="finish",
    )(pos, merged, momentum, own, away, q)


TURNS = (2, 1, 3, 0)


def shards(inputs, key_grads, error, momentum, q_start):
    i = lax.axis_index("dp")
    z, y, c = i // 8, (i // 2) % 4, i % 2
    pos = jnp.stack([c, y, z])

    args = (inputs, key_grads, error)
    other, pos = lax.optimization_barrier((merge(pos, TURNS[:1], *args), pos))
    sent_opp = dp_shift(other, dc=1)
    other, sent_opp = lax.optimization_barrier((merge(pos, TURNS[1:], *args), sent_opp))
    sent = dp_shift(other, dc=1)
    opposite = merge(pos, TURNS[:1], *args, sent_opp)
    sums = merge(pos, TURNS[1:], *args, sent)
    parts = ring_sum(opposite, sums[0:2], sums[2:4], sums[4:6], lambda x, d: dp_shift(x, dy=d))
    *opposite, after, before, own = sum_turn(pos, parts)
    came = small_ring_sum(opposite, after, before, lambda x, d: dp_shift(x, dz=d))
    copies, unit = spread([own, *came], 4, keep=True)
    units = [unit] + [dp_shift(unit, dy=dy) for dy in (1, 2)]
    of_y = exchange(copies, Z_GROUPS).reshape(256, 512)
    of_y, *units = lax.optimization_barrier((of_y, *units))

    to_core, part = g_block(pos, units, of_y)
    to_core, of_y = lax.optimization_barrier((to_core, of_y))
    part = part + dp_shift(to_core, dc=1)
    m1, m3 = dp_shift(of_y, dy=1), dp_shift(of_y, dy=-1)
    (copies,) = spread([exchange(part, None, "shard")], 16, leading=True)
    copies, m1, m3 = lax.optimization_barrier((copies, m1, m3))
    part = exchange(copies, ZY_GROUPS)
    part, m1, m3, args, q_t = lax.optimization_barrier((part, m1, m3, args, q_start.T))
    m2_top, m2_end = dp_shift(m1[:128], dy=1), dp_shift(m3[128:], dy=-1)
    part = exchange(spread([part], 8)[0], None, "shard")
    part, m2_top, m2_end, merged, q_parts = lax.optimization_barrier(
        (part, m2_top, m2_end, *merge_all(*args, q_t))
    )
    q_t, w = iterate(pos, part, dp_shift(part, dc=1), q_parts)

    blocks = [of_y, m1, m3, m2_top, m2_end]
    own = left(pos, w, blocks)
    away = dp_shift(own, dc=1)
    new_error, new_momentum = finish(pos, merged, momentum, own, away, q_t)
    return (new_error, new_momentum, q_t.T)


def solution(mesh):
    return jax.shard_map(
        shards,
        mesh=mesh,
        in_specs=(P("dp", "shard"), P("dp", None), P("dp", "shard", None), P("shard", None), P()),
        out_specs=(P("dp", "shard", None), P("shard", None), P()),
        check_vma=False,
    )
```

```python
import functools
import math

import jax
import jax.numpy as jnp
from jax import lax
from jax.experimental import pallas as pl
from jax.experimental.pallas import tpu as pltpu
from jax.sharding import PartitionSpec as P

ITERS = 3
HIGH = lax.Precision.HIGHEST
ROWS = (((0,), (0,)), ((), ()))
LANES = (((1,), (1,)), ((), ()))
F32 = jnp.float32
BF16 = jnp.bfloat16
VMEM = pl.BlockSpec(memory_space=pltpu.VMEM)
SMEM = pl.BlockSpec(memory_space=pltpu.SMEM)

ZY_GROUPS = [[z * 8 + y * 2 + c for z in range(4) for y in range(4)] for c in range(2)]


def dp_shift(x, dz=0, dy=0, dc=0):
    pairs = []
    for i in range(32):
        z, y, c = i // 8, (i // 2) % 4, i % 2
        pairs.append((i, (z + dz) % 4 * 8 + (y + dy) % 4 * 2 + (c + dc) % 2))
    return lax.ppermute(x, "dp", pairs)


def ring_sum(opposite, following, before, own, step):
    relay_on, relay_back = step(opposite[0], 1), step(opposite[1], -1)
    second, first = step(following[1], 1), step(before[0], -1)
    on, back = step(following[0] + relay_on, 1), step(before[1] + relay_back, -1)
    return own[0] + first, own[1] + second, on, back


def small_ring_sum(opposite, following, before, step):
    n = opposite[0].shape[0]
    relay_on, relay_back = step(opposite[0], 1), step(opposite[1], -1)
    on = step(following + jnp.pad(relay_on, ((0, n), (0, 0))), 1)
    back = step(before + jnp.pad(relay_back, ((n, 0), (0, 0))), -1)
    return on, back


def exchange(x, groups, axis="dp"):
    return lax.all_to_all(x, axis, 0, 0, axis_index_groups=groups)


def params(mib, **more):
    return pltpu.CompilerParams(vmem_limit_bytes=mib << 20, **more)


def cost(flops, read):
    return pl.CostEstimate(flops=flops, bytes_accessed=read, transcendentals=0)


def split2(x):
    hi = x.astype(BF16)
    return hi, (x - hi.astype(F32)).astype(BF16)


def split3(x):
    hi = x.astype(BF16)
    rest = x - hi.astype(F32)
    mid = rest.astype(BF16)
    return hi, mid, (rest - mid.astype(F32)).astype(BF16)


def merge_kernel(turns, own, pos_ref, acts, grads, err, *refs):
    half = pos_ref[0] if own else 1 - pos_ref[0]
    d = acts.shape[1] // 2
    at_d = pl.ds(pl.multiple_of(half * d, 512), d)
    factor = 1.0 / math.sqrt(acts.shape[0])
    x = acts[:, at_d]
    for n, turn in enumerate(turns):
        cols = pl.ds(pl.multiple_of((pos_ref[1] + turn) % 4 * 256, 256), 256)
        product = lax.dot_general(x, grads[:, cols], ROWS, preferred_element_type=F32)
        merged = product * factor + err[0, at_d, cols].astype(F32)
        if own:
            total = merged + refs[0][n]
            refs[1 + 2 * n][...] = total[:d // 2]
            refs[2 + 2 * n][...] = total[d // 2:]
        else:
            refs[0][n] = merged


def merge(pos, turns, inputs, key_grads, error, sent=None):
    tok, d = inputs.shape
    d = d // 2
    n = len(turns)
    own = sent is not None
    outs = (jax.ShapeDtypeStruct((d // 2, 256), F32),) * (2 * n) if own else jax.ShapeDtypeStruct((n, d, 256), F32)
    return pl.pallas_call(
        functools.partial(merge_kernel, turns, own),
        out_shape=outs,
        in_specs=[SMEM] + [VMEM] * (3 + own),
        out_specs=(VMEM,) * (2 * n) if own else VMEM,
        compiler_params=params(16),
        cost_estimate=cost(2 * tok * d * 256 * n, (1 + 2 * n) << 19),
        name="merge",
    )(pos, inputs, key_grads, error, *([sent] if own else []))


def merge_all_kernel(acts, grads, err, q, out_ref, q_parts):
    factor = 1.0 / math.sqrt(acts.shape[0])
    product = lax.dot_general(acts[...], grads[...], ROWS, preferred_element_type=F32)
    out_ref[...] = product * factor + err[0].astype(F32)

    @pl.when(pl.program_id(0) == 0)
    def _():
        for n, part in enumerate(split3(q[...])):
            q_parts[n] = part


def merge_all(inputs, key_grads, error, q):
    tok, d = inputs.shape
    k = key_grads.shape[1]
    rows = 256
    return pl.pallas_call(
        merge_all_kernel,
        out_shape=(jax.ShapeDtypeStruct((d, k), F32), jax.ShapeDtypeStruct((3,) + q.shape, BF16)),
        grid=(d // rows,),
        in_specs=[
            pl.BlockSpec((tok, rows), lambda i: (0, i)),
            pl.BlockSpec((tok, k), lambda i: (0, 0)),
            pl.BlockSpec((1, rows, k), lambda i: (0, i, 0)),
            pl.BlockSpec(q.shape, lambda i: (0, 0)),
        ],
        out_specs=(
            pl.BlockSpec((rows, k), lambda i: (i, 0)),
            pl.BlockSpec((3,) + q.shape, lambda i: (0, 0, 0)),
        ),
        compiler_params=params(16),
        cost_estimate=cost(2 * tok * d * k, 8 << 20),
        name="merge_all",
    )(inputs, key_grads, error, q)


def sum_turn_kernel(pos_ref, top, end, on, back, opp_top, opp_end, after, before, own, turned):
    turned[:, :256] = (top[...] + on[...]).T
    turned[:, 256:] = (end[...] + back[...]).T
    z = pos_ref[2]

    def rows(turn, start, size):
        return turned[pl.ds(pl.multiple_of((z + turn) % 4 * 64 + start, 32), size), :]

    opp_top[...] = rows(2, 0, 32)
    opp_end[...] = rows(2, 32, 32)
    after[...] = rows(1, 0, 64)
    before[...] = rows(3, 0, 64)
    own[...] = rows(0, 0, 64)


def sum_turn(pos, parts):
    outs = tuple(jax.ShapeDtypeStruct((n, 512), F32) for n in (32, 32, 64, 64, 64))
    return pl.pallas_call(
        sum_turn_kernel,
        out_shape=outs,
        in_specs=[SMEM] + [VMEM] * 4,
        out_specs=(VMEM,) * 5,
        scratch_shapes=[pltpu.VMEM((256, 512), F32)],
        compiler_params=params(12),
        cost_estimate=cost(4 << 17, 3 << 20),
        name="sum_turn",
    )(pos, *parts)


def spread_kernel(leading, x_ref, copies_ref):
    total = x_ref[0] if leading else x_ref[...]
    for i in range(1, x_ref.shape[0] if leading else 1):
        total = total + x_ref[i]
    for i in range(copies_ref.shape[0]):
        copies_ref[i] = total


def spread(x, copies, leading=False, grant=10):
    return pl.pallas_call(
        functools.partial(spread_kernel, leading),
        out_shape=jax.ShapeDtypeStruct((copies,) + x.shape[leading:], F32),
        in_specs=[VMEM],
        out_specs=VMEM,
        compiler_params=params(grant),
        cost_estimate=cost(1 << 17, 1 << 20),
        name="spread",
    )(x)


def block_kernel(pos_ref, unit, u1, u2, z1, z3, z2, sent_ref, mine_ref, of_y):
    core, z = pos_ref[0], pos_ref[2]
    for turn, ref in ((0, unit), (3, z1), (1, z3), (2, z2)):
        of_y[pl.ds(pl.multiple_of((z + turn) % 4 * 64, 64), 64), :] = ref[...]
    rows = jnp.concatenate([unit[...], u1[...], u2[...]], axis=0)
    block = lax.dot_general(rows, of_y[...], LANES, precision=HIGH, preferred_element_type=F32)

    def put(ref, part):
        for e in range(3):
            for s in range(8):
                ref[s, e] = part[64 * e + 8 * s:64 * e + 8 * s + 8]

    @pl.when(core == 0)
    def _():
        put(mine_ref, block[:, :128])
        put(sent_ref, block[:, 128:])

    @pl.when(core == 1)
    def _():
        put(mine_ref, block[:, 128:])
        put(sent_ref, block[:, :128])


def g_block(pos, units):
    k, d = units[0].shape
    return pl.pallas_call(
        block_kernel,
        out_shape=(jax.ShapeDtypeStruct((8, 3, 8, 128), F32),) * 2 + (jax.ShapeDtypeStruct((4 * k, d), F32),),
        in_specs=[SMEM] + [VMEM] * 6,
        out_specs=(VMEM,) * 3,
        compiler_params=params(12),
        cost_estimate=cost(2 * 6 * 192 * 4 * k * d, 2 << 20),
        name="g_block",
    )(pos, *units)


def inverse_factor(gram):
    n = gram.shape[0]
    tiles = n // 8
    row = lax.broadcasted_iota(jnp.int32, (n, n), 0)
    col = lax.broadcasted_iota(jnp.int32, (n, n), 1)
    diagonal = jnp.where(row == col, gram, 0.0)
    scale = lax.rsqrt(jnp.sum(diagonal, axis=0, keepdims=True))
    gram = gram * lax.rsqrt(jnp.sum(diagonal, axis=1, keepdims=True)) * scale
    both = jnp.concatenate([gram, jnp.where(row == col, 1.0, 0.0)], axis=1)
    b = [both[8 * r:8 * r + 8] for r in range(tiles)]
    sub = lax.broadcasted_iota(jnp.int32, (8, 2 * n), 0)

    def spread_row(x, k):
        return jnp.broadcast_to(x[k:k + 1], (8, 2 * n))

    out = []
    for t in range(tiles):
        c = {
            (r, k): jnp.broadcast_to(b[r][:, 8 * t + k:8 * t + k + 1], (8, 2 * n))
            for r in range(t, tiles)
            for k in range(8)
        }
        pivots = jnp.ones((8, 2 * n), F32)
        for k in range(0, 8, 2):
            here, after = c[t, k], c[t, k + 1]
            p11, p12 = spread_row(here, k), spread_row(after, k)
            p21, p22 = spread_row(here, k + 1), spread_row(after, k + 1)
            det = p11 * p22 - p12 * p21
            turn, turn_one = 1.0 / det, 1.0 / p11
            pivots = jnp.where(sub == k, p11, jnp.where(sub == k + 1, det * turn_one, pivots))
            lead, lead_after = spread_row(b[t], k), spread_row(b[t], k + 1)
            heads = {l: (spread_row(c[t, l], k), spread_row(c[t, l], k + 1)) for l in range(k + 2, 8)}
            for r in range(t, tiles):
                m = (c[r, k] * p22 - c[r, k + 1] * p21) * turn
                m_after = (c[r, k + 1] * p11 - c[r, k] * p12) * turn
                for l in range(k + 2, 8):
                    c[r, l] = c[r, l] - (m * heads[l][0] + m_after * heads[l][1])
                if r == t:
                    m = jnp.where(sub > k + 1, m, jnp.where(sub == k + 1, p21 * turn_one, 0.0))
                    m_after = jnp.where(sub > k + 1, m_after, 0.0)
                b[r] = b[r] - (m * lead + m_after * lead_after)
        out.append(b[t] / jnp.sqrt(pivots))
    return jnp.concatenate(out, axis=0)[:, n:] * scale


def iterate_kernel(pos_ref, own_ref, away_ref, q_ref, q_out, w_out, hi_ref, mid_ref, low_ref):
    s = pl.program_id(0)
    parts = (hi_ref, mid_ref, low_ref)
    for ref, core in ((own_ref, pos_ref[0]), (away_ref, 1 - pos_ref[0])):
        for z in range(4):
            ready = []
            for y in range(4):
                for e in range(3):
                    both = jnp.concatenate([ref[0, z * 4 + y, e], ref[1, z * 4 + y, e]], axis=0)
                    ready.append((y, e, split3(both)))
            for y, e, values in ready:
                to = pl.ds(pl.multiple_of(y * 256 + core * 128, 128), 128)
                at = pl.ds(pl.multiple_of((y - e) % 4 * 256 + z * 64 + s * 16, 16), 16)
                for part, value in zip(parts, values):
                    part[at, to] = value

    @pl.when(s == pl.num_programs(0) - 1)
    def _():
        for y in range(4):
            here, after = pl.ds(y * 256, 256), pl.ds((y + 1) % 4 * 256, 256)
            for part in parts:
                part[after, here] = part[here, after].T
        n = q_out.shape[0]
        def product(x, y_hi, y_mid, y_low, dims):
            hi, mid, low = x
            by_hi = lax.dot_general(jnp.concatenate([hi, mid, low], axis=0), y_hi, dims, preferred_element_type=F32)
            by_mid = lax.dot_general(jnp.concatenate([hi, mid], axis=0), y_mid, dims, preferred_element_type=F32)
            by_low = lax.dot_general(hi, y_low, dims, preferred_element_type=F32)
            small = by_hi[2 * n:] + by_mid[n:] + by_low
            return by_hi[:n] + (by_hi[n:2 * n] + by_mid[:n] + small)

        def solve(inv, x):
            hi, mid, low = split3(inv)
            left_parts = jnp.concatenate([hi, hi, mid, mid, hi, low], axis=1)
            right_parts = jnp.concatenate([x[0], x[1], x[0], x[1], x[2], x[0]], axis=0)
            return jnp.dot(left_parts, right_parts, preferred_element_type=F32)

        def times_g(x):
            return product(x, hi_ref[...], mid_ref[...], low_ref[...], (((1,), (0,)), ((), ())))

        q_parts = [q_ref[i] for i in range(3)]
        u = times_g(q_parts)
        for turn in range(ITERS):
            u_parts = split3(u)
            gram = product(u_parts, *q_parts, LANES)
            last = turn == ITERS - 1
            v_parts = None if last else split3(times_g(u_parts))
            inv = inverse_factor(gram)
            if last:
                w_out[...] = solve(inv, q_parts)
            q = solve(inv, u_parts) * (1.0 / 32)
            if not last:
                q_parts = split3(q)
                u = solve(inv, v_parts) * (1.0 / 32)
        q_out[...] = q


def iterate(pos, own, away, q_parts):
    _, n, k = q_parts.shape
    part = pl.BlockSpec((2,) + own.shape[1:], lambda s: (s, 0, 0, 0, 0))
    whole = pl.BlockSpec((n, k), lambda s: (0, 0))
    return pl.pallas_call(
        iterate_kernel,
        out_shape=(jax.ShapeDtypeStruct((n, k), F32),) * 2,
        grid=(own.shape[0] // 2,),
        in_specs=[SMEM, part, part, pl.BlockSpec((3, n, k), lambda s: (0, 0, 0))],
        out_specs=(whole, whole),
        scratch_shapes=[pltpu.VMEM((k, k), BF16)] * 3,
        compiler_params=params(20),
        cost_estimate=cost(36 * n * k * k, 4 * k * k),
        name="iterations",
    )(pos, own, away, q_parts)


def left_kernel(pos_ref, w_ref, m0, m1, m3, m2_top, m2_end, out_ref):
    total = None
    n = w_ref.shape[0]
    for turn, start, ref in ((0, 0, m0), (3, 0, m1), (1, 0, m3), (2, 0, m2_top), (2, 128, m2_end)):
        at = pl.multiple_of((pos_ref[1] + turn) % 4 * 256 + start, 128)
        whi, wlow = split2(w_ref[:, pl.ds(at, ref.shape[0])])
        mhi, mlow = split2(ref[...])
        both = jnp.dot(jnp.concatenate([whi, wlow], axis=0), mhi, preferred_element_type=F32)
        part = both[:n] + (both[n:] + jnp.dot(whi, mlow, preferred_element_type=F32))
        total = part if total is None else total + part
    out_ref[...] = total


def left(pos, w, blocks):
    n, d = w.shape[0], blocks[0].shape[1]
    return pl.pallas_call(
        left_kernel,
        out_shape=jax.ShapeDtypeStruct((n, d), F32),
        in_specs=[SMEM] + [VMEM] * 6,
        out_specs=VMEM,
        compiler_params=params(12),
        cost_estimate=cost(6 * n * d * 1024, 2 << 20),
        name="left",
    )(pos, w, *blocks)


def finish_kernel(pos_ref, merged, mom, own, away, q, err_out, mom_out, q_parts):
    i = pl.program_id(0)

    @pl.when(i == 0)
    def _():
        hi, low = split2(q[...])
        q_parts[...] = jnp.concatenate([hi, hi, low, low], axis=0)

    first = i < pl.num_programs(0) // 2
    hi, low = split2(jnp.where(first, own[...], away[...]))
    p_parts = jnp.concatenate([hi, low, hi, low], axis=0)
    for n in range(4):
        cols = pl.ds(256 * n, 256)
        approx = lax.dot_general(p_parts, q_parts[:, cols], ROWS, preferred_element_type=F32)
        err_out[0, :, cols] = (merged[:, cols] - approx).astype(BF16)
        mom_out[:, cols] = (0.9 * mom[:, cols].astype(F32) + approx).astype(BF16)


def finish(pos, merged, momentum, own, away, q):
    n, k = q.shape
    d = momentum.shape[0]
    rows = 256
    half = d // rows // 2

    def row(i, pos):
        return jnp.where(i < half, pos[0], 1 - pos[0]) * half + i % half

    block = pl.BlockSpec((rows, k), lambda i, pos: (row(i, pos), 0))
    return pl.pallas_call(
        finish_kernel,
        out_shape=(jax.ShapeDtypeStruct((1, d, k), BF16), jax.ShapeDtypeStruct(momentum.shape, BF16)),
        grid_spec=pltpu.PrefetchScalarGridSpec(
            num_scalar_prefetch=1,
            grid=(d // rows,),
            in_specs=[
                block,
                block,
                pl.BlockSpec((n, rows), lambda i, pos: (0, jnp.minimum(i, half - 1))),
                pl.BlockSpec((n, rows), lambda i, pos: (0, jnp.maximum(i - half, 0))),
                pl.BlockSpec((n, k), lambda i, pos: (0, 0)),
            ],
            out_specs=(pl.BlockSpec((1, rows, k), lambda i, pos: (0, row(i, pos), 0)), block),
            scratch_shapes=[pltpu.VMEM((4 * n, k), BF16)],
        ),
        compiler_params=params(16),
        cost_estimate=cost(8 * n * d * k, 12 << 20),
        name="finish",
    )(pos, merged, momentum, own, away, q)


TURNS = (2, 1, 3, 0)


def shards(inputs, key_grads, error, momentum, q_start):
    i = lax.axis_index("dp")
    z, y, c = i // 8, (i // 2) % 4, i % 2
    pos = jnp.stack([c, y, z])

    args = (inputs, key_grads, error)
    other, pos = lax.optimization_barrier((merge(pos, TURNS[:1], *args), pos))
    sent_opp = dp_shift(other, dc=1)
    other, sent_opp = lax.optimization_barrier((merge(pos, TURNS[1:], *args), sent_opp))
    sent = dp_shift(other, dc=1)
    opposite = merge(pos, TURNS[:1], *args, sent_opp)
    sums = merge(pos, TURNS[1:], *args, sent)
    parts = ring_sum(opposite, sums[0:2], sums[2:4], sums[4:6], lambda x, d: dp_shift(x, dy=d))
    *opposite, after, before, own = sum_turn(pos, parts)
    came = small_ring_sum(opposite, after, before, lambda x, d: dp_shift(x, dz=d))
    unit = own + (came[0] + came[1])
    z1, z3 = dp_shift(unit, dz=1), dp_shift(unit, dz=-1)
    u1, u2 = dp_shift(unit, dy=1), dp_shift(unit, dy=2)
    units = [unit, u1, u2, z1, z3, dp_shift(z1, dz=1)]

    to_core, part, of_y = g_block(pos, units)
    to_core, of_y = lax.optimization_barrier((to_core, of_y))
    part = part + dp_shift(to_core, dc=1)
    m1, m3 = dp_shift(of_y, dy=1), dp_shift(of_y, dy=-1)
    copies = spread(exchange(part, None, "shard"), 16, leading=True)
    copies, m1, m3 = lax.optimization_barrier((copies, m1, m3))
    part = exchange(copies, ZY_GROUPS)
    part, m1, m3, args, q_t = lax.optimization_barrier((part, m1, m3, args, q_start.T))
    m2_top, m2_end = dp_shift(m1[:128], dy=1), dp_shift(m3[128:], dy=-1)
    part = exchange(spread(part, 8, grant=58), None, "shard")
    part, m2_top, m2_end, merged, q_parts = lax.optimization_barrier(
        (part, m2_top, m2_end, *merge_all(*args, q_t))
    )
    q_t, w = iterate(pos, part, dp_shift(part, dc=1), q_parts)

    blocks = [of_y, m1, m3, m2_top, m2_end]
    own = left(pos, w, blocks)
    away = dp_shift(own, dc=1)
    new_error, new_momentum = finish(pos, merged, momentum, own, away, q_t)
    return (new_error, new_momentum, q_t.T)


def solution(mesh):
    return jax.shard_map(
        shards,
        mesh=mesh,
        in_specs=(P("dp", "shard"), P("dp", None), P("dp", "shard", None), P("shard", None), P()),
        out_specs=(P("dp", "shard", None), P("shard", None), P()),
        check_vma=False,
    )
```

```python
import functools
import math

import jax
import jax.numpy as jnp
from jax import lax
from jax.experimental import pallas as pl
from jax.experimental.pallas import tpu as pltpu
from jax.sharding import PartitionSpec as P

ITERS = 3
HIGH = lax.Precision.HIGHEST
ROWS = (((0,), (0,)), ((), ()))
LANES = (((1,), (1,)), ((), ()))
F32 = jnp.float32
BF16 = jnp.bfloat16
VMEM = pl.BlockSpec(memory_space=pltpu.VMEM)
SMEM = pl.BlockSpec(memory_space=pltpu.SMEM)

ZY_GROUPS = [[z * 8 + y * 2 + c for z in range(4) for y in range(4)] for c in range(2)]


def dp_shift(x, dz=0, dy=0, dc=0):
    pairs = []
    for i in range(32):
        z, y, c = i // 8, (i // 2) % 4, i % 2
        pairs.append((i, (z + dz) % 4 * 8 + (y + dy) % 4 * 2 + (c + dc) % 2))
    return lax.ppermute(x, "dp", pairs)


def ring_sum(opposite, following, before, own, step):
    relay_on, relay_back = step(opposite[0], 1), step(opposite[1], -1)
    second, first = step(following[1], 1), step(before[0], -1)
    on, back = step(following[0] + relay_on, 1), step(before[1] + relay_back, -1)
    return own[0] + first, own[1] + second, on, back


def small_ring_sum(opposite, following, before, step):
    n = opposite[0].shape[0]
    relay_on, relay_back = step(opposite[0], 1), step(opposite[1], -1)
    on = step(following + jnp.pad(relay_on, ((0, n), (0, 0))), 1)
    back = step(before + jnp.pad(relay_back, ((n, 0), (0, 0))), -1)
    return on, back


def exchange(x, groups, axis="dp"):
    return lax.all_to_all(x, axis, 0, 0, axis_index_groups=groups)


def params(mib, **more):
    return pltpu.CompilerParams(vmem_limit_bytes=mib << 20, **more)


def cost(flops, read):
    return pl.CostEstimate(flops=flops, bytes_accessed=read, transcendentals=0)


def split2(x):
    hi = x.astype(BF16)
    return hi, (x - hi.astype(F32)).astype(BF16)


def split3(x):
    hi = x.astype(BF16)
    rest = x - hi.astype(F32)
    mid = rest.astype(BF16)
    return hi, mid, (rest - mid.astype(F32)).astype(BF16)


def merge_kernel(turns, own, pos_ref, acts, grads, err, *refs):
    half = pos_ref[0] if own else 1 - pos_ref[0]
    d = acts.shape[1] // 2
    at_d = pl.ds(pl.multiple_of(half * d, 512), d)
    factor = 1.0 / math.sqrt(acts.shape[0])
    x = acts[:, at_d]
    for n, turn in enumerate(turns):
        cols = pl.ds(pl.multiple_of((pos_ref[1] + turn) % 4 * 256, 256), 256)
        product = lax.dot_general(x, grads[:, cols], ROWS, preferred_element_type=F32)
        merged = product * factor + err[0, at_d, cols].astype(F32)
        if own:
            total = merged + refs[0][n]
            refs[1 + 2 * n][...] = total[:d // 2]
            refs[2 + 2 * n][...] = total[d // 2:]
        else:
            refs[0][n] = merged


def merge(pos, turns, inputs, key_grads, error, sent=None):
    tok, d = inputs.shape
    d = d // 2
    n = len(turns)
    own = sent is not None
    outs = (jax.ShapeDtypeStruct((d // 2, 256), F32),) * (2 * n) if own else jax.ShapeDtypeStruct((n, d, 256), F32)
    return pl.pallas_call(
        functools.partial(merge_kernel, turns, own),
        out_shape=outs,
        in_specs=[SMEM] + [VMEM] * (3 + own),
        out_specs=(VMEM,) * (2 * n) if own else VMEM,
        compiler_params=params(16),
        cost_estimate=cost(2 * tok * d * 256 * n, (1 + 2 * n) << 19),
        name="merge",
    )(pos, inputs, key_grads, error, *([sent] if own else []))


def merge_all_kernel(acts, grads, err, q, out_ref, q_parts):
    factor = 1.0 / math.sqrt(acts.shape[0])
    product = lax.dot_general(acts[...], grads[...], ROWS, preferred_element_type=F32)
    out_ref[...] = product * factor + err[0].astype(F32)

    @pl.when(pl.program_id(0) == 0)
    def _():
        for n, part in enumerate(split3(q[...])):
            q_parts[n] = part


def merge_all(inputs, key_grads, error, q):
    tok, d = inputs.shape
    k = key_grads.shape[1]
    rows = 256
    return pl.pallas_call(
        merge_all_kernel,
        out_shape=(jax.ShapeDtypeStruct((d, k), F32), jax.ShapeDtypeStruct((3,) + q.shape, BF16)),
        grid=(d // rows,),
        in_specs=[
            pl.BlockSpec((tok, rows), lambda i: (0, i)),
            pl.BlockSpec((tok, k), lambda i: (0, 0)),
            pl.BlockSpec((1, rows, k), lambda i: (0, i, 0)),
            pl.BlockSpec(q.shape, lambda i: (0, 0)),
        ],
        out_specs=(
            pl.BlockSpec((rows, k), lambda i: (i, 0)),
            pl.BlockSpec((3,) + q.shape, lambda i: (0, 0, 0)),
        ),
        compiler_params=params(16),
        cost_estimate=cost(2 * tok * d * k, 8 << 20),
        name="merge_all",
    )(inputs, key_grads, error, q)


def sum_turn_kernel(pos_ref, top, end, on, back, opp_top, opp_end, after, before, own, turned):
    turned[:, :256] = (top[...] + on[...]).T
    turned[:, 256:] = (end[...] + back[...]).T
    z = pos_ref[2]

    def rows(turn, start, size):
        return turned[pl.ds(pl.multiple_of((z + turn) % 4 * 64 + start, 32), size), :]

    opp_top[...] = rows(2, 0, 32)
    opp_end[...] = rows(2, 32, 32)
    after[...] = rows(1, 0, 64)
    before[...] = rows(3, 0, 64)
    own[...] = rows(0, 0, 64)


def sum_turn(pos, parts):
    outs = tuple(jax.ShapeDtypeStruct((n, 512), F32) for n in (32, 32, 64, 64, 64))
    return pl.pallas_call(
        sum_turn_kernel,
        out_shape=outs,
        in_specs=[SMEM] + [VMEM] * 4,
        out_specs=(VMEM,) * 5,
        scratch_shapes=[pltpu.VMEM((256, 512), F32)],
        compiler_params=params(12),
        cost_estimate=cost(4 << 17, 3 << 20),
        name="sum_turn",
    )(pos, *parts)


def spread_kernel(leading, x_ref, copies_ref):
    total = x_ref[0] if leading else x_ref[...]
    for i in range(1, x_ref.shape[0] if leading else 1):
        total = total + x_ref[i]
    for i in range(copies_ref.shape[0]):
        copies_ref[i] = total


def spread(x, copies, leading=False, grant=10):
    return pl.pallas_call(
        functools.partial(spread_kernel, leading),
        out_shape=jax.ShapeDtypeStruct((copies,) + x.shape[leading:], F32),
        in_specs=[VMEM],
        out_specs=VMEM,
        compiler_params=params(grant),
        cost_estimate=cost(1 << 17, 1 << 20),
        name="spread",
    )(x)


def block_kernel(pos_ref, unit, u1, u2, z1, z3, z2, sent_ref, mine_ref, of_y):
    core, z = pos_ref[0], pos_ref[2]
    for turn, ref in ((0, unit), (3, z1), (1, z3), (2, z2)):
        of_y[pl.ds(pl.multiple_of((z + turn) % 4 * 64, 64), 64), :] = ref[...]
    rows = jnp.concatenate([unit[...], u1[...], u2[...]], axis=0)
    block = lax.dot_general(rows, of_y[...], LANES, precision=HIGH, preferred_element_type=F32)

    def put(ref, part):
        for e in range(3):
            for s in range(8):
                ref[s, e] = part[64 * e + 8 * s:64 * e + 8 * s + 8]

    @pl.when(core == 0)
    def _():
        put(mine_ref, block[:, :128])
        put(sent_ref, block[:, 128:])

    @pl.when(core == 1)
    def _():
        put(mine_ref, block[:, 128:])
        put(sent_ref, block[:, :128])


def g_block(pos, units):
    k, d = units[0].shape
    return pl.pallas_call(
        block_kernel,
        out_shape=(jax.ShapeDtypeStruct((8, 3, 8, 128), F32),) * 2 + (jax.ShapeDtypeStruct((4 * k, d), F32),),
        in_specs=[SMEM] + [VMEM] * 6,
        out_specs=(VMEM,) * 3,
        compiler_params=params(12),
        cost_estimate=cost(2 * 6 * 192 * 4 * k * d, 2 << 20),
        name="g_block",
    )(pos, *units)


def inverse_factor(gram):
    n = gram.shape[0]
    tiles = n // 8
    row = lax.broadcasted_iota(jnp.int32, (n, n), 0)
    col = lax.broadcasted_iota(jnp.int32, (n, n), 1)
    diagonal = jnp.where(row == col, gram, 0.0)
    scale = lax.rsqrt(jnp.sum(diagonal, axis=0, keepdims=True))
    gram = gram * lax.rsqrt(jnp.sum(diagonal, axis=1, keepdims=True)) * scale
    both = jnp.concatenate([gram, jnp.where(row == col, 1.0, 0.0)], axis=1)
    b = [both[8 * r:8 * r + 8] for r in range(tiles)]
    sub = lax.broadcasted_iota(jnp.int32, (8, 2 * n), 0)

    def spread_row(x, k):
        return jnp.broadcast_to(x[k:k + 1], (8, 2 * n))

    out = []
    for t in range(tiles):
        c = {
            (r, k): jnp.broadcast_to(b[r][:, 8 * t + k:8 * t + k + 1], (8, 2 * n))
            for r in range(t, tiles)
            for k in range(8)
        }
        pivots = jnp.ones((8, 2 * n), F32)
        for k in range(0, 8, 2):
            here, after = c[t, k], c[t, k + 1]
            p11, p12 = spread_row(here, k), spread_row(after, k)
            p21, p22 = spread_row(here, k + 1), spread_row(after, k + 1)
            det = p11 * p22 - p12 * p21
            turn, turn_one = 1.0 / det, 1.0 / p11
            pivots = jnp.where(sub == k, p11, jnp.where(sub == k + 1, det * turn_one, pivots))
            lead, lead_after = spread_row(b[t], k), spread_row(b[t], k + 1)
            heads = {l: (spread_row(c[t, l], k), spread_row(c[t, l], k + 1)) for l in range(k + 2, 8)}
            for r in range(t, tiles):
                m = (c[r, k] * p22 - c[r, k + 1] * p21) * turn
                m_after = (c[r, k + 1] * p11 - c[r, k] * p12) * turn
                for l in range(k + 2, 8):
                    c[r, l] = c[r, l] - (m * heads[l][0] + m_after * heads[l][1])
                if r == t:
                    m = jnp.where(sub > k + 1, m, jnp.where(sub == k + 1, p21 * turn_one, 0.0))
                    m_after = jnp.where(sub > k + 1, m_after, 0.0)
                b[r] = b[r] - (m * lead + m_after * lead_after)
        out.append(b[t] / jnp.sqrt(pivots))
    return jnp.concatenate(out, axis=0)[:, n:] * scale


BLOCKS = ((0, 0, 256), (3, 0, 256), (1, 0, 256), (2, 0, 128), (2, 128, 128))


def iterate_kernel(pos_ref, own_ref, away_ref, q_hbm, m0, m1, m3, m2_top, m2_end,
                   q_out, p_out, hi_ref, mid_ref, low_ref, q_ref, m_ref, sems):
    s = pl.program_id(0)
    copies = [pltpu.make_async_copy(q_hbm, q_ref, sems.at[0])]
    for n, ((turn, start, size), ref) in enumerate(zip(BLOCKS, (m0, m1, m3, m2_top, m2_end))):
        at = pl.ds(pl.multiple_of((pos_ref[1] + turn) % 4 * 256 + start, 128), size)
        copies.append(pltpu.make_async_copy(ref, m_ref.at[at, :], sems.at[1 + n]))

    @pl.when(s == 0)
    def _():
        for copy in copies:
            copy.start()

    parts = (hi_ref, mid_ref, low_ref)
    for ref, core in ((own_ref, pos_ref[0]), (away_ref, 1 - pos_ref[0])):
        for z in range(4):
            ready = []
            for y in range(4):
                for e in range(3):
                    both = jnp.concatenate([ref[0, z * 4 + y, e], ref[1, z * 4 + y, e]], axis=0)
                    ready.append((y, e, split3(both)))
            for y, e, values in ready:
                to = pl.ds(pl.multiple_of(y * 256 + core * 128, 128), 128)
                at = pl.ds(pl.multiple_of((y - e) % 4 * 256 + z * 64 + s * 16, 16), 16)
                for part, value in zip(parts, values):
                    part[at, to] = value

    @pl.when(s == pl.num_programs(0) - 1)
    def _():
        for y in range(4):
            here, after = pl.ds(y * 256, 256), pl.ds((y + 1) % 4 * 256, 256)
            for part in parts:
                part[after, here] = part[here, after].T
        copies[0].wait()
        n = q_out.shape[0]
        def product(x, y_hi, y_mid, y_low, dims):
            hi, mid, low = x
            by_hi = lax.dot_general(jnp.concatenate([hi, mid, low], axis=0), y_hi, dims, preferred_element_type=F32)
            by_mid = lax.dot_general(jnp.concatenate([hi, mid], axis=0), y_mid, dims, preferred_element_type=F32)
            by_low = lax.dot_general(hi, y_low, dims, preferred_element_type=F32)
            small = by_hi[2 * n:] + by_mid[n:] + by_low
            return by_hi[:n] + (by_hi[n:2 * n] + by_mid[:n] + small)

        def solve(inv, x):
            hi, mid, low = split3(inv)
            left_parts = jnp.concatenate([hi, hi, mid, mid, hi, low], axis=1)
            right_parts = jnp.concatenate([x[0], x[1], x[0], x[1], x[2], x[0]], axis=0)
            return jnp.dot(left_parts, right_parts, preferred_element_type=F32)

        def times_g(x):
            return product(x, hi_ref[...], mid_ref[...], low_ref[...], (((1,), (0,)), ((), ())))

        q_parts = [q_ref[i] for i in range(3)]
        u = times_g(q_parts)
        for turn in range(ITERS):
            u_parts = split3(u)
            gram = product(u_parts, *q_parts, LANES)
            last = turn == ITERS - 1
            v_parts = None if last else split3(times_g(u_parts))
            inv = inverse_factor(gram)
            if last:
                w = solve(inv, q_parts)
            q = solve(inv, u_parts) * (1.0 / 32)
            if not last:
                q_parts = split3(q)
                u = solve(inv, v_parts) * (1.0 / 32)
        q_out[...] = q
        w_hi, w_low = split2(w)
        for copy in copies[1:]:
            copy.wait()
        m_hi, m_low = split2(m_ref[...])
        both = jnp.dot(jnp.concatenate([w_hi, w_low], axis=0), m_hi, preferred_element_type=F32)
        p_out[...] = both[:n] + (both[n:] + jnp.dot(w_hi, m_low, preferred_element_type=F32))


def iterate(pos, own, away, q_parts, blocks):
    _, n, k = q_parts.shape
    d = blocks[0].shape[1]
    part = pl.BlockSpec((2,) + own.shape[1:], lambda s: (s, 0, 0, 0, 0))
    anywhere = pl.BlockSpec(memory_space=pl.ANY)
    return pl.pallas_call(
        iterate_kernel,
        out_shape=(jax.ShapeDtypeStruct((n, k), F32), jax.ShapeDtypeStruct((n, d), F32)),
        grid=(own.shape[0] // 2,),
        in_specs=[SMEM, part, part] + [anywhere] * 6,
        out_specs=(pl.BlockSpec((n, k), lambda s: (0, 0)), pl.BlockSpec((n, d), lambda s: (0, 0))),
        scratch_shapes=[pltpu.VMEM((k, k), BF16)] * 3 + [
            pltpu.VMEM((3, n, k), BF16),
            pltpu.VMEM((k, d), F32),
            pltpu.SemaphoreType.DMA((6,)),
        ],
        compiler_params=params(26),
        cost_estimate=cost(36 * n * k * k, 4 * k * k),
        name="iterations",
    )(pos, own, away, q_parts, *blocks)


def finish_kernel(pos_ref, merged, mom, own, away, q, err_out, mom_out, q_parts):
    i = pl.program_id(0)

    @pl.when(i == 0)
    def _():
        hi, low = split2(q[...])
        q_parts[...] = jnp.concatenate([hi, hi, low, low], axis=0)

    first = i < pl.num_programs(0) // 2
    hi, low = split2(jnp.where(first, own[...], away[...]))
    p_parts = jnp.concatenate([hi, low, hi, low], axis=0)
    for n in range(4):
        cols = pl.ds(256 * n, 256)
        approx = lax.dot_general(p_parts, q_parts[:, cols], ROWS, preferred_element_type=F32)
        err_out[0, :, cols] = (merged[:, cols] - approx).astype(BF16)
        mom_out[:, cols] = (0.9 * mom[:, cols].astype(F32) + approx).astype(BF16)


def finish(pos, merged, momentum, own, away, q):
    n, k = q.shape
    d = momentum.shape[0]
    rows = 256
    half = d // rows // 2

    def row(i, pos):
        return jnp.where(i < half, pos[0], 1 - pos[0]) * half + i % half

    block = pl.BlockSpec((rows, k), lambda i, pos: (row(i, pos), 0))
    return pl.pallas_call(
        finish_kernel,
        out_shape=(jax.ShapeDtypeStruct((1, d, k), BF16), jax.ShapeDtypeStruct(momentum.shape, BF16)),
        grid_spec=pltpu.PrefetchScalarGridSpec(
            num_scalar_prefetch=1,
            grid=(d // rows,),
            in_specs=[
                block,
                block,
                pl.BlockSpec((n, rows), lambda i, pos: (0, jnp.minimum(i, half - 1))),
                pl.BlockSpec((n, rows), lambda i, pos: (0, jnp.maximum(i - half, 0))),
                pl.BlockSpec((n, k), lambda i, pos: (0, 0)),
            ],
            out_specs=(pl.BlockSpec((1, rows, k), lambda i, pos: (0, row(i, pos), 0)), block),
            scratch_shapes=[pltpu.VMEM((4 * n, k), BF16)],
        ),
        compiler_params=params(16),
        cost_estimate=cost(8 * n * d * k, 12 << 20),
        name="finish",
    )(pos, merged, momentum, own, away, q)


TURNS = (2, 1, 3, 0)


def shards(inputs, key_grads, error, momentum, q_start):
    i = lax.axis_index("dp")
    z, y, c = i // 8, (i // 2) % 4, i % 2
    pos = jnp.stack([c, y, z])

    args = (inputs, key_grads, error)
    other, pos = lax.optimization_barrier((merge(pos, TURNS[:1], *args), pos))
    sent_opp = dp_shift(other, dc=1)
    other, sent_opp = lax.optimization_barrier((merge(pos, TURNS[1:], *args), sent_opp))
    sent = dp_shift(other, dc=1)
    opposite = merge(pos, TURNS[:1], *args, sent_opp)
    sums = merge(pos, TURNS[1:], *args, sent)
    parts = ring_sum(opposite, sums[0:2], sums[2:4], sums[4:6], lambda x, d: dp_shift(x, dy=d))
    *opposite, after, before, own = sum_turn(pos, parts)
    came = small_ring_sum(opposite, after, before, lambda x, d: dp_shift(x, dz=d))
    unit = own + (came[0] + came[1])
    z1, z3 = dp_shift(unit, dz=1), dp_shift(unit, dz=-1)
    u1, u2 = dp_shift(unit, dy=1), dp_shift(unit, dy=2)
    units = [unit, u1, u2, z1, z3, dp_shift(z1, dz=1)]

    to_core, part, of_y = g_block(pos, units)
    to_core, of_y = lax.optimization_barrier((to_core, of_y))
    part = part + dp_shift(to_core, dc=1)
    m1, m3 = dp_shift(of_y, dy=1), dp_shift(of_y, dy=-1)
    copies = spread(exchange(part, None, "shard"), 16, leading=True)
    part = exchange(copies, ZY_GROUPS)
    part, m1, m3, args, q_t = lax.optimization_barrier((part, m1, m3, args, q_start.T))
    m2_top, m2_end = dp_shift(m1[:128], dy=1), dp_shift(m3[128:], dy=-1)
    part = exchange(spread(part, 8, grant=58), None, "shard")
    part, m2_top, m2_end, merged, q_parts = lax.optimization_barrier(
        (part, m2_top, m2_end, *merge_all(*args, q_t))
    )
    blocks = [of_y, m1, m3, m2_top, m2_end]
    q_t, own = iterate(pos, part, dp_shift(part, dc=1), q_parts, blocks)

    away = dp_shift(own, dc=1)
    new_error, new_momentum = finish(pos, merged, momentum, own, away, q_t)
    return (new_error, new_momentum, q_t.T)


def solution(mesh):
    return jax.shard_map(
        shards,
        mesh=mesh,
        in_specs=(P("dp", "shard"), P("dp", None), P("dp", "shard", None), P("shard", None), P()),
        out_specs=(P("dp", "shard", None), P("shard", None), P()),
        check_vma=False,
    )
```

```python
import functools
import math

import jax
import jax.numpy as jnp
from jax import lax
from jax.experimental import pallas as pl
from jax.experimental.pallas import tpu as pltpu
from jax.sharding import PartitionSpec as P

ITERS = 3
HIGH = lax.Precision.HIGHEST
ROWS = (((0,), (0,)), ((), ()))
LANES = (((1,), (1,)), ((), ()))
F32 = jnp.float32
BF16 = jnp.bfloat16
VMEM = pl.BlockSpec(memory_space=pltpu.VMEM)
SMEM = pl.BlockSpec(memory_space=pltpu.SMEM)


def dp_shift(x, dz=0, dy=0, dc=0):
    pairs = []
    for i in range(32):
        z, y, c = i // 8, (i // 2) % 4, i % 2
        pairs.append((i, (z + dz) % 4 * 8 + (y + dy) % 4 * 2 + (c + dc) % 2))
    return lax.ppermute(x, "dp", pairs)


def ring_sum(opposite, following, before, own, step):
    relay_on, relay_back = step(opposite[0], 1), step(opposite[1], -1)
    second, first = step(following[1], 1), step(before[0], -1)
    on, back = step(following[0] + relay_on, 1), step(before[1] + relay_back, -1)
    return own[0] + first, own[1] + second, on, back


def small_ring_sum(opposite, following, before, step):
    n = opposite[0].shape[0]
    relay_on, relay_back = step(opposite[0], 1), step(opposite[1], -1)
    on = step(following + jnp.pad(relay_on, ((0, n), (0, 0))), 1)
    back = step(before + jnp.pad(relay_back, ((n, 0), (0, 0))), -1)
    return on, back


def exchange(x, axis):
    return lax.all_to_all(x, axis, 0, 0)


def params(mib, **more):
    return pltpu.CompilerParams(vmem_limit_bytes=mib << 20, **more)


def cost(flops, read):
    return pl.CostEstimate(flops=flops, bytes_accessed=read, transcendentals=0)


def split2(x):
    hi = x.astype(BF16)
    return hi, (x - hi.astype(F32)).astype(BF16)


def split3(x):
    hi = x.astype(BF16)
    rest = x - hi.astype(F32)
    mid = rest.astype(BF16)
    return hi, mid, (rest - mid.astype(F32)).astype(BF16)


def merge_kernel(turns, own, pos_ref, acts, grads, err, *refs):
    half = pos_ref[0] if own else 1 - pos_ref[0]
    d = acts.shape[1] // 2
    at_d = pl.ds(pl.multiple_of(half * d, 512), d)
    factor = 1.0 / math.sqrt(acts.shape[0])
    x = acts[:, at_d]
    for n, turn in enumerate(turns):
        cols = pl.ds(pl.multiple_of((pos_ref[1] + turn) % 4 * 256, 256), 256)
        product = lax.dot_general(x, grads[:, cols], ROWS, preferred_element_type=F32)
        merged = product * factor + err[0, at_d, cols].astype(F32)
        if own:
            total = merged + refs[0][n]
            refs[1 + 2 * n][...] = total[:d // 2]
            refs[2 + 2 * n][...] = total[d // 2:]
        else:
            refs[0][n] = merged


def merge(pos, turns, inputs, key_grads, error, sent=None):
    tok, d = inputs.shape
    d = d // 2
    n = len(turns)
    own = sent is not None
    outs = (jax.ShapeDtypeStruct((d // 2, 256), F32),) * (2 * n) if own else jax.ShapeDtypeStruct((n, d, 256), F32)
    return pl.pallas_call(
        functools.partial(merge_kernel, turns, own),
        out_shape=outs,
        in_specs=[SMEM] + [VMEM] * (3 + own),
        out_specs=(VMEM,) * (2 * n) if own else VMEM,
        compiler_params=params(16),
        cost_estimate=cost(2 * tok * d * 256 * n, (1 + 2 * n) << 19),
        name="merge",
    )(pos, inputs, key_grads, error, *([sent] if own else []))


def merge_all_kernel(acts, grads, err, q, out_ref, q_parts):
    factor = 1.0 / math.sqrt(acts.shape[0])
    product = lax.dot_general(acts[...], grads[...], ROWS, preferred_element_type=F32)
    out_ref[...] = product * factor + err[0].astype(F32)

    @pl.when(pl.program_id(0) == 0)
    def _():
        for n, part in enumerate(split3(q[...])):
            q_parts[n] = part


def merge_all(inputs, key_grads, error, q):
    tok, d = inputs.shape
    k = key_grads.shape[1]
    rows = 256
    return pl.pallas_call(
        merge_all_kernel,
        out_shape=(jax.ShapeDtypeStruct((d, k), F32), jax.ShapeDtypeStruct((3,) + q.shape, BF16)),
        grid=(d // rows,),
        in_specs=[
            pl.BlockSpec((tok, rows), lambda i: (0, i)),
            pl.BlockSpec((tok, k), lambda i: (0, 0)),
            pl.BlockSpec((1, rows, k), lambda i: (0, i, 0)),
            pl.BlockSpec(q.shape, lambda i: (0, 0)),
        ],
        out_specs=(
            pl.BlockSpec((rows, k), lambda i: (i, 0)),
            pl.BlockSpec((3,) + q.shape, lambda i: (0, 0, 0)),
        ),
        compiler_params=params(16),
        cost_estimate=cost(2 * tok * d * k, 8 << 20),
        name="merge_all",
    )(inputs, key_grads, error, q)


def sum_turn_kernel(pos_ref, top, end, on, back, opp_top, opp_end, after, before, own, turned):
    turned[:, :256] = (top[...] + on[...]).T
    turned[:, 256:] = (end[...] + back[...]).T
    z = pos_ref[2]

    def rows(turn, start, size):
        return turned[pl.ds(pl.multiple_of((z + turn) % 4 * 64 + start, 32), size), :]

    opp_top[...] = rows(2, 0, 32)
    opp_end[...] = rows(2, 32, 32)
    after[...] = rows(1, 0, 64)
    before[...] = rows(3, 0, 64)
    own[...] = rows(0, 0, 64)


def sum_turn(pos, parts):
    outs = tuple(jax.ShapeDtypeStruct((n, 512), F32) for n in (32, 32, 64, 64, 64))
    return pl.pallas_call(
        sum_turn_kernel,
        out_shape=outs,
        in_specs=[SMEM] + [VMEM] * 4,
        out_specs=(VMEM,) * 5,
        scratch_shapes=[pltpu.VMEM((256, 512), F32)],
        compiler_params=params(12),
        cost_estimate=cost(4 << 17, 3 << 20),
        name="sum_turn",
    )(pos, *parts)


RING = (0, 3, 1, 2)


def order_kernel(pos_ref, *refs):
    for turn, ref in zip(RING, refs):
        refs[-1][(pos_ref[2] + turn) % 4] = ref[...]


def order(pos, pieces):
    return pl.pallas_call(
        order_kernel,
        out_shape=jax.ShapeDtypeStruct((4,) + pieces[0].shape, F32),
        in_specs=[SMEM] + [VMEM] * 4,
        out_specs=VMEM,
        compiler_params=params(10),
        cost_estimate=cost(1 << 14, 1 << 17),
        name="order",
    )(pos, *pieces)


def spread_kernel(pos_ref, a, b, c, d, out, whole, sems):
    for turn, ref in zip(RING, (a, b, c, d)):
        for z in range(4):
            whole[z, (pos_ref[1] + turn) % 4] = ref[z]
    copies = [pltpu.make_async_copy(whole, out.at[i], sems.at[i]) for i in range(8)]
    for copy in copies:
        copy.start()
    for copy in copies:
        copy.wait()


def spread(pos, pieces):
    shape = (4,) + pieces[0].shape
    return pl.pallas_call(
        spread_kernel,
        out_shape=jax.ShapeDtypeStruct((8,) + shape, F32),
        in_specs=[SMEM] + [VMEM] * 4,
        out_specs=pl.BlockSpec(memory_space=pl.ANY),
        scratch_shapes=[pltpu.VMEM(shape, F32), pltpu.SemaphoreType.DMA((8,))],
        compiler_params=params(10),
        cost_estimate=cost(1 << 17, 2 << 20),
        name="spread",
    )(pos, *pieces)


def block_kernel(pos_ref, unit, u1, u2, z1, z3, z2, sent_ref, mine_ref, of_y):
    core, z = pos_ref[0], pos_ref[2]
    for turn, ref in ((0, unit), (3, z1), (1, z3), (2, z2)):
        of_y[pl.ds(pl.multiple_of((z + turn) % 4 * 64, 64), 64), :] = ref[...]
    rows = jnp.concatenate([unit[...], u1[...], u2[...]], axis=0)
    block = lax.dot_general(rows, of_y[...], LANES, precision=HIGH, preferred_element_type=F32)

    def put(ref, part):
        for e in range(3):
            for s in range(8):
                ref[s, e] = part[64 * e + 8 * s:64 * e + 8 * s + 8]

    @pl.when(core == 0)
    def _():
        put(mine_ref, block[:, :128])
        put(sent_ref, block[:, 128:])

    @pl.when(core == 1)
    def _():
        put(mine_ref, block[:, 128:])
        put(sent_ref, block[:, :128])


def g_block(pos, units):
    k, d = units[0].shape
    return pl.pallas_call(
        block_kernel,
        out_shape=(jax.ShapeDtypeStruct((8, 3, 8, 128), F32),) * 2 + (jax.ShapeDtypeStruct((4 * k, d), F32),),
        in_specs=[SMEM] + [VMEM] * 6,
        out_specs=(VMEM,) * 3,
        compiler_params=params(12),
        cost_estimate=cost(2 * 6 * 192 * 4 * k * d, 2 << 20),
        name="g_block",
    )(pos, *units)


def inverse_factor(gram):
    n = gram.shape[0]
    tiles = n // 8
    row = lax.broadcasted_iota(jnp.int32, (n, n), 0)
    col = lax.broadcasted_iota(jnp.int32, (n, n), 1)
    diagonal = jnp.where(row == col, gram, 0.0)
    scale = lax.rsqrt(jnp.sum(diagonal, axis=0, keepdims=True))
    gram = gram * lax.rsqrt(jnp.sum(diagonal, axis=1, keepdims=True)) * scale
    both = jnp.concatenate([gram, jnp.where(row == col, 1.0, 0.0)], axis=1)
    b = [both[8 * r:8 * r + 8] for r in range(tiles)]
    sub = lax.broadcasted_iota(jnp.int32, (8, 2 * n), 0)

    def spread_row(x, k):
        return jnp.broadcast_to(x[k:k + 1], (8, 2 * n))

    out = []
    for t in range(tiles):
        c = {
            (r, k): jnp.broadcast_to(b[r][:, 8 * t + k:8 * t + k + 1], (8, 2 * n))
            for r in range(t, tiles)
            for k in range(8)
        }
        pivots = jnp.ones((8, 2 * n), F32)
        for k in range(0, 8, 2):
            here, after = c[t, k], c[t, k + 1]
            p11, p12 = spread_row(here, k), spread_row(after, k)
            p21, p22 = spread_row(here, k + 1), spread_row(after, k + 1)
            det = p11 * p22 - p12 * p21
            turn, turn_one = 1.0 / det, 1.0 / p11
            pivots = jnp.where(sub == k, p11, jnp.where(sub == k + 1, det * turn_one, pivots))
            lead, lead_after = spread_row(b[t], k), spread_row(b[t], k + 1)
            heads = {l: (spread_row(c[t, l], k), spread_row(c[t, l], k + 1)) for l in range(k + 2, 8)}
            for r in range(t, tiles):
                m = (c[r, k] * p22 - c[r, k + 1] * p21) * turn
                m_after = (c[r, k + 1] * p11 - c[r, k] * p12) * turn
                for l in range(k + 2, 8):
                    c[r, l] = c[r, l] - (m * heads[l][0] + m_after * heads[l][1])
                if r == t:
                    m = jnp.where(sub > k + 1, m, jnp.where(sub == k + 1, p21 * turn_one, 0.0))
                    m_after = jnp.where(sub > k + 1, m_after, 0.0)
                b[r] = b[r] - (m * lead + m_after * lead_after)
        out.append(b[t] / jnp.sqrt(pivots))
    return jnp.concatenate(out, axis=0)[:, n:] * scale


def iterate_kernel(pos_ref, own_ref, away_ref, q_ref, q_out, w_out, hi_ref, mid_ref, low_ref):
    s = pl.program_id(0)
    parts = (hi_ref, mid_ref, low_ref)
    for ref, core in ((own_ref, pos_ref[0]), (away_ref, 1 - pos_ref[0])):
        for z in range(4):
            ready = []
            for y in range(4):
                for e in range(3):
                    both = jnp.concatenate([ref[0, z * 4 + y, e], ref[1, z * 4 + y, e]], axis=0)
                    ready.append((y, e, split3(both)))
            for y, e, values in ready:
                to = pl.ds(pl.multiple_of(y * 256 + core * 128, 128), 128)
                at = pl.ds(pl.multiple_of((y - e) % 4 * 256 + z * 64 + s * 16, 16), 16)
                for part, value in zip(parts, values):
                    part[at, to] = value

    @pl.when(s == pl.num_programs(0) - 1)
    def _():
        for y in range(4):
            here, after = pl.ds(y * 256, 256), pl.ds((y + 1) % 4 * 256, 256)
            for part in parts:
                part[after, here] = part[here, after].T
        n = q_out.shape[0]
        def product(x, y_hi, y_mid, y_low, dims):
            hi, mid, low = x
            by_hi = lax.dot_general(jnp.concatenate([hi, mid, low], axis=0), y_hi, dims, preferred_element_type=F32)
            by_mid = lax.dot_general(jnp.concatenate([hi, mid], axis=0), y_mid, dims, preferred_element_type=F32)
            by_low = lax.dot_general(hi, y_low, dims, preferred_element_type=F32)
            small = by_hi[2 * n:] + by_mid[n:] + by_low
            return by_hi[:n] + (by_hi[n:2 * n] + by_mid[:n] + small)

        def solve(inv, x):
            hi, mid, low = split3(inv)
            left_parts = jnp.concatenate([hi, hi, mid, mid, hi, low], axis=1)
            right_parts = jnp.concatenate([x[0], x[1], x[0], x[1], x[2], x[0]], axis=0)
            return jnp.dot(left_parts, right_parts, preferred_element_type=F32)

        def times_g(x):
            return product(x, hi_ref[...], mid_ref[...], low_ref[...], (((1,), (0,)), ((), ())))

        q_parts = [q_ref[i] for i in range(3)]
        u = times_g(q_parts)
        for turn in range(ITERS):
            u_parts = split3(u)
            gram = product(u_parts, *q_parts, LANES)
            last = turn == ITERS - 1
            v_parts = None if last else split3(times_g(u_parts))
            inv = inverse_factor(gram)
            if last:
                w_out[...] = solve(inv, q_parts)
            q = solve(inv, u_parts) * (1.0 / 32)
            if not last:
                q_parts = split3(q)
                u = solve(inv, v_parts) * (1.0 / 32)
        q_out[...] = q


def iterate(pos, own, away, q_parts):
    _, n, k = q_parts.shape
    part = pl.BlockSpec((2,) + own.shape[1:], lambda s: (s, 0, 0, 0, 0))
    whole = pl.BlockSpec((n, k), lambda s: (0, 0))
    return pl.pallas_call(
        iterate_kernel,
        out_shape=(jax.ShapeDtypeStruct((n, k), F32),) * 2,
        grid=(own.shape[0] // 2,),
        in_specs=[SMEM, part, part, pl.BlockSpec((3, n, k), lambda s: (0, 0, 0))],
        out_specs=(whole, whole),
        scratch_shapes=[pltpu.VMEM((k, k), BF16)] * 3,
        compiler_params=params(20),
        cost_estimate=cost(36 * n * k * k, 4 * k * k),
        name="iterations",
    )(pos, own, away, q_parts)


def left_kernel(pos_ref, w_ref, m0, m1, m3, m2_top, m2_end, out_ref):
    total = None
    n = w_ref.shape[0]
    for turn, start, ref in ((0, 0, m0), (3, 0, m1), (1, 0, m3), (2, 0, m2_top), (2, 128, m2_end)):
        at = pl.multiple_of((pos_ref[1] + turn) % 4 * 256 + start, 128)
        whi, wlow = split2(w_ref[:, pl.ds(at, ref.shape[0])])
        mhi, mlow = split2(ref[...])
        both = jnp.dot(jnp.concatenate([whi, wlow], axis=0), mhi, preferred_element_type=F32)
        part = both[:n] + (both[n:] + jnp.dot(whi, mlow, preferred_element_type=F32))
        total = part if total is None else total + part
    out_ref[...] = total


def left(pos, w, blocks):
    n, d = w.shape[0], blocks[0].shape[1]
    return pl.pallas_call(
        left_kernel,
        out_shape=jax.ShapeDtypeStruct((n, d), F32),
        in_specs=[SMEM] + [VMEM] * 6,
        out_specs=VMEM,
        compiler_params=params(12),
        cost_estimate=cost(6 * n * d * 1024, 2 << 20),
        name="left",
    )(pos, w, *blocks)


def finish_kernel(pos_ref, merged, mom, own, away, q, err_out, mom_out, q_parts):
    i = pl.program_id(0)

    @pl.when(i == 0)
    def _():
        hi, low = split2(q[...])
        q_parts[...] = jnp.concatenate([hi, hi, low, low], axis=0)

    first = i < pl.num_programs(0) // 2
    hi, low = split2(jnp.where(first, own[...], away[...]))
    p_parts = jnp.concatenate([hi, low, hi, low], axis=0)
    for n in range(4):
        cols = pl.ds(256 * n, 256)
        approx = lax.dot_general(p_parts, q_parts[:, cols], ROWS, preferred_element_type=F32)
        err_out[0, :, cols] = (merged[:, cols] - approx).astype(BF16)
        mom_out[:, cols] = (0.9 * mom[:, cols].astype(F32) + approx).astype(BF16)


def finish(pos, merged, momentum, own, away, q):
    n, k = q.shape
    d = momentum.shape[0]
    rows = 256
    half = d // rows // 2

    def row(i, pos):
        return jnp.where(i < half, pos[0], 1 - pos[0]) * half + i % half

    block = pl.BlockSpec((rows, k), lambda i, pos: (row(i, pos), 0))
    return pl.pallas_call(
        finish_kernel,
        out_shape=(jax.ShapeDtypeStruct((1, d, k), BF16), jax.ShapeDtypeStruct(momentum.shape, BF16)),
        grid_spec=pltpu.PrefetchScalarGridSpec(
            num_scalar_prefetch=1,
            grid=(d // rows,),
            in_specs=[
                block,
                block,
                pl.BlockSpec((n, rows), lambda i, pos: (0, jnp.minimum(i, half - 1))),
                pl.BlockSpec((n, rows), lambda i, pos: (0, jnp.maximum(i - half, 0))),
                pl.BlockSpec((n, k), lambda i, pos: (0, 0)),
            ],
            out_specs=(pl.BlockSpec((1, rows, k), lambda i, pos: (0, row(i, pos), 0)), block),
            scratch_shapes=[pltpu.VMEM((4 * n, k), BF16)],
        ),
        compiler_params=params(16),
        cost_estimate=cost(8 * n * d * k, 12 << 20),
        name="finish",
    )(pos, merged, momentum, own, away, q)


TURNS = (2, 1, 3, 0)


def shards(inputs, key_grads, error, momentum, q_start):
    i = lax.axis_index("dp")
    z, y, c = i // 8, (i // 2) % 4, i % 2
    pos = jnp.stack([c, y, z])

    args = (inputs, key_grads, error)
    other, pos = lax.optimization_barrier((merge(pos, TURNS[:1], *args), pos))
    sent_opp = dp_shift(other, dc=1)
    other, sent_opp = lax.optimization_barrier((merge(pos, TURNS[1:], *args), sent_opp))
    sent = dp_shift(other, dc=1)
    opposite = merge(pos, TURNS[:1], *args, sent_opp)
    sums = merge(pos, TURNS[1:], *args, sent)
    parts = ring_sum(opposite, sums[0:2], sums[2:4], sums[4:6], lambda x, d: dp_shift(x, dy=d))
    *opposite, after, before, own = sum_turn(pos, parts)
    came = small_ring_sum(opposite, after, before, lambda x, d: dp_shift(x, dz=d))
    unit = own + (came[0] + came[1])
    z1, z3 = dp_shift(unit, dz=1), dp_shift(unit, dz=-1)
    u1, u2 = dp_shift(unit, dy=1), dp_shift(unit, dy=2)
    units = [unit, u1, u2, z1, z3, dp_shift(z1, dz=1)]

    to_core, part, of_y = g_block(pos, units)
    to_core, of_y = lax.optimization_barrier((to_core, of_y))
    part = part + dp_shift(to_core, dc=1)
    m1, m3 = dp_shift(of_y, dy=1), dp_shift(of_y, dy=-1)
    part = exchange(part, "shard").sum(axis=0)
    part = order(pos, [part] + [dp_shift(part, dz=d) for d in (1, -1, 2)])
    near = [part] + [dp_shift(part, dy=d) for d in (1, -1, 2)]
    near, m1, m3, args, q_t = lax.optimization_barrier((near, m1, m3, args, q_start.T))
    m2_top, m2_end = dp_shift(m1[:128], dy=1), dp_shift(m3[128:], dy=-1)
    part = exchange(spread(pos, near).reshape(8, 16, 3, 8, 128), "shard")
    part, m2_top, m2_end, merged, q_parts = lax.optimization_barrier(
        (part, m2_top, m2_end, *merge_all(*args, q_t))
    )
    q_t, w = iterate(pos, part, dp_shift(part, dc=1), q_parts)

    blocks = [of_y, m1, m3, m2_top, m2_end]
    own = left(pos, w, blocks)
    away = dp_shift(own, dc=1)
    new_error, new_momentum = finish(pos, merged, momentum, own, away, q_t)
    return (new_error, new_momentum, q_t.T)


def solution(mesh):
    return jax.shard_map(
        shards,
        mesh=mesh,
        in_specs=(P("dp", "shard"), P("dp", None), P("dp", "shard", None), P("shard", None), P()),
        out_specs=(P("dp", "shard", None), P("shard", None), P()),
        check_vma=False,
    )
```

```python
import functools
import math

import jax
import jax.numpy as jnp
from jax import lax
from jax.experimental import pallas as pl
from jax.experimental.pallas import tpu as pltpu
from jax.sharding import PartitionSpec as P

ITERS = 3
HIGH = lax.Precision.HIGHEST
ROWS = (((0,), (0,)), ((), ()))
LANES = (((1,), (1,)), ((), ()))
F32 = jnp.float32
BF16 = jnp.bfloat16
VMEM = pl.BlockSpec(memory_space=pltpu.VMEM)
SMEM = pl.BlockSpec(memory_space=pltpu.SMEM)

ZY_GROUPS = [[z * 8 + y * 2 + c for z in range(4) for y in range(4)] for c in range(2)]


def dp_shift(x, dz=0, dy=0, dc=0):
    pairs = []
    for i in range(32):
        z, y, c = i // 8, (i // 2) % 4, i % 2
        pairs.append((i, (z + dz) % 4 * 8 + (y + dy) % 4 * 2 + (c + dc) % 2))
    return lax.ppermute(x, "dp", pairs)


def ring_sum(opposite, following, before, own, step):
    relay_on, relay_back = step(opposite[0], 1), step(opposite[1], -1)
    second, first = step(following[1], 1), step(before[0], -1)
    on, back = step(following[0] + relay_on, 1), step(before[1] + relay_back, -1)
    return own[0] + first, own[1] + second, on, back


def small_ring_sum(opposite, following, before, step):
    n = opposite[0].shape[0]
    relay_on, relay_back = step(opposite[0], 1), step(opposite[1], -1)
    on = step(following + jnp.pad(relay_on, ((0, n), (0, 0))), 1)
    back = step(before + jnp.pad(relay_back, ((n, 0), (0, 0))), -1)
    return on, back


def exchange(x, groups, axis="dp"):
    return lax.all_to_all(x, axis, 0, 0, axis_index_groups=groups)


def params(mib, **more):
    return pltpu.CompilerParams(vmem_limit_bytes=mib << 20, **more)


def cost(flops, read):
    return pl.CostEstimate(flops=flops, bytes_accessed=read, transcendentals=0)


def split2(x):
    hi = x.astype(BF16)
    return hi, (x - hi.astype(F32)).astype(BF16)


def split3(x):
    hi = x.astype(BF16)
    rest = x - hi.astype(F32)
    mid = rest.astype(BF16)
    return hi, mid, (rest - mid.astype(F32)).astype(BF16)


def merge_kernel(turns, own, pos_ref, acts, grads, err, *refs):
    half = pos_ref[0] if own else 1 - pos_ref[0]
    d = acts.shape[1] // 2
    at_d = pl.ds(pl.multiple_of(half * d, 512), d)
    factor = 1.0 / math.sqrt(acts.shape[0])
    x = acts[:, at_d]
    for n, turn in enumerate(turns):
        cols = pl.ds(pl.multiple_of((pos_ref[1] + turn) % 4 * 256, 256), 256)
        product = lax.dot_general(x, grads[:, cols], ROWS, preferred_element_type=F32)
        merged = product * factor + err[0, at_d, cols].astype(F32)
        if own:
            total = merged + refs[0][n]
            refs[1 + 2 * n][...] = total[:d // 2]
            refs[2 + 2 * n][...] = total[d // 2:]
        else:
            refs[0][n] = merged


def merge(pos, turns, inputs, key_grads, error, sent=None):
    tok, d = inputs.shape
    d = d // 2
    n = len(turns)
    own = sent is not None
    outs = (jax.ShapeDtypeStruct((d // 2, 256), F32),) * (2 * n) if own else jax.ShapeDtypeStruct((n, d, 256), F32)
    return pl.pallas_call(
        functools.partial(merge_kernel, turns, own),
        out_shape=outs,
        in_specs=[SMEM] + [VMEM] * (3 + own),
        out_specs=(VMEM,) * (2 * n) if own else VMEM,
        compiler_params=params(16),
        cost_estimate=cost(2 * tok * d * 256 * n, (1 + 2 * n) << 19),
        name="merge",
    )(pos, inputs, key_grads, error, *([sent] if own else []))


def merge_all_kernel(acts, grads, err, q, out_ref, q_parts):
    factor = 1.0 / math.sqrt(acts.shape[0])
    product = lax.dot_general(acts[...], grads[...], ROWS, preferred_element_type=F32)
    out_ref[...] = product * factor + err[0].astype(F32)

    @pl.when(pl.program_id(0) == 0)
    def _():
        for n, part in enumerate(split3(q[...])):
            q_parts[n] = part


def merge_all(inputs, key_grads, error, q):
    tok, d = inputs.shape
    k = key_grads.shape[1]
    rows = 256
    return pl.pallas_call(
        merge_all_kernel,
        out_shape=(jax.ShapeDtypeStruct((d, k), F32), jax.ShapeDtypeStruct((3,) + q.shape, BF16)),
        grid=(d // rows,),
        in_specs=[
            pl.BlockSpec((tok, rows), lambda i: (0, i)),
            pl.BlockSpec((tok, k), lambda i: (0, 0)),
            pl.BlockSpec((1, rows, k), lambda i: (0, i, 0)),
            pl.BlockSpec(q.shape, lambda i: (0, 0)),
        ],
        out_specs=(
            pl.BlockSpec((rows, k), lambda i: (i, 0)),
            pl.BlockSpec((3,) + q.shape, lambda i: (0, 0, 0)),
        ),
        compiler_params=params(16),
        cost_estimate=cost(2 * tok * d * k, 8 << 20),
        name="merge_all",
    )(inputs, key_grads, error, q)


def sum_turn_kernel(pos_ref, top, end, on, back, opp_top, opp_end, after, before, own, turned):
    turned[:, :256] = (top[...] + on[...]).T
    turned[:, 256:] = (end[...] + back[...]).T
    z = pos_ref[2]

    def rows(turn, start, size):
        return turned[pl.ds(pl.multiple_of((z + turn) % 4 * 64 + start, 32), size), :]

    opp_top[...] = rows(2, 0, 32)
    opp_end[...] = rows(2, 32, 32)
    after[...] = rows(1, 0, 64)
    before[...] = rows(3, 0, 64)
    own[...] = rows(0, 0, 64)


def sum_turn(pos, parts):
    outs = tuple(jax.ShapeDtypeStruct((n, 512), F32) for n in (32, 32, 64, 64, 64))
    return pl.pallas_call(
        sum_turn_kernel,
        out_shape=outs,
        in_specs=[SMEM] + [VMEM] * 4,
        out_specs=(VMEM,) * 5,
        scratch_shapes=[pltpu.VMEM((256, 512), F32)],
        compiler_params=params(12),
        cost_estimate=cost(4 << 17, 3 << 20),
        name="sum_turn",
    )(pos, *parts)


def spread_kernel(leading, x_ref, copies_ref):
    total = x_ref[0] if leading else x_ref[...]
    for i in range(1, x_ref.shape[0] if leading else 1):
        total = total + x_ref[i]
    for i in range(copies_ref.shape[0]):
        copies_ref[i] = total


def spread(x, copies, leading=False):
    return pl.pallas_call(
        functools.partial(spread_kernel, leading),
        out_shape=jax.ShapeDtypeStruct((copies,) + x.shape[leading:], F32),
        in_specs=[VMEM],
        out_specs=VMEM,
        compiler_params=params(10),
        cost_estimate=cost(1 << 17, 1 << 20),
        name="spread",
    )(x)


def block_kernel(pos_ref, unit, u1, u2, z1, z3, z2, sent_ref, mine_ref, of_y):
    core, z = pos_ref[0], pos_ref[2]
    for turn, ref in ((0, unit), (3, z1), (1, z3), (2, z2)):
        of_y[pl.ds(pl.multiple_of((z + turn) % 4 * 64, 64), 64), :] = ref[...]
    rows = jnp.concatenate([unit[...], u1[...], u2[...]], axis=0)
    block = lax.dot_general(rows, of_y[...], LANES, precision=HIGH, preferred_element_type=F32)

    def put(ref, part):
        for e in range(3):
            for s in range(8):
                ref[s, e] = part[64 * e + 8 * s:64 * e + 8 * s + 8]

    @pl.when(core == 0)
    def _():
        put(mine_ref, block[:, :128])
        put(sent_ref, block[:, 128:])

    @pl.when(core == 1)
    def _():
        put(mine_ref, block[:, 128:])
        put(sent_ref, block[:, :128])


def g_block(pos, units):
    k, d = units[0].shape
    return pl.pallas_call(
        block_kernel,
        out_shape=(jax.ShapeDtypeStruct((8, 3, 8, 128), F32),) * 2 + (jax.ShapeDtypeStruct((4 * k, d), F32),),
        in_specs=[SMEM] + [VMEM] * 6,
        out_specs=(VMEM,) * 3,
        compiler_params=params(12),
        cost_estimate=cost(2 * 6 * 192 * 4 * k * d, 2 << 20),
        name="g_block",
    )(pos, *units)


def inverse_factor(gram):
    n = gram.shape[0]
    tiles = n // 8
    row = lax.broadcasted_iota(jnp.int32, (n, n), 0)
    col = lax.broadcasted_iota(jnp.int32, (n, n), 1)
    diagonal = jnp.where(row == col, gram, 0.0)
    scale = lax.rsqrt(jnp.sum(diagonal, axis=0, keepdims=True))
    gram = gram * lax.rsqrt(jnp.sum(diagonal, axis=1, keepdims=True)) * scale
    both = jnp.concatenate([gram, jnp.where(row == col, 1.0, 0.0)], axis=1)
    b = [both[8 * r:8 * r + 8] for r in range(tiles)]
    sub = lax.broadcasted_iota(jnp.int32, (8, 2 * n), 0)

    def spread_row(x, k):
        return jnp.broadcast_to(x[k:k + 1], (8, 2 * n))

    out = []
    for t in range(tiles):
        c = {
            (r, k): jnp.broadcast_to(b[r][:, 8 * t + k:8 * t + k + 1], (8, 2 * n))
            for r in range(t, tiles)
            for k in range(8)
        }
        pivots = jnp.ones((8, 2 * n), F32)
        for k in range(0, 8, 2):
            here, after = c[t, k], c[t, k + 1]
            p11, p12 = spread_row(here, k), spread_row(after, k)
            p21, p22 = spread_row(here, k + 1), spread_row(after, k + 1)
            det = p11 * p22 - p12 * p21
            turn, turn_one = 1.0 / det, 1.0 / p11
            pivots = jnp.where(sub == k, p11, jnp.where(sub == k + 1, det * turn_one, pivots))
            lead, lead_after = spread_row(b[t], k), spread_row(b[t], k + 1)
            heads = {l: (spread_row(c[t, l], k), spread_row(c[t, l], k + 1)) for l in range(k + 2, 8)}
            for r in range(t, tiles):
                m = (c[r, k] * p22 - c[r, k + 1] * p21) * turn
                m_after = (c[r, k + 1] * p11 - c[r, k] * p12) * turn
                for l in range(k + 2, 8):
                    c[r, l] = c[r, l] - (m * heads[l][0] + m_after * heads[l][1])
                if r == t:
                    m = jnp.where(sub > k + 1, m, jnp.where(sub == k + 1, p21 * turn_one, 0.0))
                    m_after = jnp.where(sub > k + 1, m_after, 0.0)
                b[r] = b[r] - (m * lead + m_after * lead_after)
        out.append(b[t] / jnp.sqrt(pivots))
    return jnp.concatenate(out, axis=0)[:, n:] * scale


def iterate_kernel(pos_ref, own_ref, away_ref, q_ref, q_out, w_out, hi_ref, mid_ref, low_ref):
    s = pl.program_id(0)
    parts = (hi_ref, mid_ref, low_ref)
    for ref, core in ((own_ref, pos_ref[0]), (away_ref, 1 - pos_ref[0])):
        for z in range(4):
            ready = []
            for y in range(4):
                for e in range(3):
                    both = jnp.concatenate([ref[0, z * 4 + y, e], ref[1, z * 4 + y, e]], axis=0)
                    ready.append((y, e, split3(both)))
            for y, e, values in ready:
                to = pl.ds(pl.multiple_of(y * 256 + core * 128, 128), 128)
                at = pl.ds(pl.multiple_of((y - e) % 4 * 256 + z * 64 + s * 16, 16), 16)
                for part, value in zip(parts, values):
                    part[at, to] = value

    @pl.when(s == pl.num_programs(0) - 1)
    def _():
        for y in range(4):
            here, after = pl.ds(y * 256, 256), pl.ds((y + 1) % 4 * 256, 256)
            for part in parts:
                part[after, here] = part[here, after].T
        n = q_out.shape[0]
        def product(x, y_hi, y_mid, y_low, dims):
            hi, mid, low = x
            by_hi = lax.dot_general(jnp.concatenate([hi, mid, low], axis=0), y_hi, dims, preferred_element_type=F32)
            by_mid = lax.dot_general(jnp.concatenate([hi, mid], axis=0), y_mid, dims, preferred_element_type=F32)
            by_low = lax.dot_general(hi, y_low, dims, preferred_element_type=F32)
            small = by_hi[2 * n:] + by_mid[n:] + by_low
            return by_hi[:n] + (by_hi[n:2 * n] + by_mid[:n] + small)

        def solve(inv, x):
            hi, mid, low = split3(inv)
            left_parts = jnp.concatenate([hi, hi, mid, mid, hi, low], axis=1)
            right_parts = jnp.concatenate([x[0], x[1], x[0], x[1], x[2], x[0]], axis=0)
            return jnp.dot(left_parts, right_parts, preferred_element_type=F32)

        def times_g(x):
            return product(x, hi_ref[...], mid_ref[...], low_ref[...], (((1,), (0,)), ((), ())))

        q_parts = [q_ref[i] for i in range(3)]
        u = times_g(q_parts)
        for turn in range(ITERS):
            u_parts = split3(u)
            gram = product(u_parts, *q_parts, LANES)
            last = turn == ITERS - 1
            v_parts = None if last else split3(times_g(u_parts))
            inv = inverse_factor(gram)
            if last:
                w_out[...] = solve(inv, q_parts)
            q = solve(inv, u_parts) * (1.0 / 32)
            if not last:
                q_parts = split3(q)
                u = solve(inv, v_parts) * (1.0 / 32)
        q_out[...] = q


def iterate(pos, own, away, q_parts):
    _, n, k = q_parts.shape
    part = pl.BlockSpec((2,) + own.shape[1:], lambda s: (s, 0, 0, 0, 0))
    whole = pl.BlockSpec((n, k), lambda s: (0, 0))
    return pl.pallas_call(
        iterate_kernel,
        out_shape=(jax.ShapeDtypeStruct((n, k), F32),) * 2,
        grid=(own.shape[0] // 2,),
        in_specs=[SMEM, part, part, pl.BlockSpec((3, n, k), lambda s: (0, 0, 0))],
        out_specs=(whole, whole),
        scratch_shapes=[pltpu.VMEM((k, k), BF16)] * 3,
        compiler_params=params(20),
        cost_estimate=cost(36 * n * k * k, 4 * k * k),
        name="iterations",
    )(pos, own, away, q_parts)


def left_kernel(pos_ref, w_ref, m0, m1, m3, m2_top, m2_end, out_ref):
    total = None
    n = w_ref.shape[0]
    for turn, start, ref in ((0, 0, m0), (3, 0, m1), (1, 0, m3), (2, 0, m2_top), (2, 128, m2_end)):
        at = pl.multiple_of((pos_ref[1] + turn) % 4 * 256 + start, 128)
        whi, wlow = split2(w_ref[:, pl.ds(at, ref.shape[0])])
        mhi, mlow = split2(ref[...])
        both = jnp.dot(jnp.concatenate([whi, wlow], axis=0), mhi, preferred_element_type=F32)
        part = both[:n] + (both[n:] + jnp.dot(whi, mlow, preferred_element_type=F32))
        total = part if total is None else total + part
    out_ref[...] = total


def left(pos, w, blocks):
    n, d = w.shape[0], blocks[0].shape[1]
    return pl.pallas_call(
        left_kernel,
        out_shape=jax.ShapeDtypeStruct((n, d), F32),
        in_specs=[SMEM] + [VMEM] * 6,
        out_specs=VMEM,
        compiler_params=params(12),
        cost_estimate=cost(6 * n * d * 1024, 2 << 20),
        name="left",
    )(pos, w, *blocks)


def finish_kernel(pos_ref, merged, mom, own, away, q, err_out, mom_out, q_parts):
    i = pl.program_id(0)

    @pl.when(i == 0)
    def _():
        hi, low = split2(q[...])
        q_parts[...] = jnp.concatenate([hi, hi, low, low], axis=0)

    first = i < pl.num_programs(0) // 2
    hi, low = split2(jnp.where(first, own[...], away[...]))
    p_parts = jnp.concatenate([hi, low, hi, low], axis=0)
    for n in range(4):
        cols = pl.ds(256 * n, 256)
        approx = lax.dot_general(p_parts, q_parts[:, cols], ROWS, preferred_element_type=F32)
        err_out[0, :, cols] = (merged[:, cols] - approx).astype(BF16)
        mom_out[:, cols] = (0.9 * mom[:, cols].astype(F32) + approx).astype(BF16)


def finish(pos, merged, momentum, own, away, q):
    n, k = q.shape
    d = momentum.shape[0]
    rows = 256
    half = d // rows // 2

    def row(i, pos):
        return jnp.where(i < half, pos[0], 1 - pos[0]) * half + i % half

    block = pl.BlockSpec((rows, k), lambda i, pos: (row(i, pos), 0))
    return pl.pallas_call(
        finish_kernel,
        out_shape=(jax.ShapeDtypeStruct((1, d, k), BF16), jax.ShapeDtypeStruct(momentum.shape, BF16)),
        grid_spec=pltpu.PrefetchScalarGridSpec(
            num_scalar_prefetch=1,
            grid=(d // rows,),
            in_specs=[
                block,
                block,
                pl.BlockSpec((n, rows), lambda i, pos: (0, jnp.minimum(i, half - 1))),
                pl.BlockSpec((n, rows), lambda i, pos: (0, jnp.maximum(i - half, 0))),
                pl.BlockSpec((n, k), lambda i, pos: (0, 0)),
            ],
            out_specs=(pl.BlockSpec((1, rows, k), lambda i, pos: (0, row(i, pos), 0)), block),
            scratch_shapes=[pltpu.VMEM((4 * n, k), BF16)],
        ),
        compiler_params=params(16),
        cost_estimate=cost(8 * n * d * k, 12 << 20),
        name="finish",
    )(pos, merged, momentum, own, away, q)


TURNS = (2, 1, 3, 0)


def shards(inputs, key_grads, error, momentum, q_start):
    i = lax.axis_index("dp")
    z, y, c = i // 8, (i // 2) % 4, i % 2
    pos = jnp.stack([c, y, z])

    args = (inputs, key_grads, error)
    other, pos = lax.optimization_barrier((merge(pos, TURNS[:1], *args), pos))
    sent_opp = dp_shift(other, dc=1)
    other, sent_opp = lax.optimization_barrier((merge(pos, TURNS[1:], *args), sent_opp))
    sent = dp_shift(other, dc=1)
    opposite = merge(pos, TURNS[:1], *args, sent_opp)
    sums = merge(pos, TURNS[1:], *args, sent)
    parts = ring_sum(opposite, sums[0:2], sums[2:4], sums[4:6], lambda x, d: dp_shift(x, dy=d))
    *opposite, after, before, own = sum_turn(pos, parts)
    came = small_ring_sum(opposite, after, before, lambda x, d: dp_shift(x, dz=d))
    unit = own + (came[0] + came[1])
    z1, z3 = dp_shift(unit, dz=1), dp_shift(unit, dz=-1)
    u1, u2 = dp_shift(unit, dy=1), dp_shift(unit, dy=2)
    units = [unit, u1, u2, z1, z3, dp_shift(z1, dz=1)]

    to_core, part, of_y = g_block(pos, units)
    to_core, of_y = lax.optimization_barrier((to_core, of_y))
    part = part + dp_shift(to_core, dc=1)
    m1, m3 = dp_shift(of_y, dy=1), dp_shift(of_y, dy=-1)
    copies = spread(exchange(part, None, "shard"), 16, leading=True)
    part = exchange(copies, ZY_GROUPS)
    part, m1, m3, args, q_t = lax.optimization_barrier((part, m1, m3, args, q_start.T))
    m2_top, m2_end = dp_shift(m1[:128], dy=1), dp_shift(m3[128:], dy=-1)
    part = exchange(spread(part, 8), None, "shard")
    part, m2_top, m2_end, merged, q_parts = lax.optimization_barrier(
        (part, m2_top, m2_end, *merge_all(*args, q_t))
    )
    q_t, w = iterate(pos, part, dp_shift(part, dc=1), q_parts)

    blocks = [of_y, m1, m3, m2_top, m2_end]
    own = left(pos, w, blocks)
    away = dp_shift(own, dc=1)
    new_error, new_momentum = finish(pos, merged, momentum, own, away, q_t)
    return (new_error, new_momentum, q_t.T)


def solution(mesh):
    return jax.shard_map(
        shards,
        mesh=mesh,
        in_specs=(P("dp", "shard"), P("dp", None), P("dp", "shard", None), P("shard", None), P()),
        out_specs=(P("dp", "shard", None), P("shard", None), P()),
        check_vma=False,
    )
```

```python
import functools
import math

import jax
import jax.numpy as jnp
from jax import lax
from jax.experimental import pallas as pl
from jax.experimental.pallas import tpu as pltpu
from jax.sharding import PartitionSpec as P

ITERS = 3
HIGH = lax.Precision.HIGHEST
ROWS = (((0,), (0,)), ((), ()))
LANES = (((1,), (1,)), ((), ()))
F32 = jnp.float32
BF16 = jnp.bfloat16
VMEM = pl.BlockSpec(memory_space=pltpu.VMEM)
SMEM = pl.BlockSpec(memory_space=pltpu.SMEM)

ZY_GROUPS = [[z * 8 + y * 2 + c for z in range(4) for y in range(4)] for c in range(2)]


def dp_shift(x, dz=0, dy=0, dc=0):
    pairs = []
    for i in range(32):
        z, y, c = i // 8, (i // 2) % 4, i % 2
        pairs.append((i, (z + dz) % 4 * 8 + (y + dy) % 4 * 2 + (c + dc) % 2))
    return lax.ppermute(x, "dp", pairs)


def ring_sum(opposite, following, before, own, step):
    relay_on, relay_back = step(opposite[0], 1), step(opposite[1], -1)
    second, first = step(following[1], 1), step(before[0], -1)
    on, back = step(following[0] + relay_on, 1), step(before[1] + relay_back, -1)
    return own[0] + first, own[1] + second, on, back


def small_ring_sum(opposite, following, before, step):
    n = opposite[0].shape[0]
    relay_on, relay_back = step(opposite[0], 1), step(opposite[1], -1)
    on = step(following + jnp.pad(relay_on, ((0, n), (0, 0))), 1)
    back = step(before + jnp.pad(relay_back, ((n, 0), (0, 0))), -1)
    return on, back


def exchange(x, groups, axis="dp"):
    return lax.all_to_all(x, axis, 0, 0, axis_index_groups=groups)


def params(mib, **more):
    return pltpu.CompilerParams(vmem_limit_bytes=mib << 20, **more)


def cost(flops, read):
    return pl.CostEstimate(flops=flops, bytes_accessed=read, transcendentals=0)


def split2(x):
    hi = x.astype(BF16)
    return hi, (x - hi.astype(F32)).astype(BF16)


def split3(x):
    hi = x.astype(BF16)
    rest = x - hi.astype(F32)
    mid = rest.astype(BF16)
    return hi, mid, (rest - mid.astype(F32)).astype(BF16)


def merge_kernel(turns, own, pos_ref, acts, grads, err, *refs):
    half = pos_ref[0] if own else 1 - pos_ref[0]
    d = acts.shape[1] // 2
    at_d = pl.ds(pl.multiple_of(half * d, 512), d)
    factor = 1.0 / math.sqrt(acts.shape[0])
    x = acts[:, at_d]
    for n, turn in enumerate(turns):
        cols = pl.ds(pl.multiple_of((pos_ref[1] + turn) % 4 * 256, 256), 256)
        product = lax.dot_general(x, grads[:, cols], ROWS, preferred_element_type=F32)
        merged = product * factor + err[0, at_d, cols].astype(F32)
        if own:
            total = merged + refs[0][n]
            refs[1 + 2 * n][...] = total[:d // 2]
            refs[2 + 2 * n][...] = total[d // 2:]
        else:
            refs[0][n] = merged


def merge(pos, turns, inputs, key_grads, error, sent=None):
    tok, d = inputs.shape
    d = d // 2
    n = len(turns)
    own = sent is not None
    outs = (jax.ShapeDtypeStruct((d // 2, 256), F32),) * (2 * n) if own else jax.ShapeDtypeStruct((n, d, 256), F32)
    return pl.pallas_call(
        functools.partial(merge_kernel, turns, own),
        out_shape=outs,
        in_specs=[SMEM] + [VMEM] * (3 + own),
        out_specs=(VMEM,) * (2 * n) if own else VMEM,
        compiler_params=params(16),
        cost_estimate=cost(2 * tok * d * 256 * n, (1 + 2 * n) << 19),
        name="merge",
    )(pos, inputs, key_grads, error, *([sent] if own else []))


def merge_all_kernel(acts, grads, err, q, out_ref, q_parts):
    factor = 1.0 / math.sqrt(acts.shape[0])
    product = lax.dot_general(acts[...], grads[...], ROWS, preferred_element_type=F32)
    out_ref[...] = product * factor + err[0].astype(F32)

    @pl.when(pl.program_id(0) == 0)
    def _():
        for n, part in enumerate(split3(q[...])):
            q_parts[n] = part


def merge_all(inputs, key_grads, error, q):
    tok, d = inputs.shape
    k = key_grads.shape[1]
    rows = 256
    return pl.pallas_call(
        merge_all_kernel,
        out_shape=(jax.ShapeDtypeStruct((d, k), F32), jax.ShapeDtypeStruct((3,) + q.shape, BF16)),
        grid=(d // rows,),
        in_specs=[
            pl.BlockSpec((tok, rows), lambda i: (0, i)),
            pl.BlockSpec((tok, k), lambda i: (0, 0)),
            pl.BlockSpec((1, rows, k), lambda i: (0, i, 0)),
            pl.BlockSpec(q.shape, lambda i: (0, 0)),
        ],
        out_specs=(
            pl.BlockSpec((rows, k), lambda i: (i, 0)),
            pl.BlockSpec((3,) + q.shape, lambda i: (0, 0, 0)),
        ),
        compiler_params=params(16),
        cost_estimate=cost(2 * tok * d * k, 8 << 20),
        name="merge_all",
    )(inputs, key_grads, error, q)


def sum_turn_kernel(pos_ref, top, end, on, back, opp_top, opp_end, after, before, own, turned):
    turned[:, :256] = (top[...] + on[...]).T
    turned[:, 256:] = (end[...] + back[...]).T
    z = pos_ref[2]

    def rows(turn, start, size):
        return turned[pl.ds(pl.multiple_of((z + turn) % 4 * 64 + start, 32), size), :]

    opp_top[...] = rows(2, 0, 32)
    opp_end[...] = rows(2, 32, 32)
    after[...] = rows(1, 0, 64)
    before[...] = rows(3, 0, 64)
    own[...] = rows(0, 0, 64)


def sum_turn(pos, parts):
    outs = tuple(jax.ShapeDtypeStruct((n, 512), F32) for n in (32, 32, 64, 64, 64))
    return pl.pallas_call(
        sum_turn_kernel,
        out_shape=outs,
        in_specs=[SMEM] + [VMEM] * 4,
        out_specs=(VMEM,) * 5,
        scratch_shapes=[pltpu.VMEM((256, 512), F32)],
        compiler_params=params(12),
        cost_estimate=cost(4 << 17, 3 << 20),
        name="sum_turn",
    )(pos, *parts)


def spread_kernel(leading, x_ref, copies_ref):
    total = x_ref[0] if leading else x_ref[...]
    for i in range(1, x_ref.shape[0] if leading else 1):
        total = total + x_ref[i]
    for i in range(copies_ref.shape[0]):
        copies_ref[i] = total


def spread(x, copies, leading=False):
    return pl.pallas_call(
        functools.partial(spread_kernel, leading),
        out_shape=jax.ShapeDtypeStruct((copies,) + x.shape[leading:], F32),
        in_specs=[VMEM],
        out_specs=VMEM,
        compiler_params=params(10),
        cost_estimate=cost(1 << 17, 1 << 20),
        name="spread",
    )(x)


def block_kernel(pos_ref, unit, u1, u2, z1, z3, z2, sent_ref, mine_ref, of_y):
    core, z = pos_ref[0], pos_ref[2]
    for turn, ref in ((0, unit), (3, z1), (1, z3), (2, z2)):
        of_y[pl.ds(pl.multiple_of((z + turn) % 4 * 64, 64), 64), :] = ref[...]
    rows = jnp.concatenate([unit[...], u1[...], u2[...]], axis=0)
    block = lax.dot_general(rows, of_y[...], LANES, precision=HIGH, preferred_element_type=F32)

    def put(ref, part):
        for e in range(3):
            for s in range(8):
                ref[s, e] = part[64 * e + 8 * s:64 * e + 8 * s + 8]

    @pl.when(core == 0)
    def _():
        put(mine_ref, block[:, :128])
        put(sent_ref, block[:, 128:])

    @pl.when(core == 1)
    def _():
        put(mine_ref, block[:, 128:])
        put(sent_ref, block[:, :128])


def g_block(pos, units):
    k, d = units[0].shape
    return pl.pallas_call(
        block_kernel,
        out_shape=(jax.ShapeDtypeStruct((8, 3, 8, 128), F32),) * 2 + (jax.ShapeDtypeStruct((4 * k, d), F32),),
        in_specs=[SMEM] + [VMEM] * 6,
        out_specs=(VMEM,) * 3,
        compiler_params=params(12),
        cost_estimate=cost(2 * 6 * 192 * 4 * k * d, 2 << 20),
        name="g_block",
    )(pos, *units)


def inverse_factor(gram):
    n = gram.shape[0]
    tiles = n // 8
    row = lax.broadcasted_iota(jnp.int32, (n, n), 0)
    col = lax.broadcasted_iota(jnp.int32, (n, n), 1)
    diagonal = jnp.where(row == col, gram, 0.0)
    scale = lax.rsqrt(jnp.sum(diagonal, axis=0, keepdims=True))
    gram = gram * lax.rsqrt(jnp.sum(diagonal, axis=1, keepdims=True)) * scale
    both = jnp.concatenate([gram, jnp.where(row == col, 1.0, 0.0)], axis=1)
    b = [both[8 * r:8 * r + 8] for r in range(tiles)]
    sub = lax.broadcasted_iota(jnp.int32, (8, 2 * n), 0)

    def spread_row(x, k):
        return jnp.broadcast_to(x[k:k + 1], (8, 2 * n))

    out = []
    for t in range(tiles):
        c = {
            (r, k): jnp.broadcast_to(b[r][:, 8 * t + k:8 * t + k + 1], (8, 2 * n))
            for r in range(t, tiles)
            for k in range(8)
        }
        pivots = jnp.ones((8, 2 * n), F32)
        for k in range(0, 8, 2):
            here, after = c[t, k], c[t, k + 1]
            p11, p12 = spread_row(here, k), spread_row(after, k)
            p21, p22 = spread_row(here, k + 1), spread_row(after, k + 1)
            det = p11 * p22 - p12 * p21
            turn, turn_one = 1.0 / det, 1.0 / p11
            pivots = jnp.where(sub == k, p11, jnp.where(sub == k + 1, det * turn_one, pivots))
            lead, lead_after = spread_row(b[t], k), spread_row(b[t], k + 1)
            heads = {l: (spread_row(c[t, l], k), spread_row(c[t, l], k + 1)) for l in range(k + 2, 8)}
            for r in range(t, tiles):
                m = (c[r, k] * p22 - c[r, k + 1] * p21) * turn
                m_after = (c[r, k + 1] * p11 - c[r, k] * p12) * turn
                for l in range(k + 2, 8):
                    c[r, l] = c[r, l] - (m * heads[l][0] + m_after * heads[l][1])
                if r == t:
                    m = jnp.where(sub > k + 1, m, jnp.where(sub == k + 1, p21 * turn_one, 0.0))
                    m_after = jnp.where(sub > k + 1, m_after, 0.0)
                b[r] = b[r] - (m * lead + m_after * lead_after)
        out.append(b[t] / jnp.sqrt(pivots))
    return jnp.concatenate(out, axis=0)[:, n:] * scale


def iterate_kernel(pos_ref, own_ref, away_ref, q_ref, q_out, w_out, hi_ref, mid_ref, low_ref):
    s = pl.program_id(0)
    parts = (hi_ref, mid_ref, low_ref)
    for ref, core in ((own_ref, pos_ref[0]), (away_ref, 1 - pos_ref[0])):
        for z in range(4):
            ready = []
            for y in range(4):
                for e in range(3):
                    both = jnp.concatenate([ref[0, z * 4 + y, e], ref[1, z * 4 + y, e]], axis=0)
                    ready.append((y, e, split3(both)))
            for y, e, values in ready:
                to = pl.ds(pl.multiple_of(y * 256 + core * 128, 128), 128)
                at = pl.ds(pl.multiple_of((y - e) % 4 * 256 + z * 64 + s * 16, 16), 16)
                for part, value in zip(parts, values):
                    part[at, to] = value

    @pl.when(s == pl.num_programs(0) - 1)
    def _():
        for y in range(4):
            here, after = pl.ds(y * 256, 256), pl.ds((y + 1) % 4 * 256, 256)
            for part in parts:
                part[after, here] = part[here, after].T
        n = q_out.shape[0]
        def product(x, y_hi, y_mid, y_low, dims):
            hi, mid, low = x
            by_hi = lax.dot_general(jnp.concatenate([hi, mid, low], axis=0), y_hi, dims, preferred_element_type=F32)
            by_mid = lax.dot_general(jnp.concatenate([hi, mid], axis=0), y_mid, dims, preferred_element_type=F32)
            by_low = lax.dot_general(hi, y_low, dims, preferred_element_type=F32)
            small = by_hi[2 * n:] + by_mid[n:] + by_low
            return by_hi[:n] + (by_hi[n:2 * n] + by_mid[:n] + small)

        def solve(inv, x):
            hi, mid, low = split3(inv)
            left_parts = jnp.concatenate([hi, hi, mid, mid, hi, low], axis=1)
            right_parts = jnp.concatenate([x[0], x[1], x[0], x[1], x[2], x[0]], axis=0)
            return jnp.dot(left_parts, right_parts, preferred_element_type=F32)

        def times_g(x):
            return product(x, hi_ref[...], mid_ref[...], low_ref[...], (((1,), (0,)), ((), ())))

        q_parts = [q_ref[i] for i in range(3)]
        u = times_g(q_parts)
        for turn in range(ITERS):
            u_parts = split3(u)
            gram = product(u_parts, *q_parts, LANES)
            last = turn == ITERS - 1
            v_parts = None if last else split3(times_g(u_parts))
            inv = inverse_factor(gram)
            if last:
                w_out[...] = solve(inv, q_parts)
            q = solve(inv, u_parts) * (1.0 / 32)
            if not last:
                q_parts = split3(q)
                u = solve(inv, v_parts) * (1.0 / 32)
        q_out[...] = q


def iterate(pos, own, away, q_parts):
    _, n, k = q_parts.shape
    part = pl.BlockSpec((2,) + own.shape[1:], lambda s: (s, 0, 0, 0, 0))
    whole = pl.BlockSpec((n, k), lambda s: (0, 0))
    return pl.pallas_call(
        iterate_kernel,
        out_shape=(jax.ShapeDtypeStruct((n, k), F32),) * 2,
        grid=(own.shape[0] // 2,),
        in_specs=[SMEM, part, part, pl.BlockSpec((3, n, k), lambda s: (0, 0, 0))],
        out_specs=(whole, whole),
        scratch_shapes=[pltpu.VMEM((k, k), BF16)] * 3,
        compiler_params=params(17),
        cost_estimate=cost(36 * n * k * k, 4 * k * k),
        name="iterations",
    )(pos, own, away, q_parts)


def left_kernel(pos_ref, w_ref, m0, m1, m3, m2_top, m2_end, out_ref):
    total = None
    n = w_ref.shape[0]
    for turn, start, ref in ((0, 0, m0), (3, 0, m1), (1, 0, m3), (2, 0, m2_top), (2, 128, m2_end)):
        at = pl.multiple_of((pos_ref[1] + turn) % 4 * 256 + start, 128)
        whi, wlow = split2(w_ref[:, pl.ds(at, ref.shape[0])])
        mhi, mlow = split2(ref[...])
        both = jnp.dot(jnp.concatenate([whi, wlow], axis=0), mhi, preferred_element_type=F32)
        part = both[:n] + (both[n:] + jnp.dot(whi, mlow, preferred_element_type=F32))
        total = part if total is None else total + part
    out_ref[...] = total


def left(pos, w, blocks):
    n, d = w.shape[0], blocks[0].shape[1]
    return pl.pallas_call(
        left_kernel,
        out_shape=jax.ShapeDtypeStruct((n, d), F32),
        in_specs=[SMEM] + [VMEM] * 6,
        out_specs=VMEM,
        compiler_params=params(12),
        cost_estimate=cost(6 * n * d * 1024, 2 << 20),
        name="left",
    )(pos, w, *blocks)


def finish_kernel(pos_ref, merged, mom, own, away, q, err_out, mom_out, q_parts):
    i = pl.program_id(0)

    @pl.when(i == 0)
    def _():
        hi, low = split2(q[...])
        q_parts[...] = jnp.concatenate([hi, hi, low, low], axis=0)

    first = i < pl.num_programs(0) // 2
    hi, low = split2(jnp.where(first, own[...], away[...]))
    p_parts = jnp.concatenate([hi, low, hi, low], axis=0)
    for n in range(4):
        cols = pl.ds(256 * n, 256)
        approx = lax.dot_general(p_parts, q_parts[:, cols], ROWS, preferred_element_type=F32)
        err_out[0, :, cols] = (merged[:, cols] - approx).astype(BF16)
        mom_out[:, cols] = (0.9 * mom[:, cols].astype(F32) + approx).astype(BF16)


def finish(pos, merged, momentum, own, away, q):
    n, k = q.shape
    d = momentum.shape[0]
    rows = 256
    half = d // rows // 2

    def row(i, pos):
        return jnp.where(i < half, pos[0], 1 - pos[0]) * half + i % half

    block = pl.BlockSpec((rows, k), lambda i, pos: (row(i, pos), 0))
    return pl.pallas_call(
        finish_kernel,
        out_shape=(jax.ShapeDtypeStruct((1, d, k), BF16), jax.ShapeDtypeStruct(momentum.shape, BF16)),
        grid_spec=pltpu.PrefetchScalarGridSpec(
            num_scalar_prefetch=1,
            grid=(d // rows,),
            in_specs=[
                block,
                block,
                pl.BlockSpec((n, rows), lambda i, pos: (0, jnp.minimum(i, half - 1))),
                pl.BlockSpec((n, rows), lambda i, pos: (0, jnp.maximum(i - half, 0))),
                pl.BlockSpec((n, k), lambda i, pos: (0, 0)),
            ],
            out_specs=(pl.BlockSpec((1, rows, k), lambda i, pos: (0, row(i, pos), 0)), block),
            scratch_shapes=[pltpu.VMEM((4 * n, k), BF16)],
        ),
        compiler_params=params(16),
        cost_estimate=cost(8 * n * d * k, 12 << 20),
        name="finish",
    )(pos, merged, momentum, own, away, q)


TURNS = (2, 1, 3, 0)


def shards(inputs, key_grads, error, momentum, q_start):
    i = lax.axis_index("dp")
    z, y, c = i // 8, (i // 2) % 4, i % 2
    pos = jnp.stack([c, y, z])

    args = (inputs, key_grads, error)
    other, pos = lax.optimization_barrier((merge(pos, TURNS[:1], *args), pos))
    sent_opp = dp_shift(other, dc=1)
    other, sent_opp = lax.optimization_barrier((merge(pos, TURNS[1:], *args), sent_opp))
    sent = dp_shift(other, dc=1)
    opposite = merge(pos, TURNS[:1], *args, sent_opp)
    sums = merge(pos, TURNS[1:], *args, sent)
    parts = ring_sum(opposite, sums[0:2], sums[2:4], sums[4:6], lambda x, d: dp_shift(x, dy=d))
    *opposite, after, before, own = sum_turn(pos, parts)
    came = small_ring_sum(opposite, after, before, lambda x, d: dp_shift(x, dz=d))
    unit = own + (came[0] + came[1])
    z1, z3 = dp_shift(unit, dz=1), dp_shift(unit, dz=-1)
    u1, u2 = dp_shift(unit, dy=1), dp_shift(unit, dy=2)
    units = [unit, u1, u2, z1, z3, dp_shift(z1, dz=1)]

    to_core, part, of_y = g_block(pos, units)
    to_core, of_y = lax.optimization_barrier((to_core, of_y))
    part = part + dp_shift(to_core, dc=1)
    m1, m3 = dp_shift(of_y, dy=1), dp_shift(of_y, dy=-1)
    copies = spread(exchange(part, None, "shard"), 16, leading=True)
    part = exchange(copies, ZY_GROUPS)
    part, m1, m3, args, q_t = lax.optimization_barrier((part, m1, m3, args, q_start.T))
    m2_top, m2_end = dp_shift(m1[:128], dy=1), dp_shift(m3[128:], dy=-1)
    part = exchange(spread(part, 8), None, "shard")
    part, m2_top, m2_end, merged, q_parts = lax.optimization_barrier(
        (part, m2_top, m2_end, *merge_all(*args, q_t))
    )
    q_t, w = iterate(pos, part, dp_shift(part, dc=1), q_parts)

    blocks = [of_y, m1, m3, m2_top, m2_end]
    own = left(pos, w, blocks)
    away = dp_shift(own, dc=1)
    new_error, new_momentum = finish(pos, merged, momentum, own, away, q_t)
    return (new_error, new_momentum, q_t.T)


def solution(mesh):
    return jax.shard_map(
        shards,
        mesh=mesh,
        in_specs=(P("dp", "shard"), P("dp", None), P("dp", "shard", None), P("shard", None), P()),
        out_specs=(P("dp", "shard", None), P("shard", None), P()),
        check_vma=False,
    )
```
